32 devices in a mesh: cyl: 2 (over y), chain: 4 (over z), tensor: 4 (over x, core).
Axes of the slice: x: 2, y: 2, z: 4, core: 2. Of those that a mesh axis runs over, the one named last changes fastest.
Arguments:
- env: bfloat16 [8, 32, 10, 128, 128], P(('cyl', 'chain'), 'tensor'), parts along dimension 0, may hold values from -8 to 8, as said below
- site: bfloat16 [8, 32, 128, 128], P(('cyl', 'chain'), 'tensor'), parts along dimension 0, may hold values from -0.5 to 0.5
- seg_weight: float32 [8, 32, 128], P(('cyl', 'chain'), 'tensor'), parts along dimension 0, may hold values from 0.7 to 1.4
- ranks: int32 [64], P(('cyl', 'tensor')), parts along dimension 0, may hold values from 32 to 128
- mpo_mask: int32 [64, 10], P(('cyl', 'tensor')), parts along dimension 0, may hold values 0 or 1
Outputs:
- psi: bfloat16 [8, 32, 128, 128], P(('cyl', 'chain'), 'tensor'), parts along dimension 0
- energy: float32 [8], P(('cyl', 'chain')), parts along dimension 0
The draws below stay inside these ranges and needn't reach their ends.
There are 2 independent parts, one for each index of `cyl`. The reference program is written for one: setup_inputs(seed, part) draws one part's arguments, and reference() takes and returns one part's arrays. A program takes and returns all parts, laid end to end along the dimension named above; each array names one. Nothing has to cross between parts.
Inputs may be any that keep to these rules, and one draw needn't show every extreme that they name: `env`: every environment block is symmetric in its last two dimensions.
All inputs are finite; a program needn't handle non-finite values. No bound on the sum of `mpo_mask` on one device may be relied on, other than what follows from the above.
Results may differ from the reference program's by a relative error of at most 0.011.
Values may be sent and summed in bfloat16 or wider, within the bound.
No kernel may reach another device: no remote copies, remote signals or barrier semaphores. Data moves between devices by JAX's collectives and lax.ppermute only.
A program may use at most 192 MiB of HBM per device.

```python
import math
import jax
import jax.numpy as jnp
from jax import lax

B = 128
W = 10
ITERS = 4
SECTORS = 32
N_CHAIN = 4


def draw_env(key, part):
    key = jax.random.fold_in(key, 11)
    first = jax.random.fold_in(key, 0)
    raw = jnp.clip(jax.random.normal(first, (N_CHAIN, SECTORS, W, B, B), jnp.float32), -4.0, 4.0)
    noise = (raw + jnp.swapaxes(raw, -1, -2)) * (0.35 / jnp.sqrt(jnp.float32(B)))
    identity = (jnp.arange(B)[:, None] == jnp.arange(B)[None, :]).astype(jnp.float32)
    return (identity + noise).astype(jnp.bfloat16)


def touch_ends(entries, stream_key, least, high):
    longest = entries.shape.index(max(entries.shape))
    spots = []
    for shift in (0, 1):
        where = [jax.random.randint(jax.random.fold_in(stream_key, axis), (), 0, length) for axis, length in enumerate(entries.shape)]
        where[longest] = (where[longest] + shift) % entries.shape[longest]
        spots.append(tuple(where))
    return entries.at[spots[0]].set(least).at[spots[1]].set(high)


def block_levels(key, dims, cuts, low, high):
    factor_of, own = 1.0, jax.random.fold_in(key, 6)
    for dim, shards_of in cuts:
        steps = jnp.exp(jax.random.uniform(jax.random.fold_in(own, dim), (shards_of,), jnp.float32, low / len(cuts), high / len(cuts)))
        factor_of = factor_of * jnp.repeat(steps, dims[dim] // shards_of).reshape([-1 if axis == dim else 1 for axis in range(len(dims))])
    return factor_of


def centred(own_key, extent, scale, limit, cuts=(), kind=jnp.bfloat16):
    array = jax.random.normal(own_key, extent, jnp.float32) * scale
    if len(cuts) > 0:
        array = block_levels(own_key, extent, cuts, -0.22, 0.18) * array
    return jnp.clip(array, min=-limit, max=limit).astype(kind)


def setup_inputs(seed: int = 0, part: int = 0) -> dict:
    arg_keys = jax.random.split(jax.random.key(seed), 6)
    part_splits = jax.random.split(jax.random.fold_in(arg_keys[5], part), 6)
    env = draw_env(jax.random.fold_in(jax.random.fold_in(arg_keys[5], part), 71), part)
    site = centred(part_splits[1], (N_CHAIN, SECTORS, B, B), B ** -0.5, 0.5, ((0, 4), (1, 4)))
    seg_weight = jnp.clip(jnp.exp(math.log(1.4) - 0.6931472 * jax.random.uniform(part_splits[2], (N_CHAIN, SECTORS, B), jnp.float32) ** block_levels(part_splits[2], (N_CHAIN, SECTORS, B), ((0, 4), (1, 4)), -0.2, 0.2)), 0.7, 1.4)
    ranks = touch_ends(jax.random.randint(part_splits[3], (SECTORS,), B // 4, B + 1), jax.random.fold_in(part_splits[3], 1), B // 4, B).astype(jnp.int32)
    mpo_mask = touch_ends((jax.random.randint(part_splits[4], (SECTORS, W), 0, 2) < 1).astype(jnp.int32), jax.random.fold_in(part_splits[4], 1), 0, 1)
    return {"env": env, "site": site, "seg_weight": seg_weight, "ranks": ranks, "mpo_mask": mpo_mask}


STEP_SIZE = 0.5

def davidson(left, right, left_site, right_site, ranks, mpo_mask):
    hi = lax.Precision.HIGHEST
    sectors = left.shape[0]
    edge = left.shape[2]
    count = float(sectors * edge * edge)
    rowmask = (jnp.arange(edge)[None, :] < ranks[:, None]).astype(jnp.float32)[:, :, None]
    weights = mpo_mask.astype(jnp.float32)
    start = jnp.einsum('sij,sjk->sik', left_site.astype(jnp.float32), right_site.astype(jnp.float32), precision=hi)
    vector = rowmask * start
    diag_left = jnp.diagonal(left, axis1=2, axis2=3).astype(jnp.float32)
    diag_right = jnp.diagonal(right, axis1=2, axis2=3).astype(jnp.float32)
    diag_h = jnp.einsum('swi,swj->sij', weights[:, :, None] * diag_left, diag_right, precision=hi)
    left_f = left.astype(jnp.float32)
    right_f = right.astype(jnp.float32)
    mask_b = mpo_mask.astype(jnp.bfloat16)[:, :, None, None]
    theta = jnp.float32(0.0)
    for step in range(ITERS):
        low = vector.astype(jnp.bfloat16).astype(jnp.float32)
        inner = jnp.einsum('sij,swjk->swik', low, right_f, precision=hi).astype(jnp.bfloat16) * mask_b
        image = rowmask * jnp.einsum('swij,swjk->sik', left_f, inner.astype(jnp.float32), precision=hi)
        along = jnp.sum(vector * image)
        square = jnp.sum(vector * vector)
        theta = along / (square + 1e-06)
        resid = image - theta * vector
        correct = resid / (1.0 + jnp.abs(diag_h - theta))
        vector = (vector - STEP_SIZE * correct) / jnp.sqrt(square / count + 1e-06)
    final = jnp.sum(vector * vector)
    return ((vector / jnp.sqrt(final / count + 1e-06)).astype(jnp.bfloat16), theta)

def reference(env, site, seg_weight, ranks, mpo_mask):
    chain = env.shape[0]
    cumulative = jnp.cumprod(seg_weight, axis=0)
    even = (jnp.arange(chain) % 2 == 0)[:, None, None]
    scale = jnp.where(even, cumulative, seg_weight)
    pairs = chain // 2
    env_pairs = env.reshape((pairs, 2) + env.shape[1:])
    site_pairs = site.reshape((pairs, 2) + site.shape[1:])
    scale_pairs = scale.reshape((pairs, 2) + scale.shape[1:])

    def one_boundary(items):
        blocks, tensors, factors = items
        scaled = (factors[:, :, None, :, None] * blocks.astype(jnp.float32) * factors[:, :, None, None, :]).astype(jnp.bfloat16)
        return davidson(scaled[0], scaled[1], tensors[0], tensors[1], ranks, mpo_mask)
    psi, energy = lax.map(one_boundary, (env_pairs, site_pairs, scale_pairs))
    return (jnp.repeat(psi, 2, axis=0), jnp.repeat(energy, 2, axis=0))
```

```python
import functools

import jax
import jax.numpy as jnp
from jax import lax
from jax.experimental import pallas as pl
from jax.experimental.pallas import tpu as pltpu
from jax.sharding import PartitionSpec as P

ITERS = 4
STEP_SIZE = 0.5
EPS = 1e-6
BF16 = jnp.bfloat16
F32 = jnp.float32
VMEM_LIMIT = 48 * 2**20
VM = pl.BlockSpec(memory_space=pltpu.VMEM)
SM = pl.BlockSpec(memory_space=pltpu.SMEM)


def params():
    return pltpu.CompilerParams(vmem_limit_bytes=VMEM_LIMIT)


def cost(flops, bytes_accessed):
    return pl.CostEstimate(flops=int(flops), bytes_accessed=int(bytes_accessed), transcendentals=0)


def vmem(shape, dtype):
    return pltpu.VMEM(shape, dtype)


def keep(x):
    return pltpu.with_memory_space_constraint(x, pltpu.VMEM)


def grid_ij(edge):
    i = lax.broadcasted_iota(jnp.int32, (edge, edge), 0)
    j = lax.broadcasted_iota(jnp.int32, (edge, edge), 1)
    return i, j


def diag_row(block, i, j):
    return jnp.sum(jnp.where(i == j, block, 0.0), axis=0, keepdims=True)


def pack_kernel(cuts, sectors, chans, mask_ref, env_ref, *refs):
    chunks = refs[: len(cuts)]
    where_ref, diag_ref = refs[len(cuts) :]
    edge = env_ref.shape[-1]
    n = jnp.int32(0)
    for s in range(sectors):
        k = jnp.int32(0)
        for w in range(chans):
            m = mask_ref[s, w]
            where_ref[0, n] = jnp.int32(s * chans + w)
            where_ref[1, n] = jnp.int32(s)
            where_ref[2, n] = k
            n = n + m
            k = k + m
    where_ref[0, n] = jnp.int32(0)
    where_ref[1, n] = jnp.int32(0)
    where_ref[2, n] = jnp.int32(0)
    where_ref[3, 0] = n
    i, j = grid_ij(edge)
    pairs = (n + 1) // 2
    for (low, high), out in zip(cuts, chunks):

        def body(p, carry, low=low, out=out):
            first = env_ref[where_ref[0, 2 * p]].astype(F32)
            second = env_ref[where_ref[0, 2 * p + 1]].astype(F32)
            at = pl.multiple_of((p - low) * edge, edge)
            out[pl.ds(at, edge), :] = jnp.where(i <= j, first, second).astype(BF16)
            diag_ref[pl.ds(p - low, 1), :] = diag_row(second, i, j)
            return carry

        lax.fori_loop(low, jnp.minimum(high, pairs), body, 0)
        tail = out.shape[0] - (high - low) * edge
        out[(high - low) * edge :, :] = diag_ref[:tail, :].astype(BF16)


def unpack(low, high, here, chunk, where_ref, outer, buf, diags):
    edge = chunk.shape[-1]
    sectors = diags.shape[1]
    i, j = grid_ij(edge)
    n = where_ref[3, 0]

    def put(k, block):
        s, c = where_ref[1, k], where_ref[2, k]
        low_block = (block * outer[s]).astype(BF16)
        buf[here, s, c] = low_block
        diags[here, s, pl.ds(c, 1), :] = diag_row(low_block.astype(F32), i, j)

    tail = chunk[(high - low) * edge :, :].astype(F32)
    rows = lax.broadcasted_iota(jnp.int32, tail.shape, 0)

    def body(p, carry):
        at = pl.multiple_of((p - low) * edge, edge)
        both = chunk[pl.ds(at, edge), :].astype(F32)
        flip = both.T
        put(2 * p, jnp.where(i <= j, both, flip))

        @pl.when(2 * p + 1 < n)
        def _():
            diag = jnp.sum(jnp.where(rows == p - low, tail, 0.0), axis=0, keepdims=True)
            put(2 * p + 1, jnp.where(i > j, both, jnp.where(i == j, diag, flip)))

        return carry

    lax.fori_loop(low, jnp.minimum(high, (n + 1) // 2), body, 0)


def own_kernel(cut, where_ref, env_ref, weights, chunk, buf, diags, outer, mine):
    count, sectors, edge = weights.shape
    chans = buf.shape[2]
    at = lax.axis_index("chain")
    side = at % 2
    i, j = grid_ij(edge)
    left = weights[0]
    for c in range(1, count):
        left = left * jnp.where(c <= at - side, weights[c], 1.0)
    right = weights[at - side + 1]
    for s in range(sectors):
        row_l = jnp.broadcast_to(left[s : s + 1, :], (edge, edge))
        row_r = jnp.broadcast_to(right[s : s + 1, :], (edge, edge))
        outer_l = row_l.T * row_l
        outer_r = row_r.T * row_r
        mine[s] = jnp.where(side == 0, outer_l, outer_r)
        outer[s] = jnp.where(side == 0, outer_r, outer_l)
    diags[...] = jnp.zeros_like(diags)

    def wipe(t, carry):
        buf[0, t // chans, t % chans] = jnp.zeros((edge, edge), BF16)
        buf[1, t // chans, t % chans] = jnp.zeros((edge, edge), BF16)
        return carry

    lax.fori_loop(0, sectors * chans, wipe, 0)

    def body(k, carry):
        s, c = where_ref[1, k], where_ref[2, k]
        block = (env_ref[where_ref[0, k]].astype(F32) * mine[s]).astype(BF16)
        buf[side, s, c] = block
        diags[side, s, pl.ds(c, 1), :] = diag_row(block.astype(F32), i, j)
        return carry

    lax.fori_loop(0, where_ref[3, 0], body, 0)
    unpack(cut[0], cut[1], 1 - side, chunk, where_ref, outer, buf, diags)


def matvec(s, vector, buf, keep_row):
    chans = buf.shape[2]
    low = vector.astype(BF16)
    total = None
    for c in range(0, chans, 2):
        width = min(2, chans - c)
        right = jnp.concatenate([buf[1, s, c + d] for d in range(width)], axis=1)
        left = jnp.concatenate([buf[0, s, c + d] for d in range(width)], axis=1)
        edge = left.shape[0]
        inner = jnp.dot(low, right, preferred_element_type=F32).astype(BF16)
        inner = jnp.concatenate([inner[:, d * edge : (d + 1) * edge] for d in range(width)], axis=0)
        term = jnp.dot(left, inner, preferred_element_type=F32)
        total = term if total is None else total + term
    return jnp.where(keep_row, total, 0.0)


def store_sums(part, along, square):
    part[0:1, :] = jnp.sum(along, axis=0, keepdims=True)
    part[1:2, :] = jnp.sum(square, axis=0, keepdims=True)


def apply_all(vectors, ranks_ref, buf, vec, image, part):
    sectors, edge = buf.shape[1], buf.shape[-1]
    i, _ = grid_ij(edge)
    along = jnp.zeros((edge, edge), F32)
    square = jnp.zeros((edge, edge), F32)
    for s in range(sectors):
        vector = vectors(s)
        vec[s] = vector
        hv = matvec(s, vector, buf, i < ranks_ref[s])
        image[s] = hv
        along = along + vector * hv
        square = square + vector * vector
    store_sums(part, along, square)


def first_kernel(
    cuts, where_ref, ranks_ref, outer, own_site, other_site, *refs
):
    chunks = refs[: len(cuts)]
    _, _, buf, diags, vec, image, dh, part = refs[len(cuts) :]
    sectors, edge = buf.shape[1], buf.shape[-1]
    side = lax.axis_index("chain") % 2
    i, _ = grid_ij(edge)
    for (low, high), chunk in zip(cuts, chunks):
        unpack(low, high, 1 - side, chunk, where_ref, outer, buf, diags)

    def start(s):
        dh[s] = lax.dot_general(
            diags[0, s].astype(BF16),
            diags[1, s].astype(BF16),
            (((0,), (0,)), ((), ())),
            preferred_element_type=F32,
        )
        left = jnp.where(side == 0, own_site[s], other_site[s])
        right = jnp.where(side == 0, other_site[s], own_site[s])
        return jnp.where(i < ranks_ref[s], jnp.dot(left, right, preferred_element_type=F32), 0.0)

    apply_all(start, ranks_ref, buf, vec, image, part)


def joined(parts):
    values = [p[...] for p in parts]
    while len(values) > 1:
        values = [values[k] + values[k + 1] for k in range(0, len(values), 2)]
    total = values[0]
    along = jnp.sum(total[0:1, :], axis=1, keepdims=True)
    square = jnp.sum(total[1:2, :], axis=1, keepdims=True)
    return along, square


def step_of(count, along, square):
    theta = along / (square + EPS)
    scale = 1.0 / jnp.sqrt(square / count + EPS)

    def step(vector, hv, dh):
        resid = hv - theta * vector
        return (vector - STEP_SIZE * resid / (1.0 + jnp.abs(dh - theta))) * scale

    return theta, step


def iter_kernel(count, partners, ranks_ref, buf, vec_in, image_in, dh, *refs):
    parts = refs[:partners]
    vec, image, part = refs[partners:]
    _, step = step_of(count, *joined(parts))
    apply_all(lambda s: step(vec_in[s], image_in[s], dh[s]), ranks_ref, buf, vec, image, part)


def last_kernel(count, partners, vec_in, image_in, dh, *refs):
    parts = refs[:partners]
    vec, part, energy = refs[partners:]
    theta, step = step_of(count, *joined(parts))
    square = jnp.zeros(dh.shape[1:], F32)
    for s in range(dh.shape[0]):
        vector = step(vec_in[s], image_in[s], dh[s])
        vec[s] = vector
        square = square + vector * vector
    store_sums(part, square, square)
    energy[...] = jnp.broadcast_to(theta, energy.shape)


def psi_kernel(count, partners, vec, *refs):
    parts = refs[:partners]
    psi = refs[partners]
    square, _ = joined(parts)
    scale = 1.0 / jnp.sqrt(square / count + EPS)
    for s in range(psi.shape[0]):
        psi[s] = (vec[s] * scale).astype(BF16)


def swap(value):
    size = lax.axis_size("chain")
    return lax.ppermute(value, "chain", [(c, c ^ 1) for c in range(size)])


def gather_parts(part):
    size = lax.axis_size("tensor")
    moved = [part]
    for m in range(1, size):
        moved.append(lax.ppermute(part, "tensor", [(t, t ^ m) for t in range(size)]))
    return moved


def local(env, site, seg_weight, ranks, mpo_mask):
    sectors, chans, edge = env.shape[1:4]
    blocks = sectors * chans
    pairs = (blocks + 1) // 2
    tensor = lax.axis_size("tensor")
    count = float(sectors * tensor * edge * edge)
    base = min(pairs, -(-pairs * 3 // 5))
    cuts = [(0, base // 2), (base // 2, base), (base, pairs)]
    rows = lambda cut: (cut[1] - cut[0]) * edge + -(-(cut[1] - cut[0]) // 16) * 16

    weights = lax.all_gather(seg_weight[0], "chain")
    other_site = swap(site[0])
    block_bytes = 2 * edge * edge
    big = sectors * edge * edge * 4
    flat_env = env.reshape(blocks, edge, edge)

    packed = pl.pallas_call(
        functools.partial(pack_kernel, cuts, sectors, chans),
        out_shape=[jax.ShapeDtypeStruct((rows(c), edge), BF16) for c in cuts]
        + [jax.ShapeDtypeStruct((4, blocks + 8), jnp.int32)],
        in_specs=[SM, VM],
        out_specs=[VM] * len(cuts) + [SM],
        scratch_shapes=[pltpu.VMEM((max(-(-(c[1] - c[0]) // 16) * 16 for c in cuts), edge), F32)],
        compiler_params=params(),
        cost_estimate=cost(0, 2 * blocks * block_bytes),
        name="pack",
    )(mpo_mask, flat_env)
    sent, where = packed[:-1], packed[-1]
    got = [swap(c) for c in sent[:2]]
    active = jnp.sum(mpo_mask)
    got.append(lax.cond(active > 2 * base, swap, lambda c: c, sent[2]))

    buf_shape = (2, sectors, chans, edge, edge)
    diag_shape = (2, sectors, -(-chans // 16) * 16, edge)
    outer_shape = (sectors, edge, edge)
    buf, diags, outer = pl.pallas_call(
        functools.partial(own_kernel, cuts[0]),
        out_shape=[vmem(buf_shape, BF16), vmem(diag_shape, F32), vmem(outer_shape, F32)],
        in_specs=[SM, VM, VM, VM],
        out_specs=[VM] * 3,
        scratch_shapes=[pltpu.VMEM(outer_shape, F32)],
        compiler_params=params(),
        cost_estimate=cost(0, 4 * blocks * block_bytes),
        name="own",
    )(where, flat_env, weights, got[0])

    state = vmem(outer_shape, F32)
    sums = jax.ShapeDtypeStruct((2, edge), F32)
    work = 4.0 * blocks * edge**3
    buf, diags, vec, image, dh, part = pl.pallas_call(
        functools.partial(first_kernel, cuts[1:]),
        out_shape=[vmem(buf_shape, BF16), vmem(diag_shape, F32), state, state, state, sums],
        in_specs=[SM, SM] + [VM] * 7,
        out_specs=[VM] * 6,
        input_output_aliases={7: 0, 8: 1},
        compiler_params=params(),
        cost_estimate=cost(work, 2 * blocks * block_bytes),
        name="first",
    )(where, ranks, keep(outer), site[0], other_site, got[1], got[2], keep(buf), keep(diags))

    for _ in range(ITERS - 1):
        parts = gather_parts(part)
        vec, image, part = pl.pallas_call(
            functools.partial(iter_kernel, count, tensor),
            out_shape=[state, state, sums],
            in_specs=[SM] + [VM] * (4 + tensor),
            out_specs=[VM] * 3,
            compiler_params=params(),
            cost_estimate=cost(work, 2 * blocks * block_bytes),
            name="iterate",
        )(ranks, keep(buf), keep(vec), keep(image), keep(dh), *parts)

    parts = gather_parts(part)
    vec, part, energy = pl.pallas_call(
        functools.partial(last_kernel, count, tensor),
        out_shape=[state, sums, jax.ShapeDtypeStruct((1, edge), F32)],
        in_specs=[VM] * (3 + tensor),
        out_specs=[VM] * 3,
        compiler_params=params(),
        cost_estimate=cost(0, 3 * big),
        name="last",
    )(keep(vec), keep(image), keep(dh), *parts)
    parts = gather_parts(part)
    psi = pl.pallas_call(
        functools.partial(psi_kernel, count, tensor),
        out_shape=jax.ShapeDtypeStruct(outer_shape, BF16),
        in_specs=[VM] * (1 + tensor),
        out_specs=VM,
        compiler_params=params(),
        cost_estimate=cost(0, big),
        name="psi",
    )(keep(vec), *parts)
    return psi[None], energy[0, :1]


def solution(mesh):
    in_specs = (
        P(("cyl", "chain"), "tensor", None, None, None),
        P(("cyl", "chain"), "tensor", None, None),
        P(("cyl", "chain"), "tensor", None),
        P(("cyl", "tensor")),
        P(("cyl", "tensor"), None),
    )
    out_specs = (P(("cyl", "chain"), "tensor", None, None), P(("cyl", "chain")))
    return jax.shard_map(local, mesh=mesh, in_specs=in_specs, out_specs=out_specs, check_vma=False)
```

```python
import functools

import jax
import jax.numpy as jnp
from jax import lax
from jax.experimental import pallas as pl
from jax.experimental.pallas import tpu as pltpu
from jax.sharding import PartitionSpec as P

ITERS = 4
STEP_SIZE = 0.5
EPS = 1e-6
BF16 = jnp.bfloat16
F32 = jnp.float32
VMEM_LIMIT = 48 * 2**20
VM = pl.BlockSpec(memory_space=pltpu.VMEM)
SM = pl.BlockSpec(memory_space=pltpu.SMEM)


def params():
    return pltpu.CompilerParams(vmem_limit_bytes=VMEM_LIMIT)


def cost(flops, bytes_accessed):
    return pl.CostEstimate(flops=int(flops), bytes_accessed=int(bytes_accessed), transcendentals=0)


def vmem(shape, dtype):
    return pltpu.VMEM(shape, dtype)


def keep(x):
    return pltpu.with_memory_space_constraint(x, pltpu.VMEM)


def keep_scalars(x):
    return pltpu.with_memory_space_constraint(x, pltpu.SMEM)


def grid_ij(edge):
    i = lax.broadcasted_iota(jnp.int32, (edge, edge), 0)
    j = lax.broadcasted_iota(jnp.int32, (edge, edge), 1)
    return i, j


def diag_row(block, i, j):
    return jnp.sum(jnp.where(i == j, block, 0.0), axis=0, keepdims=True)


SOURCE, SECTOR, PLACE, TARGET, NUMBER = range(5)


def pack_kernel(cuts, group, chans, mask_ref, env_hbm, *refs):
    chunks = refs[: len(cuts)]
    table, env, own_diags, sems = refs[len(cuts) :]
    sectors, edge = mask_ref.shape[0], env.shape[-1]
    blocks = sectors * chans

    def fetch(s):
        part = pl.ds(s * chans, chans)
        return pltpu.make_async_copy(env_hbm.at[part], env.at[part], sems.at[s])

    for s in range(sectors):
        fetch(s).start()
    n = jnp.int32(0)
    for s in range(sectors):
        k = jnp.int32(0)
        for w in range(chans):
            m = mask_ref[s, w]
            table[SOURCE, n] = jnp.int32(s * chans + w)
            table[SECTOR, n] = jnp.int32(s)
            table[PLACE, n] = k
            table[TARGET, n] = s * chans + k
            n = n + m
            k = k + m
    for d in range(2 * group):
        table[SOURCE, n + d] = jnp.int32(0)
        table[SECTOR, n + d] = jnp.int32(0)
        table[PLACE, n + d] = jnp.int32(chans)
        table[TARGET, n + d] = jnp.int32(blocks)
    table[NUMBER, 0] = n
    i, j = grid_ij(edge)
    pairs = (n + 1) // 2
    here = jnp.int32(0)
    for (low, high), out in zip(cuts, chunks):

        def body(g, here, low=low, out=out):
            final = jnp.maximum(jnp.minimum(2 * (g + 1) * group, n) - 1, 0)
            need = jnp.maximum(here, table[SECTOR, final] + 1)

            def wait(s, carry):
                fetch(s).wait()
                return carry

            lax.fori_loop(here, need, wait, 0)
            for d in range(group):
                p = g * group + d
                first = env[table[SOURCE, 2 * p]].astype(F32)
                second = env[table[SOURCE, 2 * p + 1]].astype(F32)
                at = pl.multiple_of((p - low) * edge, edge)
                out[pl.ds(at, edge), :] = jnp.where(i <= j, first, second).astype(BF16)
                own_diags[pl.ds(2 * p, 1), :] = diag_row(first, i, j)
                own_diags[pl.ds(2 * p + 1, 1), :] = diag_row(second, i, j)
            return need

        stop = (jnp.minimum(high, pairs) + group - 1) // group
        here = lax.fori_loop(low // group, stop, body, here)
        size = (high - low) * edge
        tail = out.shape[0] - size
        out[size:, :] = own_diags[2 * low : 2 * low + tail, :].astype(BF16)

    def drain(s, carry):
        fetch(s).wait()
        return carry

    lax.fori_loop(here, sectors, drain, 0)


def put(k, block, side, table, outer, buf):
    buf[side, table[TARGET, k]] = (block * outer[table[SECTOR, k]]).astype(BF16)


def put_diag(k, row, side, table, outer_diag, diags):
    s = table[SECTOR, k]
    scaled = row * outer_diag[pl.ds(s, 1), :]
    diags[side, s, pl.ds(table[PLACE, k], 1), :] = scaled.astype(BF16).astype(F32)


def unpack(cut, group, side, chunk, table, outer, outer_diag, buf, diags, rows_ref):
    low, high = cut
    edge = chunk.shape[-1]
    i, j = grid_ij(edge)
    n = table[NUMBER, 0]
    size = (high - low) * edge
    rows_ref[: chunk.shape[0] - size, :] = chunk[size:, :].astype(F32)

    def body(g, carry):
        for d in range(group):
            p = g * group + d
            at = pl.multiple_of((p - low) * edge, edge)
            both = chunk[pl.ds(at, edge), :].astype(F32)
            flip = both.T
            row = rows_ref[pl.ds(2 * (p - low), 1), :]
            other = rows_ref[pl.ds(2 * (p - low) + 1, 1), :]
            put(2 * p, jnp.where(i <= j, both, flip), side, table, outer, buf)
            lower = jnp.where(i > j, both, jnp.where(i == j, other, flip))
            put(2 * p + 1, lower, side, table, outer, buf)
            put_diag(2 * p, row, side, table, outer_diag, diags)
            put_diag(2 * p + 1, other, side, table, outer_diag, diags)
        return carry

    stop = (jnp.minimum(high, (n + 1) // 2) + group - 1) // group
    lax.fori_loop(low // group, stop, body, 0)


def own_kernel(group, chans, count, table, env, own_diags, *refs):
    weights = refs[:count]
    buf, diags, outer, outer_diag, mine = refs[count:]
    sectors, edge = weights[0].shape
    at = lax.axis_index("chain")
    side = at % 2
    left = jnp.ones((sectors, edge), F32)
    right = jnp.ones((sectors, edge), F32)
    for c in range(count):
        value = weights[0][...]
        for d in range(1, count):
            value = jnp.where(at ^ d == c, weights[d][...], value)
        left = left * jnp.where(c <= at - side, value, 1.0)
        right = jnp.where(c == at - side + 1, value, right)
    own_weight = jnp.where(side == 0, left, right)
    other_weight = jnp.where(side == 0, right, left)
    outer_diag[...] = other_weight * other_weight
    for s in range(sectors):
        row = jnp.broadcast_to(own_weight[s : s + 1, :], (edge, edge))
        mine[s] = row.T * row
        row = jnp.broadcast_to(other_weight[s : s + 1, :], (edge, edge))
        outer[s] = row.T * row
    diags[...] = jnp.zeros_like(diags)

    def wipe(t, carry):
        buf[0, t] = jnp.zeros((edge, edge), BF16)
        buf[1, t] = jnp.zeros((edge, edge), BF16)
        return carry

    lax.fori_loop(0, sectors * chans, wipe, 0)
    own_square = own_weight * own_weight

    def body(g, carry):
        for d in range(2 * group):
            k = 2 * group * g + d
            put(k, env[table[SOURCE, k]].astype(F32), side, table, mine, buf)
            s = table[SECTOR, k]
            scaled = own_diags[pl.ds(k, 1), :] * mine_row(own_square, s)
            diags[side, s, pl.ds(table[PLACE, k], 1), :] = scaled.astype(BF16).astype(F32)
        return carry

    lax.fori_loop(0, (table[NUMBER, 0] + 2 * group - 1) // (2 * group), body, 0)


def mine_row(rows, s):
    index = lax.broadcasted_iota(jnp.int32, rows.shape, 0)
    return jnp.sum(jnp.where(index == s, rows, 0.0), axis=0, keepdims=True)


def mid_kernel(
    cut, group, table, ranks_ref, outer, outer_diag, own_site, other_site, chunk, *refs
):
    _, _, buf, diags, vec, rows_ref = refs
    sectors, edge = vec.shape[0], vec.shape[-1]
    side = lax.axis_index("chain") % 2
    _, j = grid_ij(edge)
    for s in range(sectors):
        left = jnp.where(side == 0, own_site[s], other_site[s])
        right = jnp.where(side == 0, other_site[s], own_site[s])
        start = jnp.dot(left, right, preferred_element_type=F32).T
        vec[s] = jnp.where(j < ranks_ref[s], start, 0.0)
    unpack(cut, group, 1 - side, chunk, table, outer, outer_diag, buf, diags, rows_ref)


def apply_all(vectors, ranks_ref, buf, vec, image, part, inner):
    sectors, edge = vec.shape[0], vec.shape[-1]
    chans = inner.shape[-1] // edge
    for s in range(sectors):
        vector = vectors(s)
        vec[s] = vector
        right = buf[1, s * chans : (s + 1) * chans].reshape(chans * edge, edge)
        image_t = jnp.dot(right, vector.astype(BF16), preferred_element_type=F32).astype(BF16)
        for c in range(chans):
            inner[s, :, c * edge : (c + 1) * edge] = image_t[c * edge : (c + 1) * edge]
    _, j = grid_ij(edge)
    along = jnp.zeros((edge, edge), F32)
    square = jnp.zeros((edge, edge), F32)
    for s in range(sectors):
        left = buf[0, s * chans : (s + 1) * chans].reshape(chans * edge, edge)
        hv = jnp.dot(inner[s], left, preferred_element_type=F32)
        hv = jnp.where(j < ranks_ref[s], hv, 0.0)
        image[s] = hv
        vector = vec[s]
        along = along + vector * hv
        square = square + vector * vector
    store_sums(part, along, square)


def store_sums(part, along, square):
    part[0:1, :] = jnp.sum(along, axis=0, keepdims=True)
    part[1:2, :] = jnp.sum(square, axis=0, keepdims=True)


def first_kernel(cuts, group, table, ranks_ref, outer, outer_diag, vec_in, *refs):
    chunks = refs[: len(cuts)]
    _, _, buf, diags, vec, image, dh, part, inner, rows_ref = refs[len(cuts) :]
    sectors = vec.shape[0]
    side = lax.axis_index("chain") % 2
    for cut, chunk in zip(cuts, chunks):
        unpack(cut, group, 1 - side, chunk, table, outer, outer_diag, buf, diags, rows_ref)
    chans = inner.shape[-1] // vec.shape[-1]
    used = lax.broadcasted_iota(jnp.int32, diags.shape[2:], 0) < chans
    for s in range(sectors):
        dh[s] = lax.dot_general(
            jnp.where(used, diags[1, s], 0.0).astype(BF16),
            jnp.where(used, diags[0, s], 0.0).astype(BF16),
            (((0,), (0,)), ((), ())),
            preferred_element_type=F32,
        )
    apply_all(lambda s: vec_in[s], ranks_ref, buf, vec, image, part, inner)


def joined(parts):
    values = [p[...] for p in parts]
    while len(values) > 1:
        values = [values[k] + values[k + 1] for k in range(0, len(values), 2)]
    total = values[0]
    along = jnp.sum(total[0:1, :], axis=1, keepdims=True)
    square = jnp.sum(total[1:2, :], axis=1, keepdims=True)
    return along, square


def step_of(count, along, square):
    theta = along / (square + EPS)
    scale = 1.0 / jnp.sqrt(square / count + EPS)

    def step(vector, hv, dh):
        resid = hv - theta * vector
        return (vector - STEP_SIZE * resid / (1.0 + jnp.abs(dh - theta))) * scale

    return theta, step


def iter_kernel(count, partners, ranks_ref, buf, vec_in, image_in, dh, *refs):
    parts = refs[:partners]
    vec, image, part, inner = refs[partners:]
    _, step = step_of(count, *joined(parts))
    apply_all(
        lambda s: step(vec_in[s], image_in[s], dh[s]), ranks_ref, buf, vec, image, part, inner
    )


def last_kernel(count, partners, vec_in, image_in, dh, *refs):
    parts = refs[:partners]
    vec, part, energy = refs[partners:]
    theta, step = step_of(count, *joined(parts))
    square = jnp.zeros(dh.shape[1:], F32)
    for s in range(dh.shape[0]):
        vector = step(vec_in[s], image_in[s], dh[s])
        vec[s] = vector
        square = square + vector * vector
    store_sums(part, square, square)
    energy[...] = jnp.broadcast_to(theta, energy.shape)


def turn_kernel(vec, turned):
    for s in range(vec.shape[0]):
        turned[s] = vec[s].T


def psi_kernel(count, partners, vec, *refs):
    parts = refs[:partners]
    psi = refs[partners]
    square, _ = joined(parts)
    scale = 1.0 / jnp.sqrt(square / count + EPS)
    for s in range(psi.shape[0]):
        psi[s] = (vec[s] * scale).astype(BF16)


def swap(value):
    return swapped(value, "chain", 1)


def swapped(value, axis, mask):
    size = lax.axis_size(axis)
    return lax.ppermute(value, axis, [(k, k ^ mask) for k in range(size)])


def from_all(value, axis):
    return [value] + [swapped(value, axis, m) for m in range(1, lax.axis_size(axis))]


def gather_parts(part):
    return [keep(p) for p in from_all(part, "tensor")]


def local(env, site, seg_weight, ranks, mpo_mask):
    sectors, chans, edge = env.shape[1:4]
    blocks = sectors * chans
    tensor = lax.axis_size("tensor")
    count = float(sectors * tensor * edge * edge)
    group = 4
    pairs = -(-blocks // (2 * group)) * group
    base = min(pairs, -(-pairs * 3 // 5 // (2 * group)) * 2 * group)
    cuts = [(0, base // 2), (base // 2, base), (base, pairs)]
    tails = [-(-2 * (c[1] - c[0]) // 16) * 16 for c in cuts]
    rows = [(c[1] - c[0]) * edge + t for c, t in zip(cuts, tails)]
    block_bytes = 2 * edge * edge
    big = sectors * edge * edge * 4

    weights = from_all(seg_weight[0], "chain")
    other_site = swap(site[0])
    flat_env = env.reshape(blocks, edge, edge)

    packed = pl.pallas_call(
        functools.partial(pack_kernel, cuts, group, chans),
        out_shape=[vmem((r, edge), BF16) for r in rows]
        + [
            pltpu.SMEM((5, blocks + 2 * group), jnp.int32),
            vmem((blocks, edge, edge), BF16),
            vmem((2 * pairs + 16, edge), F32),
        ],
        in_specs=[SM, pl.BlockSpec(memory_space=pltpu.HBM)],
        out_specs=[VM] * len(cuts) + [SM, VM, VM],
        scratch_shapes=[pltpu.SemaphoreType.DMA((sectors,))],
        compiler_params=params(),
        cost_estimate=cost(0, 2 * blocks * block_bytes),
        name="pack",
    )(mpo_mask, flat_env)
    sent, (table, env_here, own_diags) = packed[:-3], packed[-3:]
    table = keep_scalars(table)
    got = [swap(sent[0])]
    later, other_site = lax.optimization_barrier((sent[1], other_site))
    got.append(swap(later))
    active = jnp.sum(mpo_mask)
    got.append(lax.cond(active > 2 * base, swap, lambda c: c, sent[2]))
    got = [keep(g) for g in got]

    buf_shape = vmem((2, blocks + 1, edge, edge), BF16)
    diag_shape = vmem((2, sectors, -(-(chans + 1) // 16) * 16, edge), F32)
    state_shape = (sectors, edge, edge)
    state = vmem(state_shape, F32)
    row_shape = vmem((sectors, edge), F32)
    sums = vmem((2, edge), F32)
    tail_rows = pltpu.VMEM((max(tails), edge), F32)
    inner_shape = pltpu.VMEM((sectors, edge, chans * edge), BF16)
    work = 4.0 * blocks * edge**3

    buf, diags, outer, outer_diag = pl.pallas_call(
        functools.partial(own_kernel, group, chans, len(weights)),
        out_shape=[buf_shape, diag_shape, state, row_shape],
        in_specs=[SM] + [VM] * (2 + len(weights)),
        out_specs=[VM] * 4,
        scratch_shapes=[pltpu.VMEM(state_shape, F32)],
        compiler_params=params(),
        cost_estimate=cost(0, 4 * blocks * block_bytes),
        name="own",
    )(table, keep(env_here), keep(own_diags), *[keep(w) for w in weights])

    buf, diags, vec = pl.pallas_call(
        functools.partial(mid_kernel, cuts[0], group),
        out_shape=[buf_shape, diag_shape, state],
        in_specs=[SM, SM] + [VM] * 7,
        out_specs=[VM] * 3,
        scratch_shapes=[tail_rows],
        input_output_aliases={7: 0, 8: 1},
        compiler_params=params(),
        cost_estimate=cost(0, blocks * block_bytes),
        name="mid",
    )(
        table, ranks, keep(outer), keep(outer_diag), keep(site[0]), keep(other_site), got[0],
        keep(buf), keep(diags),
    )

    buf, diags, vec, image, dh, part = pl.pallas_call(
        functools.partial(first_kernel, cuts[1:], group),
        out_shape=[buf_shape, diag_shape, state, state, state, sums],
        in_specs=[SM, SM] + [VM] * 7,
        out_specs=[VM] * 6,
        scratch_shapes=[inner_shape, tail_rows],
        input_output_aliases={7: 0, 8: 1},
        compiler_params=params(),
        cost_estimate=cost(work, 2 * blocks * block_bytes),
        name="first",
    )(
        table, ranks, keep(outer), keep(outer_diag), keep(vec), got[1], got[2],
        keep(buf), keep(diags),
    )

    for _ in range(ITERS - 1):
        parts = gather_parts(part)
        vec, image, part = pl.pallas_call(
            functools.partial(iter_kernel, count, tensor),
            out_shape=[state, state, sums],
            in_specs=[SM] + [VM] * (4 + tensor),
            out_specs=[VM] * 3,
            scratch_shapes=[inner_shape],
            compiler_params=params(),
            cost_estimate=cost(work, 2 * blocks * block_bytes),
            name="iterate",
        )(ranks, keep(buf), keep(vec), keep(image), keep(dh), *parts)

    parts = gather_parts(part)
    vec, part, energy = pl.pallas_call(
        functools.partial(last_kernel, count, tensor),
        out_shape=[state, sums, jax.ShapeDtypeStruct((1, edge), F32)],
        in_specs=[VM] * (3 + tensor),
        out_specs=[VM] * 3,
        compiler_params=params(),
        cost_estimate=cost(0, 3 * big),
        name="last",
    )(keep(vec), keep(image), keep(dh), *parts)
    parts = gather_parts(part)
    turned = pl.pallas_call(
        turn_kernel,
        out_shape=state,
        in_specs=[VM],
        out_specs=VM,
        compiler_params=params(),
        cost_estimate=cost(0, 2 * big),
        name="turn",
    )(keep(vec))
    psi = pl.pallas_call(
        functools.partial(psi_kernel, count, tensor),
        out_shape=jax.ShapeDtypeStruct(state_shape, BF16),
        in_specs=[VM] * (1 + tensor),
        out_specs=VM,
        compiler_params=params(),
        cost_estimate=cost(0, big),
        name="psi",
    )(keep(turned), *parts)
    return psi[None], energy[0, :1]


def solution(mesh):
    in_specs = (
        P(("cyl", "chain"), "tensor", None, None, None),
        P(("cyl", "chain"), "tensor", None, None),
        P(("cyl", "chain"), "tensor", None),
        P(("cyl", "tensor")),
        P(("cyl", "tensor"), None),
    )
    out_specs = (P(("cyl", "chain"), "tensor", None, None), P(("cyl", "chain")))
    return jax.shard_map(local, mesh=mesh, in_specs=in_specs, out_specs=out_specs, check_vma=False)
```

```python
import functools

import jax
import jax.numpy as jnp
from jax import lax
from jax.experimental import pallas as pl
from jax.experimental.pallas import tpu as pltpu
from jax.sharding import PartitionSpec as P

ITERS = 4
STEP_SIZE = 0.5
PACK_COST = 10**7
REST_COST = 10**10
EPS = 1e-6
BF16 = jnp.bfloat16
F32 = jnp.float32
VMEM_LIMIT = 16 * 2**20
VM = pl.BlockSpec(memory_space=pltpu.VMEM)
SM = pl.BlockSpec(memory_space=pltpu.SMEM)


def params():
    return pltpu.CompilerParams(vmem_limit_bytes=VMEM_LIMIT)


def cost(flops, bytes_accessed):
    return pl.CostEstimate(flops=int(flops), bytes_accessed=int(bytes_accessed), transcendentals=0)


def vmem(shape, dtype):
    return pltpu.VMEM(shape, dtype)


def keep(x):
    return pltpu.with_memory_space_constraint(x, pltpu.VMEM)


def keep_scalars(x):
    return pltpu.with_memory_space_constraint(x, pltpu.SMEM)


def stay(x):
    return pltpu.with_memory_space_constraint(x, pltpu.HBM)


def grid_ij(edge):
    i = lax.broadcasted_iota(jnp.int32, (edge, edge), 0)
    j = lax.broadcasted_iota(jnp.int32, (edge, edge), 1)
    return i, j


def diag_row(block, i, j):
    return jnp.sum(jnp.where(i == j, block, 0.0), axis=0, keepdims=True)


SOURCE, SECTOR, PLACE, TARGET, RANK, NUMBER = range(6)


def pack(cut, group, table, env, own_diags, out, before=lambda g, carry: carry, carry=0):
    low, high = cut
    edge = env.shape[-1]
    i, j = grid_ij(edge)

    def body(g, carry):
        carry = before(g, carry)
        for d in range(group):
            p = g * group + d
            first = env[table[SOURCE, 2 * p]].astype(F32)
            second = env[table[SOURCE, 2 * p + 1]].astype(F32)
            at = pl.multiple_of((p - low) * edge, edge)
            out[pl.ds(at, edge), :] = jnp.where(i <= j, first, second).astype(BF16)
            own_diags[pl.ds(2 * p, 1), :] = diag_row(first, i, j)
            own_diags[pl.ds(2 * p + 1, 1), :] = diag_row(second, i, j)
        return carry

    pairs = (table[NUMBER, 0] + 1) // 2
    stop = (jnp.minimum(high, pairs) + group - 1) // group
    carry = lax.fori_loop(low // group, stop, body, carry)
    size = (high - low) * edge
    tail = out.shape[0] - size
    out[size:, :] = own_diags[2 * low : 2 * low + tail, :].astype(BF16)
    return carry


def pack_kernel(cut, group, chans, mask_ref, ranks_ref, env_hbm, out, table, own_diags, env, sems):
    sectors = mask_ref.shape[0]
    blocks = sectors * chans

    def fetch(s):
        part = pl.ds(s * chans, chans)
        return pltpu.make_async_copy(env_hbm.at[part], env.at[part], sems.at[s])

    for s in range(sectors):
        fetch(s).start()
    n = jnp.int32(0)
    for s in range(sectors):
        table[RANK, s] = ranks_ref[s]
        k = jnp.int32(0)
        for w in range(chans):
            m = mask_ref[s, w]
            table[SOURCE, n] = jnp.int32(s * chans + w)
            table[SECTOR, n] = jnp.int32(s)
            table[PLACE, n] = k
            table[TARGET, n] = s * chans + k
            n = n + m
            k = k + m
    for d in range(2 * group):
        table[SOURCE, n + d] = jnp.int32(0)
        table[SECTOR, n + d] = jnp.int32(0)
        table[PLACE, n + d] = jnp.int32(chans)
        table[TARGET, n + d] = jnp.int32(blocks)
    table[NUMBER, 0] = n

    def wait(s, carry):
        fetch(s).wait()
        return carry

    def before(g, here):
        final = jnp.maximum(jnp.minimum(2 * (g + 1) * group, n) - 1, 0)
        need = jnp.maximum(here, table[SECTOR, final] + 1)
        lax.fori_loop(here, need, wait, 0)
        return need

    here = pack(cut, group, table, env, own_diags, out, before, jnp.int32(0))
    lax.fori_loop(here, sectors, wait, 0)


def rest_kernel(cuts, group, table, env, own_site, other_site, *refs):
    count = len(refs) - len(cuts) - 3
    weights, chunks, (own_diags, both, vec) = refs[:count], refs[count:-3], refs[-3:]
    for cut, out in zip(cuts, chunks):
        pack(cut, group, table, env, own_diags, out)
    sectors, edge = weights[0].shape
    at = lax.axis_index("chain")
    side = at % 2
    left = jnp.ones((sectors, edge), F32)
    right = left
    for c in range(count):
        value = weights[0][...]
        for d in range(1, count):
            value = jnp.where(at ^ d == c, weights[d][...], value)
        left = left * jnp.where(c <= at - side, value, 1.0)
        right = jnp.where(c == at - side + 1, value, right)
    both[0] = left
    both[1] = right
    _, j = grid_ij(edge)
    for s in range(sectors):
        first = jnp.where(side == 0, own_site[s], other_site[s])
        second = jnp.where(side == 0, other_site[s], own_site[s])
        start = jnp.dot(first, second, preferred_element_type=F32).T
        vec[s] = jnp.where(j < table[RANK, s], start, 0.0)


def put(k, block, side, table, outer, buf):
    buf[side, table[TARGET, k]] = (block * outer[table[SECTOR, k]]).astype(BF16)


def put_diag(k, row, side, table, outer_diag, diags):
    s = table[SECTOR, k]
    scaled = row * outer_diag[pl.ds(s, 1), :]
    diags[side, s, pl.ds(table[PLACE, k], 1), :] = scaled.astype(BF16).astype(F32)


def unpack(cut, group, side, chunk, table, outer, outer_diag, buf, diags, rows_ref):
    low, high = cut
    edge = chunk.shape[-1]
    i, j = grid_ij(edge)
    n = table[NUMBER, 0]
    size = (high - low) * edge
    rows_ref[: chunk.shape[0] - size, :] = chunk[size:, :].astype(F32)

    def body(g, carry):
        for d in range(group):
            p = g * group + d
            at = pl.multiple_of((p - low) * edge, edge)
            both = chunk[pl.ds(at, edge), :].astype(F32)
            flip = both.T
            row = rows_ref[pl.ds(2 * (p - low), 1), :]
            other = rows_ref[pl.ds(2 * (p - low) + 1, 1), :]
            put(2 * p, jnp.where(i <= j, both, flip), side, table, outer, buf)
            lower = jnp.where(i > j, both, jnp.where(i == j, other, flip))
            put(2 * p + 1, lower, side, table, outer, buf)
            put_diag(2 * p, row, side, table, outer_diag, diags)
            put_diag(2 * p + 1, other, side, table, outer_diag, diags)
        return carry

    stop = (jnp.minimum(high, (n + 1) // 2) + group - 1) // group
    lax.fori_loop(low // group, stop, body, 0)


def own_kernel(group, chans, split, table, env, own_diags, later_diags, both, buf, diags, outer, outer_diag, mine, mine_diag):
    sectors, edge = mine.shape[0], mine.shape[-1]
    side = lax.axis_index("chain") % 2
    own_weight, other_weight = both[side], both[1 - side]
    outer_diag[...] = other_weight * other_weight
    mine_diag[...] = own_weight * own_weight
    for s in range(sectors):
        row = jnp.broadcast_to(own_weight[s : s + 1, :], (edge, edge))
        mine[s] = row.T * row
        row = jnp.broadcast_to(other_weight[s : s + 1, :], (edge, edge))
        outer[s] = row.T * row
    diags[...] = jnp.zeros_like(diags)

    def wipe(t, carry):
        buf[0, t] = jnp.zeros((edge, edge), BF16)
        buf[1, t] = jnp.zeros((edge, edge), BF16)
        return carry

    lax.fori_loop(0, sectors * chans, wipe, 0)

    def body(g, carry):
        for d in range(2 * group):
            k = 2 * group * g + d
            put(k, env[table[SOURCE, k]].astype(F32), side, table, mine, buf)
            at = pl.ds(k, 1)
            row = jnp.where(k < 2 * split, own_diags[at, :], later_diags[at, :])
            put_diag(k, row, side, table, mine_diag, diags)
        return carry

    lax.fori_loop(0, (table[NUMBER, 0] + 2 * group - 1) // (2 * group), body, 0)


def mid_kernel(cut, group, table, outer, outer_diag, chunk, *refs):
    _, _, buf, diags, rows_ref = refs
    side = lax.axis_index("chain") % 2
    unpack(cut, group, 1 - side, chunk, table, outer, outer_diag, buf, diags, rows_ref)


def apply_all(vectors, table, buf, vec, image, part, inner):
    sectors, edge = vec.shape[0], vec.shape[-1]
    chans = inner.shape[-1] // edge
    for s in range(sectors):
        vector = vectors(s)
        vec[s] = vector
        right = buf[1, s * chans : (s + 1) * chans].reshape(chans * edge, edge)
        image_t = jnp.dot(right, vector.astype(BF16), preferred_element_type=F32).astype(BF16)
        for c in range(chans):
            inner[s, :, c * edge : (c + 1) * edge] = image_t[c * edge : (c + 1) * edge]
    _, j = grid_ij(edge)
    along = jnp.zeros((edge, edge), F32)
    square = jnp.zeros((edge, edge), F32)
    for s in range(sectors):
        left = buf[0, s * chans : (s + 1) * chans].reshape(chans * edge, edge)
        hv = jnp.dot(inner[s], left, preferred_element_type=F32)
        hv = jnp.where(j < table[RANK, s], hv, 0.0)
        image[s] = hv
        vector = vec[s]
        along = along + vector * hv
        square = square + vector * vector
    store_sums(part, along, square)


def store_sums(part, along, square):
    part[0:1, :] = jnp.sum(along, axis=0, keepdims=True)
    part[1:2, :] = jnp.sum(square, axis=0, keepdims=True)


def first_kernel(cuts, group, table, outer, outer_diag, vec_in, *refs):
    chunks = refs[: len(cuts)]
    _, _, buf, diags, vec, image, dh, part, inner, rows_ref = refs[len(cuts) :]
    sectors = vec.shape[0]
    side = lax.axis_index("chain") % 2
    for cut, chunk in zip(cuts, chunks):
        unpack(cut, group, 1 - side, chunk, table, outer, outer_diag, buf, diags, rows_ref)
    chans = inner.shape[-1] // vec.shape[-1]
    used = lax.broadcasted_iota(jnp.int32, diags.shape[2:], 0) < chans
    for s in range(sectors):
        dh[s] = lax.dot_general(
            jnp.where(used, diags[1, s], 0.0).astype(BF16),
            jnp.where(used, diags[0, s], 0.0).astype(BF16),
            (((0,), (0,)), ((), ())),
            preferred_element_type=F32,
        )
    apply_all(lambda s: vec_in[s], table, buf, vec, image, part, inner)


def joined(parts):
    values = [p[...] for p in parts]
    while len(values) > 1:
        values = [values[k] + values[k + 1] for k in range(0, len(values), 2)]
    total = values[0]
    along = jnp.sum(total[0:1, :], axis=1, keepdims=True)
    square = jnp.sum(total[1:2, :], axis=1, keepdims=True)
    return along, square


def step_of(count, along, square):
    theta = along / (square + EPS)
    scale = 1.0 / jnp.sqrt(square / count + EPS)

    def step(vector, hv, dh):
        resid = hv - theta * vector
        return (vector - STEP_SIZE * resid / (1.0 + jnp.abs(dh - theta))) * scale

    return theta, step


def iter_kernel(count, partners, table, buf, vec_in, image_in, dh, *refs):
    parts = refs[:partners]
    vec, image, part, inner = refs[partners:]
    _, step = step_of(count, *joined(parts))
    apply_all(
        lambda s: step(vec_in[s], image_in[s], dh[s]), table, buf, vec, image, part, inner
    )


def last_kernel(count, partners, vec_in, image_in, dh, *refs):
    parts = refs[:partners]
    vec, part, energy = refs[partners:]
    theta, step = step_of(count, *joined(parts))
    square = jnp.zeros(dh.shape[1:], F32)
    for s in range(dh.shape[0]):
        vector = step(vec_in[s], image_in[s], dh[s])
        vec[s] = vector
        square = square + vector * vector
    store_sums(part, square, square)
    energy[...] = jnp.broadcast_to(theta, energy.shape)


def turn_kernel(vec, turned):
    for s in range(vec.shape[0]):
        turned[s] = vec[s].T


def psi_kernel(count, partners, vec, *refs):
    parts = refs[:partners]
    psi = refs[partners]
    square, _ = joined(parts)
    scale = 1.0 / jnp.sqrt(square / count + EPS)
    for s in range(psi.shape[0]):
        psi[s] = (vec[s] * scale).astype(BF16)


def swap(value):
    return swapped(value, "chain", 1)


def swapped(value, axis, mask):
    size = lax.axis_size(axis)
    return lax.ppermute(value, axis, [(k, k ^ mask) for k in range(size)])


def from_all(value, axis):
    return [value] + [swapped(value, axis, m) for m in range(1, lax.axis_size(axis))]


def gather_parts(part):
    return [keep(p) for p in from_all(part, "tensor")]


def local(env, site, seg_weight, ranks, mpo_mask):
    sectors, chans, edge = env.shape[1:4]
    blocks = sectors * chans
    tensor = lax.axis_size("tensor")
    count = float(sectors * tensor * edge * edge)
    group = 4
    pairs = -(-blocks // (2 * group)) * group
    base = min(pairs, -(-pairs * 3 // 5 // (2 * group)) * 2 * group)
    cuts = [(0, base // 2), (base // 2, base), (base, pairs)]
    tails = [-(-2 * (c[1] - c[0]) // 16) * 16 for c in cuts]
    rows = [(c[1] - c[0]) * edge + t for c, t in zip(cuts, tails)]
    block_bytes = 2 * edge * edge
    big = sectors * edge * edge * 4

    weights = [keep(w) for w in from_all(seg_weight[0], "chain")]
    other_site = swap(site[0])
    flat_env = env.reshape(blocks, edge, edge)
    state_shape = (sectors, edge, edge)
    state = vmem(state_shape, F32)
    row_shape = vmem((sectors, edge), F32)

    diag_rows = vmem((2 * pairs + 16, edge), F32)
    first_sent, table, own_diags, env_here = pl.pallas_call(
        functools.partial(pack_kernel, cuts[0], group, chans),
        out_shape=[
            vmem((rows[0], edge), BF16),
            pltpu.SMEM((6, blocks + 2 * group), jnp.int32),
            diag_rows,
            vmem((blocks, edge, edge), BF16),
        ],
        in_specs=[SM, SM, pl.BlockSpec(memory_space=pltpu.HBM)],
        out_specs=[VM, SM, VM, VM],
        scratch_shapes=[pltpu.SemaphoreType.DMA((sectors,))],
        compiler_params=params(),
        cost_estimate=cost(PACK_COST, 2 * blocks * block_bytes),
        name="pack",
    )(stay(mpo_mask), stay(ranks), stay(flat_env))
    table = keep_scalars(table)
    env_here = keep(env_here)
    *sent, later_diags, both, vec = pl.pallas_call(
        functools.partial(rest_kernel, cuts[1:], group),
        out_shape=[vmem((r, edge), BF16) for r in rows[1:]]
        + [diag_rows, vmem((2, sectors, edge), F32), state],
        in_specs=[SM] + [VM] * (3 + len(weights)),
        out_specs=[VM] * (len(cuts) + 2),
        compiler_params=params(),
        cost_estimate=cost(REST_COST, 2 * blocks * block_bytes),
        name="rest",
    )(table, env_here, site[0], keep(other_site), *weights)
    sent = [first_sent, *sent]
    got = [swap(sent[0]), swap(sent[1])]
    active = jnp.sum(mpo_mask)
    got.append(lax.cond(active > 2 * base, swap, lambda c: c, sent[2]))
    got = [keep(g) for g in got]

    buf_shape = vmem((2, blocks + 1, edge, edge), BF16)
    diag_shape = vmem((2, sectors, -(-(chans + 1) // 16) * 16, edge), F32)
    sums = vmem((2, edge), F32)
    tail_rows = pltpu.VMEM((max(tails), edge), F32)
    inner_shape = pltpu.VMEM((sectors, edge, chans * edge), BF16)
    work = 4.0 * blocks * edge**3

    buf, diags, outer, outer_diag = pl.pallas_call(
        functools.partial(own_kernel, group, chans, cuts[0][1]),
        out_shape=[buf_shape, diag_shape, state, row_shape],
        in_specs=[SM] + [VM] * 4,
        out_specs=[VM] * 4,
        scratch_shapes=[pltpu.VMEM(state_shape, F32), pltpu.VMEM((sectors, edge), F32)],
        compiler_params=params(),
        cost_estimate=cost(0, 0),
        name="own",
    )(table, env_here, keep(own_diags), keep(later_diags), keep(both))

    buf, diags = pl.pallas_call(
        functools.partial(mid_kernel, cuts[0], group),
        out_shape=[buf_shape, diag_shape],
        in_specs=[SM] + [VM] * 5,
        out_specs=[VM] * 2,
        scratch_shapes=[tail_rows],
        input_output_aliases={4: 0, 5: 1},
        compiler_params=params(),
        cost_estimate=cost(0, 0),
        name="mid",
    )(table, keep(outer), keep(outer_diag), got[0], keep(buf), keep(diags))

    buf, diags, vec, image, dh, part = pl.pallas_call(
        functools.partial(first_kernel, cuts[1:], group),
        out_shape=[buf_shape, diag_shape, state, state, state, sums],
        in_specs=[SM] + [VM] * 7,
        out_specs=[VM] * 6,
        scratch_shapes=[inner_shape, tail_rows],
        input_output_aliases={6: 0, 7: 1},
        compiler_params=params(),
        cost_estimate=cost(work, 2 * blocks * block_bytes),
        name="first",
    )(
        table, keep(outer), keep(outer_diag), keep(vec), got[1], got[2],
        keep(buf), keep(diags),
    )

    for _ in range(ITERS - 1):
        parts = gather_parts(part)
        vec, image, part = pl.pallas_call(
            functools.partial(iter_kernel, count, tensor),
            out_shape=[state, state, sums],
            in_specs=[SM] + [VM] * (4 + tensor),
            out_specs=[VM] * 3,
            scratch_shapes=[inner_shape],
            compiler_params=params(),
            cost_estimate=cost(work, 2 * blocks * block_bytes),
            name="iterate",
        )(table, keep(buf), keep(vec), keep(image), keep(dh), *parts)

    parts = gather_parts(part)
    vec, part, energy = pl.pallas_call(
        functools.partial(last_kernel, count, tensor),
        out_shape=[state, sums, jax.ShapeDtypeStruct((1, edge), F32)],
        in_specs=[VM] * (3 + tensor),
        out_specs=[VM] * 3,
        compiler_params=params(),
        cost_estimate=cost(0, 3 * big),
        name="last",
    )(keep(vec), keep(image), keep(dh), *parts)
    parts = gather_parts(part)
    turned = pl.pallas_call(
        turn_kernel,
        out_shape=state,
        in_specs=[VM],
        out_specs=VM,
        compiler_params=params(),
        cost_estimate=cost(0, 2 * big),
        name="turn",
    )(keep(vec))
    psi = pl.pallas_call(
        functools.partial(psi_kernel, count, tensor),
        out_shape=jax.ShapeDtypeStruct(state_shape, BF16),
        in_specs=[VM] * (1 + tensor),
        out_specs=VM,
        compiler_params=params(),
        cost_estimate=cost(0, big),
        name="psi",
    )(keep(turned), *parts)
    return psi[None], energy[0, :1]


def solution(mesh):
    in_specs = (
        P(("cyl", "chain"), "tensor", None, None, None),
        P(("cyl", "chain"), "tensor", None, None),
        P(("cyl", "chain"), "tensor", None),
        P(("cyl", "tensor")),
        P(("cyl", "tensor"), None),
    )
    out_specs = (P(("cyl", "chain"), "tensor", None, None), P(("cyl", "chain")))
    return jax.shard_map(local, mesh=mesh, in_specs=in_specs, out_specs=out_specs, check_vma=False)
```

```python
import functools

import jax
import jax.numpy as jnp
from jax import lax
from jax.experimental import pallas as pl
from jax.experimental.pallas import tpu as pltpu
from jax.sharding import PartitionSpec as P

ITERS = 4
STEP_SIZE = 0.5
PACK_COST = 10**7
REST_COST = 10**10
EPS = 1e-6
BF16 = jnp.bfloat16
F32 = jnp.float32
VMEM_LIMIT = 16 * 2**20
VM = pl.BlockSpec(memory_space=pltpu.VMEM)
SM = pl.BlockSpec(memory_space=pltpu.SMEM)


def params():
    return pltpu.CompilerParams(vmem_limit_bytes=VMEM_LIMIT)


def cost(flops, bytes_accessed):
    return pl.CostEstimate(flops=int(flops), bytes_accessed=int(bytes_accessed), transcendentals=0)


def vmem(shape, dtype):
    return pltpu.VMEM(shape, dtype)


def keep(x):
    return pltpu.with_memory_space_constraint(x, pltpu.VMEM)


def keep_scalars(x):
    return pltpu.with_memory_space_constraint(x, pltpu.SMEM)


def stay(x):
    return pltpu.with_memory_space_constraint(x, pltpu.HBM)


def grid_ij(edge):
    i = lax.broadcasted_iota(jnp.int32, (edge, edge), 0)
    j = lax.broadcasted_iota(jnp.int32, (edge, edge), 1)
    return i, j


def diag_row(block, i, j):
    return jnp.sum(jnp.where(i == j, block, 0.0), axis=0, keepdims=True)


SOURCE, SECTOR, PLACE, TARGET, RANK, NUMBER = range(6)


def pack(cut, group, table, env, rows_ref, out, before=lambda g, carry: carry, carry=0):
    low, high = cut
    edge = env.shape[-1]
    i, j = grid_ij(edge)

    def body(g, carry):
        carry = before(g, carry)
        for d in range(group):
            p = g * group + d
            first = env[table[SOURCE, 2 * p]].astype(F32)
            second = env[table[SOURCE, 2 * p + 1]].astype(F32)
            at = pl.multiple_of((p - low) * edge, edge)
            out[pl.ds(at, edge), :] = jnp.where(i <= j, first, second).astype(BF16)
            rows_ref[pl.ds(2 * (p - low), 1), :] = diag_row(first, i, j)
            rows_ref[pl.ds(2 * (p - low) + 1, 1), :] = diag_row(second, i, j)
        return carry

    pairs = (table[NUMBER, 0] + 1) // 2
    stop = (jnp.minimum(high, pairs) + group - 1) // group
    carry = lax.fori_loop(low // group, stop, body, carry)
    size = (high - low) * edge
    out[size:, :] = rows_ref[: out.shape[0] - size, :].astype(BF16)
    return carry


def split_rows(value):
    high = value.astype(BF16).astype(F32)
    middle = (value - high).astype(BF16).astype(F32)
    low = value - high - middle
    pad = jnp.zeros((weight_rows(value.shape[0]) - 3 * value.shape[0], value.shape[1]), F32)
    return jnp.concatenate([high, middle, low, pad], axis=0).astype(BF16)


def joined_rows(rows, sectors):
    rows = rows.astype(F32)
    return rows[:sectors] + rows[sectors : 2 * sectors] + rows[2 * sectors : 3 * sectors]


def weight_rows(sectors):
    return -(-3 * sectors // 16) * 16


def pack_kernel(cut, group, mask_hbm, ranks_hbm, weight_hbm, env_hbm, *refs):
    out, table, env, mask_ref, ranks_ref, weight_ref, rows_ref, scalar_sems, sems = refs
    sectors, chans = mask_ref.shape
    blocks = sectors * chans
    scalars = [
        pltpu.make_async_copy(mask_hbm, mask_ref, scalar_sems.at[0]),
        pltpu.make_async_copy(ranks_hbm, ranks_ref, scalar_sems.at[1]),
        pltpu.make_async_copy(weight_hbm, weight_ref, scalar_sems.at[2]),
    ]
    for c in scalars:
        c.start()

    def fetch(s):
        part = pl.ds(s * chans, chans)
        return pltpu.make_async_copy(env_hbm.at[part], env.at[part], sems.at[s])

    for s in range(sectors):
        fetch(s).start()
    for c in scalars:
        c.wait()
    n = jnp.int32(0)
    for s in range(sectors):
        table[RANK, s] = ranks_ref[s]
        k = jnp.int32(0)
        for w in range(chans):
            m = mask_ref[s, w]
            table[SOURCE, n] = jnp.int32(s * chans + w)
            table[SECTOR, n] = jnp.int32(s)
            table[PLACE, n] = k
            table[TARGET, n] = s * chans + k
            n = n + m
            k = k + m
    for d in range(2 * group):
        table[SOURCE, n + d] = jnp.int32(0)
        table[SECTOR, n + d] = jnp.int32(0)
        table[PLACE, n + d] = jnp.int32(chans)
        table[TARGET, n + d] = jnp.int32(blocks)
    table[NUMBER, 0] = n

    def wait(s, carry):
        fetch(s).wait()
        return carry

    def before(g, here):
        final = jnp.maximum(jnp.minimum(2 * (g + 1) * group, n) - 1, 0)
        need = jnp.maximum(here, table[SECTOR, final] + 1)
        lax.fori_loop(here, need, wait, 0)
        return need

    extra = weight_rows(sectors)
    out[out.shape[0] - extra :, :] = split_rows(weight_ref[...])
    bulk = out.at[: out.shape[0] - extra, :]
    here = pack(cut, group, table, env, rows_ref, bulk, before, jnp.int32(0))
    lax.fori_loop(here, sectors, wait, 0)


def rest_kernel(cuts, group, table, env, *refs):
    chunks, rows_ref = refs[-len(cuts) - 1 : -1], refs[-1]
    for cut, out in zip(cuts, chunks):
        pack(cut, group, table, env, rows_ref, out)


def put(k, block, side, table, outer, buf):
    buf[side, table[TARGET, k]] = (block * outer[table[SECTOR, k]]).astype(BF16)


def put_diag(k, row, side, table, outer_diag, diags):
    s = table[SECTOR, k]
    scaled = row * outer_diag[pl.ds(s, 1), :]
    diags[side, s, pl.ds(table[PLACE, k], 1), :] = scaled.astype(BF16).astype(F32)


def unpack(cut, group, side, chunk, table, outer, outer_diag, buf, diags, rows_ref):
    low, high = cut
    edge = chunk.shape[-1]
    i, j = grid_ij(edge)
    n = table[NUMBER, 0]
    size = (high - low) * edge
    rows_ref[: chunk.shape[0] - size, :] = chunk[size:, :].astype(F32)

    def body(g, carry):
        for d in range(group):
            p = g * group + d
            at = pl.multiple_of((p - low) * edge, edge)
            both = chunk[pl.ds(at, edge), :].astype(F32)
            flip = both.T
            row = rows_ref[pl.ds(2 * (p - low), 1), :]
            other = rows_ref[pl.ds(2 * (p - low) + 1, 1), :]
            put(2 * p, jnp.where(i <= j, both, flip), side, table, outer, buf)
            lower = jnp.where(i > j, both, jnp.where(i == j, other, flip))
            put(2 * p + 1, lower, side, table, outer, buf)
            put_diag(2 * p, row, side, table, outer_diag, diags)
            put_diag(2 * p + 1, other, side, table, outer_diag, diags)
        return carry

    stop = (jnp.minimum(high, (n + 1) // 2) + group - 1) // group
    lax.fori_loop(low // group, stop, body, 0)


def own_kernel(group, chans, table, env, own_site, other_site, *refs):
    weights, (buf, diags, prefix, vec, mine) = refs[:-5], refs[-5:]
    sectors, edge = mine.shape[0], mine.shape[-1]
    at = lax.axis_index("chain")
    side = at % 2
    before = jnp.ones((sectors, edge), F32)
    for c in range(len(weights) + 1):
        value = before
        for d, weight in enumerate(weights[1:], 2):
            value = jnp.where(at ^ d == c, weight[...], value)
        before = jnp.where(c < at - side, before * value, before)
    prefix[...] = before
    own_weight = weights[0][...]
    own_weight = jnp.where(side == 0, before * own_weight, own_weight)
    i, j = grid_ij(edge)
    for s in range(sectors):
        row = jnp.broadcast_to(own_weight[s : s + 1, :], (edge, edge))
        mine[s] = row.T * row
        first = jnp.where(side == 0, own_site[s], other_site[s])
        second = jnp.where(side == 0, other_site[s], own_site[s])
        start = jnp.dot(first, second, preferred_element_type=F32).T
        vec[s] = jnp.where(j < table[RANK, s], start, 0.0)
    diags[...] = jnp.zeros_like(diags)

    def wipe(t, carry):
        buf[0, t] = jnp.zeros((edge, edge), BF16)
        buf[1, t] = jnp.zeros((edge, edge), BF16)
        return carry

    lax.fori_loop(0, sectors * chans, wipe, 0)
    step = 2 * group

    def body(g, carry):
        for d in range(step):
            k = step * g + d
            s = table[SECTOR, k]
            block = (env[table[SOURCE, k]].astype(F32) * mine[s]).astype(BF16)
            buf[side, table[TARGET, k]] = block
            diags[side, s, pl.ds(table[PLACE, k], 1), :] = diag_row(block.astype(F32), i, j)
        return carry

    lax.fori_loop(0, (table[NUMBER, 0] + step - 1) // step, body, 0)


def outer_kernel(cut, group, table, prefix, chunk, *refs):
    _, _, buf, diags, outer, outer_diag, rows_ref = refs
    sectors, edge = outer.shape[0], outer.shape[-1]
    side = lax.axis_index("chain") % 2
    extra = weight_rows(sectors)
    start = chunk.shape[0] - extra
    other_weight = joined_rows(chunk[start:, :], sectors)
    other_weight = jnp.where(side == 0, other_weight, prefix[...] * other_weight)
    outer_diag[...] = other_weight * other_weight
    for s in range(sectors):
        row = jnp.broadcast_to(other_weight[s : s + 1, :], (edge, edge))
        outer[s] = row.T * row
    bulk = chunk.at[:start, :]
    unpack(cut, group, 1 - side, bulk, table, outer, outer_diag, buf, diags, rows_ref)


def mid_kernel(cut, group, table, outer, outer_diag, chunk, *refs):
    _, _, buf, diags, rows_ref = refs
    side = lax.axis_index("chain") % 2
    unpack(cut, group, 1 - side, chunk, table, outer, outer_diag, buf, diags, rows_ref)


def apply_all(vectors, table, buf, vec, image, part, inner):
    sectors, edge = vec.shape[0], vec.shape[-1]
    chans = inner.shape[-1] // edge
    for s in range(sectors):
        vector = vectors(s)
        vec[s] = vector
        right = buf[1, s * chans : (s + 1) * chans].reshape(chans * edge, edge)
        image_t = jnp.dot(right, vector.astype(BF16), preferred_element_type=F32).astype(BF16)
        for c in range(chans):
            inner[s, :, c * edge : (c + 1) * edge] = image_t[c * edge : (c + 1) * edge]
    _, j = grid_ij(edge)
    along = jnp.zeros((edge, edge), F32)
    square = jnp.zeros((edge, edge), F32)
    for s in range(sectors):
        left = buf[0, s * chans : (s + 1) * chans].reshape(chans * edge, edge)
        hv = jnp.dot(inner[s], left, preferred_element_type=F32)
        hv = jnp.where(j < table[RANK, s], hv, 0.0)
        image[s] = hv
        vector = vec[s]
        along = along + vector * hv
        square = square + vector * vector
    store_sums(part, along, square)


def store_sums(part, along, square):
    part[0:1, :] = jnp.sum(along, axis=0, keepdims=True)
    part[1:2, :] = jnp.sum(square, axis=0, keepdims=True)


def first_kernel(cuts, group, table, outer, outer_diag, vec_in, *refs):
    chunks = refs[: len(cuts)]
    _, _, buf, diags, vec, image, dh, part, inner, rows_ref, spare, sem = refs[len(cuts) :]
    sectors = vec.shape[0]
    side = lax.axis_index("chain") % 2
    unpack(cuts[0], group, 1 - side, chunks[0], table, outer, outer_diag, buf, diags, rows_ref)

    @pl.when(table[NUMBER, 0] > 2 * cuts[1][0])
    def _():
        copy = pltpu.make_async_copy(chunks[1], spare, sem)
        copy.start()
        copy.wait()
        unpack(cuts[1], group, 1 - side, spare, table, outer, outer_diag, buf, diags, rows_ref)

    chans = inner.shape[-1] // vec.shape[-1]
    used = lax.broadcasted_iota(jnp.int32, diags.shape[2:], 0) < chans
    for s in range(sectors):
        dh[s] = lax.dot_general(
            jnp.where(used, diags[1, s], 0.0).astype(BF16),
            jnp.where(used, diags[0, s], 0.0).astype(BF16),
            (((0,), (0,)), ((), ())),
            preferred_element_type=F32,
        )
    apply_all(lambda s: vec_in[s], table, buf, vec, image, part, inner)


def joined(parts):
    values = [p[...] for p in parts]
    while len(values) > 1:
        values = [values[k] + values[k + 1] for k in range(0, len(values), 2)]
    total = values[0]
    along = jnp.sum(total[0:1, :], axis=1, keepdims=True)
    square = jnp.sum(total[1:2, :], axis=1, keepdims=True)
    return along, square


def step_of(count, along, square):
    theta = along / (square + EPS)
    scale = 1.0 / jnp.sqrt(square / count + EPS)

    def step(vector, hv, dh):
        resid = hv - theta * vector
        return (vector - STEP_SIZE * resid / (1.0 + jnp.abs(dh - theta))) * scale

    return theta, step


def iter_kernel(count, partners, table, buf, vec_in, image_in, dh, *refs):
    parts = refs[:partners]
    vec, image, part, inner = refs[partners:]
    _, step = step_of(count, *joined(parts))
    apply_all(
        lambda s: step(vec_in[s], image_in[s], dh[s]), table, buf, vec, image, part, inner
    )


def last_kernel(count, partners, vec_in, image_in, dh, *refs):
    parts = refs[:partners]
    vec, part, energy = refs[partners:]
    theta, step = step_of(count, *joined(parts))
    square = jnp.zeros(dh.shape[1:], F32)
    for s in range(dh.shape[0]):
        vector = step(vec_in[s], image_in[s], dh[s])
        vec[s] = vector
        square = square + vector * vector
    store_sums(part, square, square)
    energy[...] = jnp.broadcast_to(theta, energy.shape)


def turn_kernel(vec, turned):
    for s in range(vec.shape[0]):
        turned[s] = vec[s].T


def psi_kernel(count, partners, vec, *refs):
    parts = refs[:partners]
    psi = refs[partners]
    square, _ = joined(parts)
    scale = 1.0 / jnp.sqrt(square / count + EPS)
    for s in range(psi.shape[0]):
        psi[s] = (vec[s] * scale).astype(BF16)


def swap(value):
    return swapped(value, "chain", 1)


def swapped(value, axis, mask):
    size = lax.axis_size(axis)
    return lax.ppermute(value, axis, [(k, k ^ mask) for k in range(size)])


def from_all(value, axis):
    return [value] + [swapped(value, axis, m) for m in range(1, lax.axis_size(axis))]


def gather_parts(part):
    return [keep(p) for p in from_all(part, "tensor")]


def local(env, site, seg_weight, ranks, mpo_mask):
    sectors, chans, edge = env.shape[1:4]
    blocks = sectors * chans
    tensor = lax.axis_size("tensor")
    count = float(sectors * tensor * edge * edge)
    group = 4
    pairs = -(-blocks // (2 * group)) * group
    base = min(pairs, -(-pairs * 3 // 5 // (2 * group)) * 2 * group)
    third = max(base // 6 // group, 1) * group
    marks = [0, base // 2, base - third, base, pairs]
    cuts = list(zip(marks[:-1], marks[1:]))
    tails = [-(-2 * (c[1] - c[0]) // 16) * 16 for c in cuts]
    rows = [(c[1] - c[0]) * edge + t for c, t in zip(cuts, tails)]
    rows[0] += weight_rows(sectors)
    block_bytes = 2 * edge * edge
    big = sectors * edge * edge * 4

    own_weight = seg_weight[0]
    weights = [swapped(own_weight, "chain", m) for m in range(2, lax.axis_size("chain"))]
    other_site = swap(site[0])
    flat_env = env.reshape(blocks, edge, edge)
    state_shape = (sectors, edge, edge)
    state = vmem(state_shape, F32)
    row_shape = vmem((sectors, edge), F32)

    hbm = pl.BlockSpec(memory_space=pltpu.HBM)
    dma = pltpu.SemaphoreType.DMA
    tail_rows = pltpu.VMEM((max(tails), edge), F32)
    first_sent, table, env_here = pl.pallas_call(
        functools.partial(pack_kernel, cuts[0], group),
        out_shape=[
            vmem((rows[0], edge), BF16),
            pltpu.SMEM((6, blocks + 2 * group), jnp.int32),
            vmem((blocks, edge, edge), BF16),
        ],
        in_specs=[hbm] * 4,
        out_specs=[VM, SM, VM],
        scratch_shapes=[
            pltpu.SMEM(mpo_mask.shape, jnp.int32),
            pltpu.SMEM(ranks.shape, jnp.int32),
            pltpu.VMEM((sectors, edge), F32),
            tail_rows,
            dma((3,)),
            dma((sectors,)),
        ],
        compiler_params=params(),
        cost_estimate=cost(PACK_COST, 2 * blocks * block_bytes),
        name="pack",
    )(stay(mpo_mask), stay(ranks), stay(own_weight), stay(flat_env))
    table = keep_scalars(table)
    sent = pl.pallas_call(
        functools.partial(rest_kernel, cuts[1:], group),
        out_shape=[vmem((r, edge), BF16) for r in rows[1:]],
        in_specs=[SM, VM] + [hbm] * (1 + len(weights)),
        out_specs=[VM] * (len(cuts) - 1),
        scratch_shapes=[tail_rows],
        compiler_params=params(),
        cost_estimate=cost(REST_COST, 2 * blocks * block_bytes),
        name="rest",
    )(table, keep(env_here), stay(other_site), *[stay(w) for w in weights])
    sent = [first_sent, *sent]
    got = [swap(c) for c in sent[:-1]]
    active = jnp.sum(mpo_mask)
    got.append(lax.cond(active > 2 * base, swap, lambda c: c, sent[-1]))
    got = [keep(g) for g in got[:-1]] + [stay(got[-1])]

    buf_shape = vmem((2, blocks + 1, edge, edge), BF16)
    diag_shape = vmem((2, sectors, -(-(chans + 1) // 16) * 16, edge), F32)
    sums = vmem((2, edge), F32)
    inner_shape = pltpu.VMEM((sectors, edge, chans * edge), BF16)
    work = 4.0 * blocks * edge**3

    buf, diags, prefix, vec = pl.pallas_call(
        functools.partial(own_kernel, group, chans),
        out_shape=[buf_shape, diag_shape, row_shape, state],
        in_specs=[SM] + [VM] * (4 + len(weights)),
        out_specs=[VM] * 4,
        scratch_shapes=[pltpu.VMEM(state_shape, F32)],
        compiler_params=params(),
        cost_estimate=cost(0, 0),
        name="own",
    )(table, keep(env_here), site[0], stay(other_site), own_weight, *[stay(w) for w in weights])

    buf, diags, outer, outer_diag = pl.pallas_call(
        functools.partial(outer_kernel, cuts[0], group),
        out_shape=[buf_shape, diag_shape, state, row_shape],
        in_specs=[SM] + [VM] * 4,
        out_specs=[VM] * 4,
        scratch_shapes=[tail_rows],
        input_output_aliases={3: 0, 4: 1},
        compiler_params=params(),
        cost_estimate=cost(0, 0),
        name="outer",
    )(table, keep(prefix), got[0], keep(buf), keep(diags))

    for cut, chunk in zip(cuts[1:-2], got[1:]):
        buf, diags = pl.pallas_call(
            functools.partial(mid_kernel, cut, group),
            out_shape=[buf_shape, diag_shape],
            in_specs=[SM] + [VM] * 5,
            out_specs=[VM] * 2,
            scratch_shapes=[tail_rows],
            input_output_aliases={4: 0, 5: 1},
            compiler_params=params(),
            cost_estimate=cost(0, 0),
            name="mid",
        )(table, keep(outer), keep(outer_diag), chunk, keep(buf), keep(diags))

    buf, diags, vec, image, dh, part = pl.pallas_call(
        functools.partial(first_kernel, cuts[-2:], group),
        out_shape=[buf_shape, diag_shape, state, state, state, sums],
        in_specs=[SM] + [VM] * 4 + [hbm] + [VM] * 2,
        out_specs=[VM] * 6,
        scratch_shapes=[inner_shape, tail_rows, pltpu.VMEM((rows[-1], edge), BF16), dma(())],
        input_output_aliases={6: 0, 7: 1},
        compiler_params=params(),
        cost_estimate=cost(work, 2 * blocks * block_bytes),
        name="first",
    )(
        table, keep(outer), keep(outer_diag), keep(vec), *got[-2:],
        keep(buf), keep(diags),
    )

    for _ in range(ITERS - 1):
        parts = gather_parts(part)
        vec, image, part = pl.pallas_call(
            functools.partial(iter_kernel, count, tensor),
            out_shape=[state, state, sums],
            in_specs=[SM] + [VM] * (4 + tensor),
            out_specs=[VM] * 3,
            scratch_shapes=[inner_shape],
            compiler_params=params(),
            cost_estimate=cost(work, 2 * blocks * block_bytes),
            name="iterate",
        )(table, keep(buf), keep(vec), keep(image), keep(dh), *parts)

    parts = gather_parts(part)
    vec, part, energy = pl.pallas_call(
        functools.partial(last_kernel, count, tensor),
        out_shape=[state, sums, jax.ShapeDtypeStruct((1, edge), F32)],
        in_specs=[VM] * (3 + tensor),
        out_specs=[VM] * 3,
        compiler_params=params(),
        cost_estimate=cost(0, 3 * big),
        name="last",
    )(keep(vec), keep(image), keep(dh), *parts)
    parts = gather_parts(part)
    turned = pl.pallas_call(
        turn_kernel,
        out_shape=state,
        in_specs=[VM],
        out_specs=VM,
        compiler_params=params(),
        cost_estimate=cost(0, 2 * big),
        name="turn",
    )(keep(vec))
    psi = pl.pallas_call(
        functools.partial(psi_kernel, count, tensor),
        out_shape=jax.ShapeDtypeStruct(state_shape, BF16),
        in_specs=[VM] * (1 + tensor),
        out_specs=VM,
        compiler_params=params(),
        cost_estimate=cost(0, big),
        name="psi",
    )(keep(turned), *parts)
    return psi[None], energy[0, :1]


def solution(mesh):
    in_specs = (
        P(("cyl", "chain"), "tensor", None, None, None),
        P(("cyl", "chain"), "tensor", None, None),
        P(("cyl", "chain"), "tensor", None),
        P(("cyl", "tensor")),
        P(("cyl", "tensor"), None),
    )
    out_specs = (P(("cyl", "chain"), "tensor", None, None), P(("cyl", "chain")))
    return jax.shard_map(local, mesh=mesh, in_specs=in_specs, out_specs=out_specs, check_vma=False)
```

```python
import functools

import jax
import jax.numpy as jnp
from jax import lax
from jax.experimental import pallas as pl
from jax.experimental.pallas import tpu as pltpu
from jax.sharding import PartitionSpec as P

ITERS = 4
STEP_SIZE = 0.5
PACK_COST = 10**7
REST_COST = 10**10
OWN_COST = 0
EPS = 1e-6
BF16 = jnp.bfloat16
F32 = jnp.float32
VMEM_LIMIT = 16 * 2**20
VM = pl.BlockSpec(memory_space=pltpu.VMEM)
SM = pl.BlockSpec(memory_space=pltpu.SMEM)


def params():
    return pltpu.CompilerParams(vmem_limit_bytes=VMEM_LIMIT)


def cost(flops, bytes_accessed):
    return pl.CostEstimate(flops=int(flops), bytes_accessed=int(bytes_accessed), transcendentals=0)


def vmem(shape, dtype):
    return pltpu.VMEM(shape, dtype)


def keep(x):
    return pltpu.with_memory_space_constraint(x, pltpu.VMEM)


def keep_scalars(x):
    return pltpu.with_memory_space_constraint(x, pltpu.SMEM)


def stay(x):
    return pltpu.with_memory_space_constraint(x, pltpu.HBM)


def grid_ij(edge):
    i = lax.broadcasted_iota(jnp.int32, (edge, edge), 0)
    j = lax.broadcasted_iota(jnp.int32, (edge, edge), 1)
    return i, j


def diag_row(block, i, j):
    return jnp.sum(jnp.where(i == j, block, 0.0), axis=0, keepdims=True)


SOURCE, SECTOR, PLACE, TARGET, RANK, COUNT, NUMBER = range(7)


def pack(cut, group, table, env, rows_ref, out, before=lambda g, carry: carry, after=None, carry=0):
    low, high = cut
    edge = env.shape[-1]
    i, j = grid_ij(edge)

    def body(g, carry):
        carry = before(g, carry)
        for d in range(group):
            p = g * group + d
            first = env[table[SOURCE, 2 * p]].astype(F32)
            second = env[table[SOURCE, 2 * p + 1]].astype(F32)
            at = pl.multiple_of((p - low) * edge, edge)
            out[pl.ds(at, edge), :] = jnp.where(i <= j, first, second).astype(BF16)
            rows_ref[pl.ds(2 * (p - low), 1), :] = diag_row(first, i, j)
            rows_ref[pl.ds(2 * (p - low) + 1, 1), :] = diag_row(second, i, j)
        if after is not None:
            after(g)
        return carry

    pairs = (table[NUMBER, 0] + 1) // 2
    stop = (jnp.minimum(high, pairs) + group - 1) // group
    carry = lax.fori_loop(low // group, stop, body, carry)
    size = (high - low) * edge
    out[size:, :] = rows_ref[: out.shape[0] - size, :].astype(BF16)
    return carry


def split_rows(value):
    high = value.astype(BF16).astype(F32)
    middle = (value - high).astype(BF16).astype(F32)
    low = value - high - middle
    pad = jnp.zeros((weight_rows(value.shape[0]) - 3 * value.shape[0], value.shape[1]), F32)
    return jnp.concatenate([high, middle, low, pad], axis=0).astype(BF16)


def joined_rows(rows, sectors):
    rows = rows.astype(F32)
    return rows[:sectors] + rows[sectors : 2 * sectors] + rows[2 * sectors : 3 * sectors]


def weight_rows(sectors):
    return -(-3 * sectors // 16) * 16


def pack_kernel(cut, group, mask_hbm, ranks_hbm, weight_hbm, env_hbm, *refs):
    out_hbm, table, flag, env, out, mask_ref, ranks_ref, weight_ref, rows_ref = refs[:9]
    scalar_sems, sems, out_sems = refs[9:]
    sectors, chans = mask_ref.shape
    blocks = sectors * chans
    scalars = [
        pltpu.make_async_copy(mask_hbm, mask_ref, scalar_sems.at[0]),
        pltpu.make_async_copy(ranks_hbm, ranks_ref, scalar_sems.at[1]),
        pltpu.make_async_copy(weight_hbm, weight_ref, scalar_sems.at[2]),
    ]
    for c in scalars:
        c.start()

    def fetch(s):
        part = pl.ds(s * chans, chans)
        return pltpu.make_async_copy(env_hbm.at[part], env.at[part], sems.at[s])

    for s in range(sectors):
        fetch(s).start()
    for c in scalars:
        c.wait()
    n = jnp.int32(0)
    for s in range(sectors):
        table[RANK, s] = ranks_ref[s]
        k = jnp.int32(0)
        for w in range(chans):
            m = mask_ref[s, w]
            table[SOURCE, n] = jnp.int32(s * chans + w)
            table[SECTOR, n] = jnp.int32(s)
            table[PLACE, n] = k
            table[TARGET, n] = s * chans + k
            n = n + m
            k = k + m
        table[COUNT, s] = k
    for d in range(2 * group):
        table[SOURCE, n + d] = jnp.int32(0)
        table[SECTOR, n + d] = jnp.int32(0)
        table[PLACE, n + d] = jnp.int32(chans)
        table[TARGET, n + d] = jnp.int32(blocks)
    table[NUMBER, 0] = n
    flag[0] = n

    def wait(s, carry):
        fetch(s).wait()
        return carry

    def before(g, here):
        final = jnp.maximum(jnp.minimum(2 * (g + 1) * group, n) - 1, 0)
        need = jnp.maximum(here, table[SECTOR, final] + 1)
        lax.fori_loop(here, need, wait, 0)
        return need

    extra = weight_rows(sectors)
    edge = env.shape[-1]
    size = (cut[1] - cut[0]) * edge
    out[out.shape[0] - extra :, :] = split_rows(weight_ref[...])
    bulk = out.at[: out.shape[0] - extra, :]

    def send(g):
        part = pl.ds(pl.multiple_of(g * group * edge, group * edge), group * edge)
        return pltpu.make_async_copy(out.at[part], out_hbm.at[part], out_sems.at[g])

    def after(g):
        send(g).start()

    here = pack(cut, group, table, env, rows_ref, bulk, before, after, jnp.int32(0))
    tail = pltpu.make_async_copy(out.at[size:], out_hbm.at[size:], out_sems.at[cut[1] // group])
    tail.start()
    lax.fori_loop(here, sectors, wait, 0)
    tail.wait()

    def drain(g, carry):
        send(g).wait()
        return carry

    stop = (jnp.minimum(cut[1], (n + 1) // 2) + group - 1) // group
    lax.fori_loop(0, stop, drain, 0)


def rest_kernel(cuts, group, table, env, *refs):
    chunks, rows_ref = refs[-len(cuts) - 1 : -1], refs[-1]
    for cut, out in zip(cuts, chunks):
        pack(cut, group, table, env, rows_ref, out)


def put(k, block, side, table, outer, buf):
    buf[side, table[TARGET, k]] = (block * outer[table[SECTOR, k]]).astype(BF16)


def put_diag(k, row, side, table, outer_diag, diags):
    s = table[SECTOR, k]
    scaled = row * outer_diag[pl.ds(s, 1), :]
    diags[side, s, pl.ds(table[PLACE, k], 1), :] = scaled.astype(BF16).astype(F32)


def unpack(cut, group, side, chunk, table, outer, outer_diag, buf, diags, rows_ref):
    low, high = cut
    edge = chunk.shape[-1]
    i, j = grid_ij(edge)
    n = table[NUMBER, 0]
    size = (high - low) * edge
    rows_ref[: chunk.shape[0] - size, :] = chunk[size:, :].astype(F32)

    def body(g, carry):
        for d in range(group):
            p = g * group + d
            at = pl.multiple_of((p - low) * edge, edge)
            both = chunk[pl.ds(at, edge), :].astype(F32)
            flip = both.T
            row = rows_ref[pl.ds(2 * (p - low), 1), :]
            other = rows_ref[pl.ds(2 * (p - low) + 1, 1), :]
            put(2 * p, jnp.where(i <= j, both, flip), side, table, outer, buf)
            lower = jnp.where(i > j, both, jnp.where(i == j, other, flip))
            put(2 * p + 1, lower, side, table, outer, buf)
            put_diag(2 * p, row, side, table, outer_diag, diags)
            put_diag(2 * p + 1, other, side, table, outer_diag, diags)
        return carry

    stop = (jnp.minimum(high, (n + 1) // 2) + group - 1) // group
    lax.fori_loop(low // group, stop, body, 0)


def widths(sectors, chans):
    parts = [10 if p < -(-sectors // 8) else 8 if p < sectors // 2 else 6 for p in range(sectors)]
    return [min(chans, -(-chans * part // 20) * 2) for part in parts]


def make_plan(plan, table, caps, chans):
    sectors = len(caps)
    counts = [table[COUNT, s] for s in range(sectors)]
    places = []
    for s in range(sectors):
        place = jnp.int32(0)
        for t in range(sectors):
            if t != s:
                ahead = counts[t] >= counts[s] if t < s else counts[t] > counts[s]
                place = place + ahead.astype(jnp.int32)
        plan[COUNT, place] = jnp.int32(s)
        plan[RANK, place] = table[RANK, s]
        places.append(place)
    fits = jnp.int32(1)
    for k, cap in enumerate(caps):
        fits = fits * (table[COUNT, plan[COUNT, k]] <= cap).astype(jnp.int32)
    n = table[NUMBER, 0]
    plan[NUMBER, 0] = n
    plan[NUMBER, 1] = fits
    start = jnp.int32(0)
    for s in range(sectors):

        def body(c, k, s=s):
            plan[SOURCE, k] = table[SOURCE, k]
            plan[SECTOR, k] = places[s]
            plan[PLACE, k] = c
            plan[TARGET, k] = places[s] * chans + c
            return k + 1

        start = lax.fori_loop(0, counts[s], body, start)

    def rest(k, carry):
        for row in (SOURCE, SECTOR, PLACE, TARGET):
            plan[row, k] = table[row, k]
        return carry

    lax.fori_loop(n, n + table.shape[1] - sectors * chans, rest, 0)


def own_kernel(group, chans, _, table, env, own_site, other_site, *refs):
    weights, (buf, diags, prefix, vec, plan, mine, rows_ref) = refs[:-7], refs[-7:]
    sectors, edge = mine.shape[0], mine.shape[-1]
    make_plan(plan, table, widths(sectors, chans), chans)
    at = lax.axis_index("chain")
    side = at % 2
    before = jnp.ones((sectors, edge), F32)
    for c in range(len(weights) + 1):
        value = before
        for d, weight in enumerate(weights[1:], 2):
            value = jnp.where(at ^ d == c, weight[...], value)
        before = jnp.where(c < at - side, before * value, before)
    prefix[...] = before
    own_weight = weights[0][...]
    rows_ref[...] = jnp.where(side == 0, before * own_weight, own_weight)
    i, j = grid_ij(edge)
    for s in range(sectors):
        old = plan[COUNT, s]
        row = jnp.broadcast_to(rows_ref[pl.ds(old, 1), :], (edge, edge))
        mine[s] = row.T * row
        first = jnp.where(side == 0, own_site[old], other_site[old])
        second = jnp.where(side == 0, other_site[old], own_site[old])
        start = jnp.dot(first, second, preferred_element_type=F32).T
        vec[s] = jnp.where(j < plan[RANK, s], start, 0.0)
    diags[...] = jnp.zeros_like(diags)

    def wipe(t, carry):
        buf[0, t] = jnp.zeros((edge, edge), BF16)
        buf[1, t] = jnp.zeros((edge, edge), BF16)
        return carry

    lax.fori_loop(0, sectors * chans, wipe, 0)
    step = 2 * group

    def body(g, carry):
        for d in range(step):
            k = step * g + d
            s = plan[SECTOR, k]
            block = (env[plan[SOURCE, k]].astype(F32) * mine[s]).astype(BF16)
            buf[side, plan[TARGET, k]] = block
            diags[side, s, pl.ds(plan[PLACE, k], 1), :] = diag_row(block.astype(F32), i, j)
        return carry

    lax.fori_loop(0, (plan[NUMBER, 0] + step - 1) // step, body, 0)


def outer_kernel(cut, group, plan, prefix, chunk, *refs):
    _, _, buf, diags, outer, outer_diag, rows_ref, weight_ref = refs
    sectors, edge = outer.shape[0], outer.shape[-1]
    side = lax.axis_index("chain") % 2
    extra = weight_rows(sectors)
    start = chunk.shape[0] - extra
    other_weight = joined_rows(chunk[start:, :], sectors)
    weight_ref[...] = jnp.where(side == 0, other_weight, prefix[...] * other_weight)
    for s in range(sectors):
        row = weight_ref[pl.ds(plan[COUNT, s], 1), :]
        outer_diag[s : s + 1, :] = row * row
        row = jnp.broadcast_to(row, (edge, edge))
        outer[s] = row.T * row
    bulk = chunk.at[:start, :]
    unpack(cut, group, 1 - side, bulk, plan, outer, outer_diag, buf, diags, rows_ref)


def mid_kernel(cut, group, table, outer, outer_diag, chunk, *refs):
    _, _, buf, diags, rows_ref = refs
    side = lax.axis_index("chain") % 2
    unpack(cut, group, 1 - side, chunk, table, outer, outer_diag, buf, diags, rows_ref)


def apply_all(vectors, plan, *state):
    vec, inner = state[1], state[-1]
    sectors, chans = vec.shape[0], inner.shape[-1] // vec.shape[-1]
    fits = plan[NUMBER, 1]

    @pl.when(fits == 1)
    def _():
        apply_some(vectors, plan, widths(sectors, chans), *state)

    @pl.when(fits == 0)
    def _():
        apply_some(vectors, plan, [chans] * sectors, *state)


def apply_some(vectors, plan, caps, buf, vec, image, part, inner):
    sectors, edge = vec.shape[0], vec.shape[-1]
    chans = inner.shape[-1] // edge
    for s, cap in enumerate(caps):
        vector = vectors(s)
        vec[s] = vector
        right = buf[1, s * chans : s * chans + cap].reshape(cap * edge, edge)
        image_t = jnp.dot(right, vector.astype(BF16), preferred_element_type=F32).astype(BF16)
        for c in range(cap):
            inner[s, :, c * edge : (c + 1) * edge] = image_t[c * edge : (c + 1) * edge]
    _, j = grid_ij(edge)
    along = jnp.zeros((edge, edge), F32)
    square = jnp.zeros((edge, edge), F32)
    for s, cap in enumerate(caps):
        left = buf[0, s * chans : s * chans + cap].reshape(cap * edge, edge)
        hv = jnp.dot(inner[s, :, : cap * edge], left, preferred_element_type=F32)
        hv = jnp.where(j < plan[RANK, s], hv, 0.0)
        image[s] = hv
        vector = vec[s]
        along = along + vector * hv
        square = square + vector * vector
    store_sums(part, along, square)


def store_sums(part, along, square):
    part[0:1, :] = jnp.sum(along, axis=0, keepdims=True)
    part[1:2, :] = jnp.sum(square, axis=0, keepdims=True)


def first_kernel(cuts, group, plan, outer, outer_diag, vec_in, *refs):
    chunks = refs[: len(cuts)]
    _, _, buf, diags, vec, image, dh, part, inner, rows_ref, spare, sem = refs[len(cuts) :]
    sectors = vec.shape[0]
    side = lax.axis_index("chain") % 2
    unpack(cuts[0], group, 1 - side, chunks[0], plan, outer, outer_diag, buf, diags, rows_ref)

    @pl.when(plan[NUMBER, 0] > 2 * cuts[1][0])
    def _():
        copy = pltpu.make_async_copy(chunks[1], spare, sem)
        copy.start()
        copy.wait()
        unpack(cuts[1], group, 1 - side, spare, plan, outer, outer_diag, buf, diags, rows_ref)

    chans = inner.shape[-1] // vec.shape[-1]
    used = lax.broadcasted_iota(jnp.int32, diags.shape[2:], 0) < chans
    for s in range(sectors):
        dh[s] = lax.dot_general(
            jnp.where(used, diags[1, s], 0.0).astype(BF16),
            jnp.where(used, diags[0, s], 0.0).astype(BF16),
            (((0,), (0,)), ((), ())),
            preferred_element_type=F32,
        )
    apply_all(lambda s: vec_in[s], plan, buf, vec, image, part, inner)


def joined(parts):
    values = [p[...] for p in parts]
    while len(values) > 1:
        values = [values[k] + values[k + 1] for k in range(0, len(values), 2)]
    total = values[0]
    along = jnp.sum(total[0:1, :], axis=1, keepdims=True)
    square = jnp.sum(total[1:2, :], axis=1, keepdims=True)
    return along, square


def step_of(count, along, square):
    theta = along / (square + EPS)
    scale = 1.0 / jnp.sqrt(square / count + EPS)

    def step(vector, hv, dh):
        resid = hv - theta * vector
        return (vector - STEP_SIZE * resid / (1.0 + jnp.abs(dh - theta))) * scale

    return theta, step


def iter_kernel(count, partners, plan, buf, vec_in, image_in, dh, *refs):
    parts = refs[:partners]
    vec, image, part, inner = refs[partners:]
    _, step = step_of(count, *joined(parts))
    apply_all(
        lambda s: step(vec_in[s], image_in[s], dh[s]), plan, buf, vec, image, part, inner
    )


def last_kernel(count, partners, vec_in, image_in, dh, *refs):
    parts = refs[:partners]
    vec, part, energy = refs[partners:]
    theta, step = step_of(count, *joined(parts))
    square = jnp.zeros(dh.shape[1:], F32)
    for s in range(dh.shape[0]):
        vector = step(vec_in[s], image_in[s], dh[s])
        vec[s] = vector
        square = square + vector * vector
    store_sums(part, square, square)
    energy[...] = jnp.broadcast_to(theta, energy.shape)


def turn_kernel(vec, turned):
    for s in range(vec.shape[0]):
        turned[s] = vec[s].T


def psi_kernel(count, partners, plan, vec, *refs):
    parts = refs[:partners]
    psi = refs[partners]
    square, _ = joined(parts)
    scale = 1.0 / jnp.sqrt(square / count + EPS)
    for s in range(psi.shape[0]):
        psi[plan[COUNT, s]] = (vec[s] * scale).astype(BF16)


def swap(value):
    return swapped(value, "chain", 1)


def swapped(value, axis, mask):
    size = lax.axis_size(axis)
    return lax.ppermute(value, axis, [(k, k ^ mask) for k in range(size)])


def from_all(value, axis):
    return [value] + [swapped(value, axis, m) for m in range(1, lax.axis_size(axis))]


def gather_parts(part):
    return [keep(p) for p in from_all(part, "tensor")]


def local(env, site, seg_weight, ranks, mpo_mask):
    sectors, chans, edge = env.shape[1:4]
    blocks = sectors * chans
    tensor = lax.axis_size("tensor")
    count = float(sectors * tensor * edge * edge)
    group = 4
    pairs = -(-blocks // (2 * group)) * group
    base = min(pairs, -(-pairs * 3 // 5 // (2 * group)) * 2 * group)
    third = max(base // 6 // group, 1) * group
    marks = [0, base // 2, base - third, base, pairs]
    cuts = list(zip(marks[:-1], marks[1:]))
    tails = [-(-2 * (c[1] - c[0]) // 16) * 16 for c in cuts]
    rows = [(c[1] - c[0]) * edge + t for c, t in zip(cuts, tails)]
    rows[0] += weight_rows(sectors)
    block_bytes = 2 * edge * edge
    big = sectors * edge * edge * 4

    own_weight = seg_weight[0]
    weights = [swapped(own_weight, "chain", m) for m in range(2, lax.axis_size("chain"))]
    other_site = swap(site[0])
    flat_env = env.reshape(blocks, edge, edge)
    state_shape = (sectors, edge, edge)
    state = vmem(state_shape, F32)
    row_shape = vmem((sectors, edge), F32)
    table_shape = pltpu.SMEM((7, blocks + 2 * group), jnp.int32)

    hbm = pl.BlockSpec(memory_space=pltpu.HBM)
    dma = pltpu.SemaphoreType.DMA
    tail_rows = pltpu.VMEM((max(tails), edge), F32)
    first_sent, table, active, env_here = pl.pallas_call(
        functools.partial(pack_kernel, cuts[0], group),
        out_shape=[
            jax.ShapeDtypeStruct((rows[0], edge), BF16),
            table_shape,
            pltpu.SMEM((1,), jnp.int32),
            vmem((blocks, edge, edge), BF16),
        ],
        in_specs=[hbm] * 4,
        out_specs=[hbm, SM, SM, VM],
        scratch_shapes=[
            pltpu.VMEM((rows[0], edge), BF16),
            pltpu.SMEM(mpo_mask.shape, jnp.int32),
            pltpu.SMEM(ranks.shape, jnp.int32),
            pltpu.VMEM((sectors, edge), F32),
            tail_rows,
            dma((3,)),
            dma((sectors,)),
            dma((cuts[0][1] // group + 1,)),
        ],
        compiler_params=params(),
        cost_estimate=cost(PACK_COST, 2 * blocks * block_bytes),
        name="pack",
    )(stay(mpo_mask), stay(ranks), stay(own_weight), stay(flat_env))
    table, env_here = keep_scalars(table), keep(env_here)
    sent = pl.pallas_call(
        functools.partial(rest_kernel, cuts[1:], group),
        out_shape=[vmem((r, edge), BF16) for r in rows[1:]],
        in_specs=[SM, VM] + [hbm] * (1 + len(weights)),
        out_specs=[VM] * (len(cuts) - 1),
        scratch_shapes=[tail_rows],
        compiler_params=params(),
        cost_estimate=cost(REST_COST, 2 * blocks * block_bytes),
        name="rest",
    )(table, env_here, stay(other_site), *[stay(w) for w in weights])
    sent = [first_sent, *sent]
    got = [swap(c) for c in sent[:-1]]
    got.append(lax.cond(active[0] > 2 * base, swap, lambda c: c, sent[-1]))
    got = [keep(g) for g in got[:-1]] + [stay(got[-1])]

    buf_shape = vmem((2, blocks + 1, edge, edge), BF16)
    diag_shape = vmem((2, sectors, -(-(chans + 1) // 16) * 16, edge), F32)
    sums = vmem((2, edge), F32)
    inner_shape = pltpu.VMEM((sectors, edge, chans * edge), BF16)
    work = 4.0 * blocks * edge**3

    buf, diags, prefix, vec, plan = pl.pallas_call(
        functools.partial(own_kernel, group, chans),
        out_shape=[buf_shape, diag_shape, row_shape, state, table_shape],
        in_specs=[hbm, SM] + [VM] * (4 + len(weights)),
        out_specs=[VM] * 4 + [SM],
        scratch_shapes=[pltpu.VMEM(state_shape, F32), pltpu.VMEM((sectors, edge), F32)],
        compiler_params=params(),
        cost_estimate=cost(OWN_COST, 0),
        name="own",
    )(got[-1], table, env_here, site[0], stay(other_site), own_weight, *[stay(w) for w in weights])
    plan = keep_scalars(plan)

    buf, diags, outer, outer_diag = pl.pallas_call(
        functools.partial(outer_kernel, cuts[0], group),
        out_shape=[buf_shape, diag_shape, state, row_shape],
        in_specs=[SM] + [VM] * 4,
        out_specs=[VM] * 4,
        scratch_shapes=[tail_rows, pltpu.VMEM((sectors, edge), F32)],
        input_output_aliases={3: 0, 4: 1},
        compiler_params=params(),
        cost_estimate=cost(0, 0),
        name="outer",
    )(plan, keep(prefix), got[0], keep(buf), keep(diags))

    for cut, chunk in zip(cuts[1:-2], got[1:]):
        buf, diags = pl.pallas_call(
            functools.partial(mid_kernel, cut, group),
            out_shape=[buf_shape, diag_shape],
            in_specs=[SM] + [VM] * 5,
            out_specs=[VM] * 2,
            scratch_shapes=[tail_rows],
            input_output_aliases={4: 0, 5: 1},
            compiler_params=params(),
            cost_estimate=cost(0, 0),
            name="mid",
        )(plan, keep(outer), keep(outer_diag), chunk, keep(buf), keep(diags))

    buf, diags, vec, image, dh, part = pl.pallas_call(
        functools.partial(first_kernel, cuts[-2:], group),
        out_shape=[buf_shape, diag_shape, state, state, state, sums],
        in_specs=[SM] + [VM] * 4 + [hbm] + [VM] * 2,
        out_specs=[VM] * 6,
        scratch_shapes=[inner_shape, tail_rows, pltpu.VMEM((rows[-1], edge), BF16), dma(())],
        input_output_aliases={6: 0, 7: 1},
        compiler_params=params(),
        cost_estimate=cost(work, 2 * blocks * block_bytes),
        name="first",
    )(
        plan, keep(outer), keep(outer_diag), keep(vec), *got[-2:],
        keep(buf), keep(diags),
    )

    for _ in range(ITERS - 1):
        parts = gather_parts(part)
        vec, image, part = pl.pallas_call(
            functools.partial(iter_kernel, count, tensor),
            out_shape=[state, state, sums],
            in_specs=[SM] + [VM] * (4 + tensor),
            out_specs=[VM] * 3,
            scratch_shapes=[inner_shape],
            compiler_params=params(),
            cost_estimate=cost(work, 2 * blocks * block_bytes),
            name="iterate",
        )(plan, keep(buf), keep(vec), keep(image), keep(dh), *parts)

    parts = gather_parts(part)
    vec, part, energy = pl.pallas_call(
        functools.partial(last_kernel, count, tensor),
        out_shape=[state, sums, jax.ShapeDtypeStruct((1, edge), F32)],
        in_specs=[VM] * (3 + tensor),
        out_specs=[VM] * 3,
        compiler_params=params(),
        cost_estimate=cost(0, 3 * big),
        name="last",
    )(keep(vec), keep(image), keep(dh), *parts)
    parts = gather_parts(part)
    turned = pl.pallas_call(
        turn_kernel,
        out_shape=state,
        in_specs=[VM],
        out_specs=VM,
        compiler_params=params(),
        cost_estimate=cost(0, 2 * big),
        name="turn",
    )(keep(vec))
    psi = pl.pallas_call(
        functools.partial(psi_kernel, count, tensor),
        out_shape=jax.ShapeDtypeStruct(state_shape, BF16),
        in_specs=[SM] + [VM] * (1 + tensor),
        out_specs=VM,
        compiler_params=params(),
        cost_estimate=cost(0, big),
        name="psi",
    )(plan, keep(turned), *parts)
    return psi[None], energy[0, :1]


def solution(mesh):
    in_specs = (
        P(("cyl", "chain"), "tensor", None, None, None),
        P(("cyl", "chain"), "tensor", None, None),
        P(("cyl", "chain"), "tensor", None),
        P(("cyl", "tensor")),
        P(("cyl", "tensor"), None),
    )
    out_specs = (P(("cyl", "chain"), "tensor", None, None), P(("cyl", "chain")))
    return jax.shard_map(local, mesh=mesh, in_specs=in_specs, out_specs=out_specs, check_vma=False)
```

```python
import functools

import jax
import jax.numpy as jnp
from jax import lax
from jax.experimental import pallas as pl
from jax.experimental.pallas import tpu as pltpu
from jax.sharding import PartitionSpec as P

ITERS = 4
STEP_SIZE = 0.5
PACK_COST = 10**7
REST_COST = 10**10
OWN_COST = 0
EPS = 1e-6
BF16 = jnp.bfloat16
F32 = jnp.float32
VMEM_LIMIT = 16 * 2**20
VM = pl.BlockSpec(memory_space=pltpu.VMEM)
SM = pl.BlockSpec(memory_space=pltpu.SMEM)


def params():
    return pltpu.CompilerParams(vmem_limit_bytes=VMEM_LIMIT)


def cost(flops, bytes_accessed):
    return pl.CostEstimate(flops=int(flops), bytes_accessed=int(bytes_accessed), transcendentals=0)


def vmem(shape, dtype):
    return pltpu.VMEM(shape, dtype)


def keep(x):
    return pltpu.with_memory_space_constraint(x, pltpu.VMEM)


def keep_scalars(x):
    return pltpu.with_memory_space_constraint(x, pltpu.SMEM)


def stay(x):
    return pltpu.with_memory_space_constraint(x, pltpu.HBM)


def grid_ij(edge):
    i = lax.broadcasted_iota(jnp.int32, (edge, edge), 0)
    j = lax.broadcasted_iota(jnp.int32, (edge, edge), 1)
    return i, j


def diag_row(block, i, j):
    return jnp.sum(jnp.where(i == j, block, 0.0), axis=0, keepdims=True)


SOURCE, SECTOR, PLACE, TARGET, RANK, COUNT, NUMBER = range(7)


def pack(cut, group, table, env, rows_ref, out, before=lambda g, carry: carry, after=None, carry=0):
    low, high = cut
    edge = env.shape[-1]
    i, j = grid_ij(edge)

    def body(g, carry):
        carry = before(g, carry)
        for d in range(group):
            p = g * group + d
            first = env[table[SOURCE, 2 * p]].astype(F32)
            second = env[table[SOURCE, 2 * p + 1]].astype(F32)
            at = pl.multiple_of((p - low) * edge, edge)
            out[pl.ds(at, edge), :] = jnp.where(i <= j, first, second).astype(BF16)
            rows_ref[pl.ds(2 * (p - low), 1), :] = diag_row(first, i, j)
            rows_ref[pl.ds(2 * (p - low) + 1, 1), :] = diag_row(second, i, j)
        if after is not None:
            after(g)
        return carry

    pairs = (table[NUMBER, 0] + 1) // 2
    stop = (jnp.minimum(high, pairs) + group - 1) // group
    carry = lax.fori_loop(low // group, stop, body, carry)
    size = (high - low) * edge
    out[size:, :] = rows_ref[: out.shape[0] - size, :].astype(BF16)
    return carry


def split_rows(value):
    high = value.astype(BF16).astype(F32)
    middle = (value - high).astype(BF16).astype(F32)
    low = value - high - middle
    pad = jnp.zeros((weight_rows(value.shape[0]) - 3 * value.shape[0], value.shape[1]), F32)
    return jnp.concatenate([high, middle, low, pad], axis=0).astype(BF16)


def joined_rows(rows, sectors):
    rows = rows.astype(F32)
    return rows[:sectors] + rows[sectors : 2 * sectors] + rows[2 * sectors : 3 * sectors]


def weight_rows(sectors):
    return -(-3 * sectors // 16) * 16


def pack_kernel(cut, overs, group, mask_hbm, ranks_hbm, weight_hbm, env_hbm, *refs):
    over_hbm, refs = refs[: len(overs)], refs[len(overs) :]
    out_hbm, table, flag, env, out, spare, mask_ref, ranks_ref, weight_ref, rows_ref = refs[:10]
    scalar_sems, sems, out_sems, over_sem = refs[10:]
    sectors, chans = mask_ref.shape
    blocks = sectors * chans
    scalars = [
        pltpu.make_async_copy(mask_hbm, mask_ref, scalar_sems.at[0]),
        pltpu.make_async_copy(ranks_hbm, ranks_ref, scalar_sems.at[1]),
        pltpu.make_async_copy(weight_hbm, weight_ref, scalar_sems.at[2]),
    ]
    for c in scalars:
        c.start()

    def fetch(s):
        part = pl.ds(s * chans, chans)
        return pltpu.make_async_copy(env_hbm.at[part], env.at[part], sems.at[s])

    for s in range(sectors):
        fetch(s).start()
    for c in scalars:
        c.wait()
    n = jnp.int32(0)
    for s in range(sectors):
        table[RANK, s] = ranks_ref[s]
        k = jnp.int32(0)
        for w in range(chans):
            m = mask_ref[s, w]
            table[SOURCE, n] = jnp.int32(s * chans + w)
            table[SECTOR, n] = jnp.int32(s)
            table[PLACE, n] = k
            table[TARGET, n] = s * chans + k
            n = n + m
            k = k + m
        table[COUNT, s] = k
    for d in range(2 * group):
        table[SOURCE, n + d] = jnp.int32(0)
        table[SECTOR, n + d] = jnp.int32(0)
        table[PLACE, n + d] = jnp.int32(chans)
        table[TARGET, n + d] = jnp.int32(blocks)
    table[NUMBER, 0] = n
    flag[0] = n

    def wait(s, carry):
        fetch(s).wait()
        return carry

    def before(g, here):
        final = jnp.maximum(jnp.minimum(2 * (g + 1) * group, n) - 1, 0)
        need = jnp.maximum(here, table[SECTOR, final] + 1)
        lax.fori_loop(here, need, wait, 0)
        return need

    extra = weight_rows(sectors)
    edge = env.shape[-1]
    size = (cut[1] - cut[0]) * edge
    out[out.shape[0] - extra :, :] = split_rows(weight_ref[...])
    bulk = out.at[: out.shape[0] - extra, :]

    def send(g):
        part = pl.ds(pl.multiple_of(g * group * edge, group * edge), group * edge)
        return pltpu.make_async_copy(out.at[part], out_hbm.at[part], out_sems.at[g])

    def after(g):
        send(g).start()

    here = pack(cut, group, table, env, rows_ref, bulk, before, after, jnp.int32(0))
    tail = pltpu.make_async_copy(out.at[size:], out_hbm.at[size:], out_sems.at[cut[1] // group])
    tail.start()
    lax.fori_loop(here, sectors, wait, 0)
    for over, to in zip(overs, over_hbm):

        @pl.when(n > 2 * over[0])
        def _(over=over, to=to):
            part = spare.at[: to.shape[0]]
            pack(over, group, table, env, rows_ref, part)
            copy = pltpu.make_async_copy(part, to, over_sem)
            copy.start()
            copy.wait()

    tail.wait()

    def drain(g, carry):
        send(g).wait()
        return carry

    stop = (jnp.minimum(cut[1], (n + 1) // 2) + group - 1) // group
    lax.fori_loop(0, stop, drain, 0)


def rest_kernel(cuts, group, table, env, *refs):
    chunks, rows_ref = refs[-len(cuts) - 1 : -1], refs[-1]
    for cut, out in zip(cuts, chunks):
        pack(cut, group, table, env, rows_ref, out)


def put(k, block, side, table, outer, buf):
    buf[side, table[TARGET, k]] = (block * outer[table[SECTOR, k]]).astype(BF16)


def put_diag(k, row, side, table, outer_diag, diags):
    s = table[SECTOR, k]
    scaled = row * outer_diag[pl.ds(s, 1), :]
    diags[side, s, pl.ds(table[PLACE, k], 1), :] = scaled.astype(BF16).astype(F32)


def unpack(cut, group, side, chunk, table, outer, outer_diag, buf, diags, rows_ref):
    low, high = cut
    edge = chunk.shape[-1]
    i, j = grid_ij(edge)
    n = table[NUMBER, 0]
    size = (high - low) * edge
    rows_ref[: chunk.shape[0] - size, :] = chunk[size:, :].astype(F32)

    def body(g, carry):
        for d in range(group):
            p = g * group + d
            at = pl.multiple_of((p - low) * edge, edge)
            both = chunk[pl.ds(at, edge), :].astype(F32)
            flip = both.T
            row = rows_ref[pl.ds(2 * (p - low), 1), :]
            other = rows_ref[pl.ds(2 * (p - low) + 1, 1), :]
            put(2 * p, jnp.where(i <= j, both, flip), side, table, outer, buf)
            lower = jnp.where(i > j, both, jnp.where(i == j, other, flip))
            put(2 * p + 1, lower, side, table, outer, buf)
            put_diag(2 * p, row, side, table, outer_diag, diags)
            put_diag(2 * p + 1, other, side, table, outer_diag, diags)
        return carry

    stop = (jnp.minimum(high, (n + 1) // 2) + group - 1) // group
    lax.fori_loop(low // group, stop, body, 0)


def widths(sectors, chans):
    parts = [10 if p < -(-sectors // 8) else 8 if p < sectors // 2 else 6 for p in range(sectors)]
    return [min(chans, -(-chans * part // 20) * 2) for part in parts]


def make_plan(plan, table, caps, chans):
    sectors = len(caps)
    counts = [table[COUNT, s] for s in range(sectors)]
    places = []
    for s in range(sectors):
        place = jnp.int32(0)
        for t in range(sectors):
            if t != s:
                ahead = counts[t] >= counts[s] if t < s else counts[t] > counts[s]
                place = place + ahead.astype(jnp.int32)
        plan[COUNT, place] = jnp.int32(s)
        plan[RANK, place] = table[RANK, s]
        places.append(place)
    fits = jnp.int32(1)
    for k, cap in enumerate(caps):
        fits = fits * (table[COUNT, plan[COUNT, k]] <= cap).astype(jnp.int32)
    n = table[NUMBER, 0]
    plan[NUMBER, 0] = n
    plan[NUMBER, 1] = fits
    start = jnp.int32(0)
    for s in range(sectors):

        def body(c, k, s=s):
            plan[SOURCE, k] = table[SOURCE, k]
            plan[SECTOR, k] = places[s]
            plan[PLACE, k] = c
            plan[TARGET, k] = places[s] * chans + c
            return k + 1

        start = lax.fori_loop(0, counts[s], body, start)

    def rest(k, carry):
        for row in (SOURCE, SECTOR, PLACE, TARGET):
            plan[row, k] = table[row, k]
        return carry

    lax.fori_loop(n, n + table.shape[1] - sectors * chans, rest, 0)


def own_kernel(group, chans, table, env, own_site, other_site, *refs):
    weights, (buf, diags, prefix, vec, plan, mine, rows_ref) = refs[:-7], refs[-7:]
    sectors, edge = mine.shape[0], mine.shape[-1]
    make_plan(plan, table, widths(sectors, chans), chans)
    at = lax.axis_index("chain")
    side = at % 2
    before = jnp.ones((sectors, edge), F32)
    for c in range(len(weights) + 1):
        value = before
        for d, weight in enumerate(weights[1:], 2):
            value = jnp.where(at ^ d == c, weight[...], value)
        before = jnp.where(c < at - side, before * value, before)
    prefix[...] = before
    own_weight = weights[0][...]
    rows_ref[...] = jnp.where(side == 0, before * own_weight, own_weight)
    i, j = grid_ij(edge)
    for s in range(sectors):
        old = plan[COUNT, s]
        row = jnp.broadcast_to(rows_ref[pl.ds(old, 1), :], (edge, edge))
        mine[s] = row.T * row
        first = jnp.where(side == 0, own_site[old], other_site[old])
        second = jnp.where(side == 0, other_site[old], own_site[old])
        start = jnp.dot(first, second, preferred_element_type=F32).T
        vec[s] = jnp.where(j < plan[RANK, s], start, 0.0)
    diags[...] = jnp.zeros_like(diags)

    def wipe(t, carry):
        buf[0, t] = jnp.zeros((edge, edge), BF16)
        buf[1, t] = jnp.zeros((edge, edge), BF16)
        return carry

    lax.fori_loop(0, sectors * chans, wipe, 0)
    step = 2 * group

    def body(g, carry):
        for d in range(step):
            k = step * g + d
            s = plan[SECTOR, k]
            block = (env[plan[SOURCE, k]].astype(F32) * mine[s]).astype(BF16)
            buf[side, plan[TARGET, k]] = block
            diags[side, s, pl.ds(plan[PLACE, k], 1), :] = diag_row(block.astype(F32), i, j)
        return carry

    lax.fori_loop(0, (plan[NUMBER, 0] + step - 1) // step, body, 0)


def outer_kernel(cut, group, plan, prefix, chunk, *refs):
    _, _, buf, diags, outer, outer_diag, rows_ref, weight_ref = refs
    sectors, edge = outer.shape[0], outer.shape[-1]
    side = lax.axis_index("chain") % 2
    extra = weight_rows(sectors)
    start = chunk.shape[0] - extra
    other_weight = joined_rows(chunk[start:, :], sectors)
    weight_ref[...] = jnp.where(side == 0, other_weight, prefix[...] * other_weight)
    for s in range(sectors):
        row = weight_ref[pl.ds(plan[COUNT, s], 1), :]
        outer_diag[s : s + 1, :] = row * row
        row = jnp.broadcast_to(row, (edge, edge))
        outer[s] = row.T * row
    bulk = chunk.at[:start, :]
    unpack(cut, group, 1 - side, bulk, plan, outer, outer_diag, buf, diags, rows_ref)


def mid_kernel(cut, group, table, outer, outer_diag, chunk, *refs):
    _, _, buf, diags, rows_ref = refs
    side = lax.axis_index("chain") % 2
    unpack(cut, group, 1 - side, chunk, table, outer, outer_diag, buf, diags, rows_ref)


def apply_all(vectors, plan, *state):
    vec, inner = state[1], state[-1]
    sectors, chans = vec.shape[0], inner.shape[-1] // vec.shape[-1]
    fits = plan[NUMBER, 1]

    @pl.when(fits == 1)
    def _():
        apply_some(vectors, plan, widths(sectors, chans), *state)

    @pl.when(fits == 0)
    def _():
        apply_some(vectors, plan, [chans] * sectors, *state)


def apply_some(vectors, plan, caps, buf, vec, image, part, inner):
    sectors, edge = vec.shape[0], vec.shape[-1]
    chans = inner.shape[-1] // edge
    for s, cap in enumerate(caps):
        vector = vectors(s)
        vec[s] = vector
        right = buf[1, s * chans : s * chans + cap].reshape(cap * edge, edge)
        image_t = jnp.dot(right, vector.astype(BF16), preferred_element_type=F32).astype(BF16)
        for c in range(cap):
            inner[s, :, c * edge : (c + 1) * edge] = image_t[c * edge : (c + 1) * edge]
    _, j = grid_ij(edge)
    along = jnp.zeros((edge, edge), F32)
    square = jnp.zeros((edge, edge), F32)
    for s, cap in enumerate(caps):
        left = buf[0, s * chans : s * chans + cap].reshape(cap * edge, edge)
        hv = jnp.dot(inner[s, :, : cap * edge], left, preferred_element_type=F32)
        hv = jnp.where(j < plan[RANK, s], hv, 0.0)
        image[s] = hv
        vector = vec[s]
        along = along + vector * hv
        square = square + vector * vector
    store_sums(part, along, square)


def store_sums(part, along, square):
    part[0:1, :] = jnp.sum(along, axis=0, keepdims=True)
    part[1:2, :] = jnp.sum(square, axis=0, keepdims=True)


def first_kernel(cuts, group, plan, outer, outer_diag, vec_in, chunk, *refs):
    overs, refs = refs[: len(cuts) - 1], refs[len(cuts) - 1 :]
    _, _, buf, diags, vec, image, dh, part, inner, rows_ref, spare, sem = refs
    sectors = vec.shape[0]
    side = lax.axis_index("chain") % 2
    unpack(cuts[0], group, 1 - side, chunk, plan, outer, outer_diag, buf, diags, rows_ref)
    for cut, over in zip(cuts[1:], overs):

        @pl.when(plan[NUMBER, 0] > 2 * cut[0])
        def _(cut=cut, over=over):
            here = spare.at[: over.shape[0]]
            copy = pltpu.make_async_copy(over, here, sem)
            copy.start()
            copy.wait()
            unpack(cut, group, 1 - side, here, plan, outer, outer_diag, buf, diags, rows_ref)

    chans = inner.shape[-1] // vec.shape[-1]
    used = lax.broadcasted_iota(jnp.int32, diags.shape[2:], 0) < chans
    for s in range(sectors):
        dh[s] = lax.dot_general(
            jnp.where(used, diags[1, s], 0.0).astype(BF16),
            jnp.where(used, diags[0, s], 0.0).astype(BF16),
            (((0,), (0,)), ((), ())),
            preferred_element_type=F32,
        )
    apply_all(lambda s: vec_in[s], plan, buf, vec, image, part, inner)


def joined(parts):
    values = [p[...] for p in parts]
    while len(values) > 1:
        values = [values[k] + values[k + 1] for k in range(0, len(values), 2)]
    total = values[0]
    along = jnp.sum(total[0:1, :], axis=1, keepdims=True)
    square = jnp.sum(total[1:2, :], axis=1, keepdims=True)
    return along, square


def step_of(count, along, square):
    theta = along / (square + EPS)
    scale = 1.0 / jnp.sqrt(square / count + EPS)

    def step(vector, hv, dh):
        resid = hv - theta * vector
        return (vector - STEP_SIZE * resid / (1.0 + jnp.abs(dh - theta))) * scale

    return theta, step


def iter_kernel(count, partners, plan, buf, vec_in, image_in, dh, *refs):
    parts = refs[:partners]
    vec, image, part, inner = refs[partners:]
    _, step = step_of(count, *joined(parts))
    apply_all(
        lambda s: step(vec_in[s], image_in[s], dh[s]), plan, buf, vec, image, part, inner
    )


def last_kernel(count, partners, vec_in, image_in, dh, *refs):
    parts = refs[:partners]
    vec, part, energy = refs[partners:]
    theta, step = step_of(count, *joined(parts))
    square = jnp.zeros(dh.shape[1:], F32)
    for s in range(dh.shape[0]):
        vector = step(vec_in[s], image_in[s], dh[s])
        vec[s] = vector
        square = square + vector * vector
    store_sums(part, square, square)
    energy[...] = jnp.broadcast_to(theta, energy.shape)


def turn_kernel(vec, turned):
    for s in range(vec.shape[0]):
        turned[s] = vec[s].T


def psi_kernel(count, partners, plan, vec, *refs):
    parts = refs[:partners]
    psi = refs[partners]
    square, _ = joined(parts)
    scale = 1.0 / jnp.sqrt(square / count + EPS)
    for s in range(psi.shape[0]):
        psi[plan[COUNT, s]] = (vec[s] * scale).astype(BF16)


def swap(value):
    return swapped(value, "chain", 1)


def swapped(value, axis, mask):
    size = lax.axis_size(axis)
    return lax.ppermute(value, axis, [(k, k ^ mask) for k in range(size)])


def from_all(value, axis):
    return [value] + [swapped(value, axis, m) for m in range(1, lax.axis_size(axis))]


def gather_parts(part):
    return [keep(p) for p in from_all(part, "tensor")]


def local(env, site, seg_weight, ranks, mpo_mask):
    sectors, chans, edge = env.shape[1:4]
    blocks = sectors * chans
    tensor = lax.axis_size("tensor")
    count = float(sectors * tensor * edge * edge)
    group = 4
    pairs = -(-blocks // (2 * group)) * group
    base = min(pairs, -(-pairs * 3 // 5 // (2 * group)) * 2 * group)
    third = max(base // 6 // group, 1) * group
    marks = [0, base // 2, base - third, base, min(base + third, pairs), pairs]
    cuts = [(a, b) for a, b in zip(marks[:-1], marks[1:]) if a < b]
    usual = 3
    tails = [-(-2 * (c[1] - c[0]) // 16) * 16 for c in cuts]
    rows = [(c[1] - c[0]) * edge + t for c, t in zip(cuts, tails)]
    rows[0] += weight_rows(sectors)
    block_bytes = 2 * edge * edge
    big = sectors * edge * edge * 4

    own_weight = seg_weight[0]
    weights = [swapped(own_weight, "chain", m) for m in range(2, lax.axis_size("chain"))]
    other_site = swap(site[0])
    flat_env = env.reshape(blocks, edge, edge)
    state_shape = (sectors, edge, edge)
    state = vmem(state_shape, F32)
    row_shape = vmem((sectors, edge), F32)
    table_shape = pltpu.SMEM((7, blocks + 2 * group), jnp.int32)

    hbm = pl.BlockSpec(memory_space=pltpu.HBM)
    dma = pltpu.SemaphoreType.DMA
    tail_rows = pltpu.VMEM((max(tails), edge), F32)
    *overs, first_sent, table, active, env_here = pl.pallas_call(
        functools.partial(pack_kernel, cuts[0], cuts[usual:], group),
        out_shape=[jax.ShapeDtypeStruct((r, edge), BF16) for r in rows[usual:]]
        + [
            jax.ShapeDtypeStruct((rows[0], edge), BF16),
            table_shape,
            pltpu.SMEM((1,), jnp.int32),
            vmem((blocks, edge, edge), BF16),
        ],
        in_specs=[hbm] * 4,
        out_specs=[hbm] * len(cuts[usual:]) + [hbm, SM, SM, VM],
        scratch_shapes=[
            pltpu.VMEM((rows[0], edge), BF16),
            pltpu.VMEM((max(rows[usual:]), edge), BF16),
            pltpu.SMEM(mpo_mask.shape, jnp.int32),
            pltpu.SMEM(ranks.shape, jnp.int32),
            pltpu.VMEM((sectors, edge), F32),
            tail_rows,
            dma((3,)),
            dma((sectors,)),
            dma((cuts[0][1] // group + 1,)),
            dma(()),
        ],
        compiler_params=params(),
        cost_estimate=cost(PACK_COST, 2 * blocks * block_bytes),
        name="pack",
    )(stay(mpo_mask), stay(ranks), stay(own_weight), stay(flat_env))
    table, env_here = keep_scalars(table), keep(env_here)

    def send(k):
        if k == len(overs):
            return []
        moved = functools.partial(lambda x: [swap(x)], overs[k])
        return lax.cond(
            active[0] > 2 * cuts[usual + k][0],
            lambda: moved() + send(k + 1),
            lambda: list(overs[k:]),
        )

    extra = [stay(x) for x in send(0)]
    sent = pl.pallas_call(
        functools.partial(rest_kernel, cuts[1:usual], group),
        out_shape=[vmem((r, edge), BF16) for r in rows[1:usual]],
        in_specs=[SM, VM] + [hbm] * (1 + len(extra) + len(weights)),
        out_specs=[VM] * (usual - 1),
        scratch_shapes=[tail_rows],
        compiler_params=params(),
        cost_estimate=cost(REST_COST, 2 * blocks * block_bytes),
        name="rest",
    )(table, env_here, *extra, stay(other_site), *[stay(w) for w in weights])
    got = [keep(swap(c)) for c in (first_sent, *sent)]

    buf_shape = vmem((2, blocks + 1, edge, edge), BF16)
    diag_shape = vmem((2, sectors, -(-(chans + 1) // 16) * 16, edge), F32)
    sums = vmem((2, edge), F32)
    inner_shape = pltpu.VMEM((sectors, edge, chans * edge), BF16)
    work = 4.0 * blocks * edge**3

    buf, diags, prefix, vec, plan = pl.pallas_call(
        functools.partial(own_kernel, group, chans),
        out_shape=[buf_shape, diag_shape, row_shape, state, table_shape],
        in_specs=[SM] + [VM] * (4 + len(weights)),
        out_specs=[VM] * 4 + [SM],
        scratch_shapes=[pltpu.VMEM(state_shape, F32), pltpu.VMEM((sectors, edge), F32)],
        compiler_params=params(),
        cost_estimate=cost(OWN_COST, 0),
        name="own",
    )(table, env_here, site[0], stay(other_site), own_weight, *[stay(w) for w in weights])
    plan = keep_scalars(plan)

    buf, diags, outer, outer_diag = pl.pallas_call(
        functools.partial(outer_kernel, cuts[0], group),
        out_shape=[buf_shape, diag_shape, state, row_shape],
        in_specs=[SM] + [VM] * 4,
        out_specs=[VM] * 4,
        scratch_shapes=[tail_rows, pltpu.VMEM((sectors, edge), F32)],
        input_output_aliases={3: 0, 4: 1},
        compiler_params=params(),
        cost_estimate=cost(0, 0),
        name="outer",
    )(plan, keep(prefix), got[0], keep(buf), keep(diags))

    for cut, chunk in zip(cuts[1 : usual - 1], got[1:]):
        buf, diags = pl.pallas_call(
            functools.partial(mid_kernel, cut, group),
            out_shape=[buf_shape, diag_shape],
            in_specs=[SM] + [VM] * 5,
            out_specs=[VM] * 2,
            scratch_shapes=[tail_rows],
            input_output_aliases={4: 0, 5: 1},
            compiler_params=params(),
            cost_estimate=cost(0, 0),
            name="mid",
        )(plan, keep(outer), keep(outer_diag), chunk, keep(buf), keep(diags))

    buf, diags, vec, image, dh, part = pl.pallas_call(
        functools.partial(first_kernel, cuts[usual - 1 :], group),
        out_shape=[buf_shape, diag_shape, state, state, state, sums],
        in_specs=[SM] + [VM] * 4 + [hbm] * len(extra) + [VM] * 2,
        out_specs=[VM] * 6,
        scratch_shapes=[inner_shape, tail_rows, pltpu.VMEM((max(rows[usual:]), edge), BF16), dma(())],
        input_output_aliases={5 + len(extra): 0, 6 + len(extra): 1},
        compiler_params=params(),
        cost_estimate=cost(work, 2 * blocks * block_bytes),
        name="first",
    )(
        plan, keep(outer), keep(outer_diag), keep(vec), got[usual - 1], *extra,
        keep(buf), keep(diags),
    )

    for _ in range(ITERS - 1):
        parts = gather_parts(part)
        vec, image, part = pl.pallas_call(
            functools.partial(iter_kernel, count, tensor),
            out_shape=[state, state, sums],
            in_specs=[SM] + [VM] * (4 + tensor),
            out_specs=[VM] * 3,
            scratch_shapes=[inner_shape],
            compiler_params=params(),
            cost_estimate=cost(work, 2 * blocks * block_bytes),
            name="iterate",
        )(plan, keep(buf), keep(vec), keep(image), keep(dh), *parts)

    parts = gather_parts(part)
    vec, part, energy = pl.pallas_call(
        functools.partial(last_kernel, count, tensor),
        out_shape=[state, sums, jax.ShapeDtypeStruct((1, edge), F32)],
        in_specs=[VM] * (3 + tensor),
        out_specs=[VM] * 3,
        compiler_params=params(),
        cost_estimate=cost(0, 3 * big),
        name="last",
    )(keep(vec), keep(image), keep(dh), *parts)
    parts = gather_parts(part)
    turned = pl.pallas_call(
        turn_kernel,
        out_shape=state,
        in_specs=[VM],
        out_specs=VM,
        compiler_params=params(),
        cost_estimate=cost(0, 2 * big),
        name="turn",
    )(keep(vec))
    psi = pl.pallas_call(
        functools.partial(psi_kernel, count, tensor),
        out_shape=jax.ShapeDtypeStruct(state_shape, BF16),
        in_specs=[SM] + [VM] * (1 + tensor),
        out_specs=VM,
        compiler_params=params(),
        cost_estimate=cost(0, big),
        name="psi",
    )(plan, keep(turned), *parts)
    return psi[None], energy[0, :1]


def solution(mesh):
    in_specs = (
        P(("cyl", "chain"), "tensor", None, None, None),
        P(("cyl", "chain"), "tensor", None, None),
        P(("cyl", "chain"), "tensor", None),
        P(("cyl", "tensor")),
        P(("cyl", "tensor"), None),
    )
    out_specs = (P(("cyl", "chain"), "tensor", None, None), P(("cyl", "chain")))
    return jax.shard_map(local, mesh=mesh, in_specs=in_specs, out_specs=out_specs, check_vma=False)
```

```python
import functools

import jax
import jax.numpy as jnp
from jax import lax
from jax.experimental import pallas as pl
from jax.experimental.pallas import tpu as pltpu
from jax.sharding import PartitionSpec as P

ITERS = 4
STEP_SIZE = 0.5
PACK_COST = 10**7
REST_COST = 10**10
OWN_COST = 0
EPS = 1e-6
BF16 = jnp.bfloat16
F32 = jnp.float32
VMEM_LIMIT = 16 * 2**20
VM = pl.BlockSpec(memory_space=pltpu.VMEM)
SM = pl.BlockSpec(memory_space=pltpu.SMEM)


def params():
    return pltpu.CompilerParams(vmem_limit_bytes=VMEM_LIMIT)


def cost(flops, bytes_accessed):
    return pl.CostEstimate(flops=int(flops), bytes_accessed=int(bytes_accessed), transcendentals=0)


def vmem(shape, dtype):
    return pltpu.VMEM(shape, dtype)


def keep(x):
    return pltpu.with_memory_space_constraint(x, pltpu.VMEM)


def keep_scalars(x):
    return pltpu.with_memory_space_constraint(x, pltpu.SMEM)


def stay(x):
    return pltpu.with_memory_space_constraint(x, pltpu.HBM)


def grid_ij(edge):
    i = lax.broadcasted_iota(jnp.int32, (edge, edge), 0)
    j = lax.broadcasted_iota(jnp.int32, (edge, edge), 1)
    return i, j


def diag_row(block, i, j):
    return jnp.sum(jnp.where(i == j, block, 0.0), axis=0, keepdims=True)


SOURCE, SECTOR, PLACE, TARGET, RANK, COUNT, NUMBER, END = range(8)


def pack(cut, group, table, env, rows_ref, out, before=lambda g, carry: carry, after=None, carry=0):
    low, high = cut
    edge = env.shape[-1]
    i, j = grid_ij(edge)

    def body(g, carry):
        carry = before(g, carry)
        for d in range(group):
            p = g * group + d
            first = env[table[SOURCE, 2 * p]].astype(F32)
            second = env[table[SOURCE, 2 * p + 1]].astype(F32)
            at = pl.multiple_of((p - low) * edge, edge)
            out[pl.ds(at, edge), :] = jnp.where(i <= j, first, second).astype(BF16)
            rows_ref[pl.ds(2 * (p - low), 1), :] = diag_row(first, i, j)
            rows_ref[pl.ds(2 * (p - low) + 1, 1), :] = diag_row(second, i, j)
        if after is not None:
            after(g)
        return carry

    pairs = (table[NUMBER, 0] + 1) // 2
    stop = (jnp.minimum(high, pairs) + group - 1) // group
    carry = lax.fori_loop(low // group, stop, body, carry)
    size = (high - low) * edge
    out[size:, :] = rows_ref[: out.shape[0] - size, :].astype(BF16)
    return carry


def split_rows(value):
    high = value.astype(BF16).astype(F32)
    middle = (value - high).astype(BF16).astype(F32)
    low = value - high - middle
    pad = jnp.zeros((weight_rows(value.shape[0]) - 3 * value.shape[0], value.shape[1]), F32)
    return jnp.concatenate([high, middle, low, pad], axis=0).astype(BF16)


def joined_rows(rows, sectors):
    rows = rows.astype(F32)
    return rows[:sectors] + rows[sectors : 2 * sectors] + rows[2 * sectors : 3 * sectors]


def weight_rows(sectors):
    return -(-3 * sectors // 16) * 16


def pack_kernel(cut, overs, group, mask_hbm, ranks_hbm, weight_hbm, env_hbm, *refs):
    over_hbm, refs = refs[: len(overs)], refs[len(overs) :]
    out_hbm, table, flag, env, out, spare, mask_ref, ranks_ref, weight_ref, rows_ref = refs[:10]
    scalar_sems, sems, out_sems, over_sem = refs[10:]
    sectors, chans = mask_ref.shape
    blocks = sectors * chans
    scalars = [
        pltpu.make_async_copy(mask_hbm, mask_ref, scalar_sems.at[0]),
        pltpu.make_async_copy(ranks_hbm, ranks_ref, scalar_sems.at[1]),
        pltpu.make_async_copy(weight_hbm, weight_ref, scalar_sems.at[2]),
    ]
    for c in scalars:
        c.start()

    def fetch(s):
        part = pl.ds(s * chans, chans)
        return pltpu.make_async_copy(env_hbm.at[part], env.at[part], sems.at[s])

    for s in range(sectors):
        fetch(s).start()
    for c in scalars:
        c.wait()
    n = jnp.int32(0)
    for s in range(sectors):
        table[RANK, s] = ranks_ref[s]
        k = jnp.int32(0)
        for w in range(chans):
            m = mask_ref[s, w]
            table[SOURCE, n] = jnp.int32(s * chans + w)
            table[SECTOR, n] = jnp.int32(s)
            table[PLACE, n] = k
            table[TARGET, n] = s * chans + k
            n = n + m
            k = k + m
        table[COUNT, s] = k
    for d in range(2 * group):
        table[SOURCE, n + d] = jnp.int32(0)
        table[SECTOR, n + d] = jnp.int32(0)
        table[PLACE, n + d] = jnp.int32(chans)
        table[TARGET, n + d] = jnp.int32(blocks)
    table[NUMBER, 0] = n
    flag[0] = n

    def wait(s, carry):
        fetch(s).wait()
        return carry

    def before(g, here):
        final = jnp.maximum(jnp.minimum(2 * (g + 1) * group, n) - 1, 0)
        need = jnp.maximum(here, table[SECTOR, final] + 1)
        lax.fori_loop(here, need, wait, 0)
        return need

    extra = weight_rows(sectors)
    edge = env.shape[-1]
    size = (cut[1] - cut[0]) * edge
    out[out.shape[0] - extra :, :] = split_rows(weight_ref[...])
    bulk = out.at[: out.shape[0] - extra, :]

    def send(g):
        part = pl.ds(pl.multiple_of(g * group * edge, group * edge), group * edge)
        return pltpu.make_async_copy(out.at[part], out_hbm.at[part], out_sems.at[g])

    def after(g):
        send(g).start()

    here = pack(cut, group, table, env, rows_ref, bulk, before, after, jnp.int32(0))
    tail = pltpu.make_async_copy(out.at[size:], out_hbm.at[size:], out_sems.at[cut[1] // group])
    tail.start()
    lax.fori_loop(here, sectors, wait, 0)
    for over, to in zip(overs, over_hbm):

        @pl.when(n > 2 * over[0])
        def _(over=over, to=to):
            part = spare.at[: to.shape[0]]
            pack(over, group, table, env, rows_ref, part)
            copy = pltpu.make_async_copy(part, to, over_sem)
            copy.start()
            copy.wait()

    tail.wait()

    def drain(g, carry):
        send(g).wait()
        return carry

    stop = (jnp.minimum(cut[1], (n + 1) // 2) + group - 1) // group
    lax.fori_loop(0, stop, drain, 0)


def rest_kernel(cuts, group, table, env, *refs):
    chunks, rows_ref = refs[-len(cuts) - 1 : -1], refs[-1]
    for cut, out in zip(cuts, chunks):
        pack(cut, group, table, env, rows_ref, out)


def put(k, block, side, table, outer, buf):
    buf[side, table[TARGET, k]] = (block * outer[table[SECTOR, k]]).astype(BF16)


def put_diag(k, row, side, table, outer_diag, diags):
    s = table[SECTOR, k]
    scaled = row * outer_diag[pl.ds(s, 1), :]
    diags[side, s, pl.ds(table[PLACE, k], 1), :] = scaled.astype(BF16).astype(F32)


def unpack(cut, group, side, chunk, table, outer, outer_diag, buf, diags, rows_ref):
    low, high = cut
    edge = chunk.shape[-1]
    i, j = grid_ij(edge)
    n = table[NUMBER, 0]
    size = (high - low) * edge
    rows_ref[: chunk.shape[0] - size, :] = chunk[size:, :].astype(F32)

    def body(g, carry):
        for d in range(group):
            p = g * group + d
            at = pl.multiple_of((p - low) * edge, edge)
            both = chunk[pl.ds(at, edge), :].astype(F32)
            flip = both.T
            row = rows_ref[pl.ds(2 * (p - low), 1), :]
            other = rows_ref[pl.ds(2 * (p - low) + 1, 1), :]
            put(2 * p, jnp.where(i <= j, both, flip), side, table, outer, buf)
            lower = jnp.where(i > j, both, jnp.where(i == j, other, flip))
            put(2 * p + 1, lower, side, table, outer, buf)
            put_diag(2 * p, row, side, table, outer_diag, diags)
            put_diag(2 * p + 1, other, side, table, outer_diag, diags)
        return carry

    stop = (jnp.minimum(high, (n + 1) // 2) + group - 1) // group
    lax.fori_loop(low // group, stop, body, 0)


def widths(sectors, chans):
    parts = [10 if p < -(-sectors // 8) else 8 if p < sectors // 2 else 6 for p in range(sectors)]
    return [min(chans, -(-chans * part // 20) * 2) for part in parts]


def make_plan(plan, table, caps, chans):
    sectors = len(caps)
    counts = [table[COUNT, s] for s in range(sectors)]
    places = []
    for s in range(sectors):
        place = jnp.int32(0)
        for t in range(sectors):
            if t != s:
                ahead = counts[t] >= counts[s] if t < s else counts[t] > counts[s]
                place = place + ahead.astype(jnp.int32)
        plan[COUNT, place] = jnp.int32(s)
        plan[RANK, place] = table[RANK, s]
        places.append(place)
    fits = jnp.int32(1)
    for k, cap in enumerate(caps):
        fits = fits * (table[COUNT, plan[COUNT, k]] <= cap).astype(jnp.int32)
    n = table[NUMBER, 0]
    plan[NUMBER, 0] = n
    plan[NUMBER, 1] = fits
    start = jnp.int32(0)
    for s in range(sectors):

        def body(c, k, s=s):
            plan[SOURCE, k] = table[SOURCE, k]
            plan[SECTOR, k] = places[s]
            plan[PLACE, k] = c
            plan[TARGET, k] = places[s] * chans + c
            return k + 1

        start = lax.fori_loop(0, counts[s], body, start)
        plan[END, places[s]] = start

    def rest(k, carry):
        for row in (SOURCE, SECTOR, PLACE, TARGET):
            plan[row, k] = table[row, k]
        return carry

    lax.fori_loop(n, n + table.shape[1] - sectors * chans, rest, 0)


def own_kernel(group, chans, table, env, own_site, other_site, *refs):
    weights, (buf, diags, prefix, vec, plan, mine, rows_ref) = refs[:-7], refs[-7:]
    sectors, edge = mine.shape[0], mine.shape[-1]
    make_plan(plan, table, widths(sectors, chans), chans)
    at = lax.axis_index("chain")
    side = at % 2
    before = jnp.ones((sectors, edge), F32)
    for c in range(len(weights) + 1):
        value = before
        for d, weight in enumerate(weights[1:], 2):
            value = jnp.where(at ^ d == c, weight[...], value)
        before = jnp.where(c < at - side, before * value, before)
    prefix[...] = before
    own_weight = weights[0][...]
    rows_ref[...] = jnp.where(side == 0, before * own_weight, own_weight)
    i, j = grid_ij(edge)
    for s in range(sectors):
        old = plan[COUNT, s]
        row = jnp.broadcast_to(rows_ref[pl.ds(old, 1), :], (edge, edge))
        mine[s] = row.T * row
        first = jnp.where(side == 0, own_site[old], other_site[old])
        second = jnp.where(side == 0, other_site[old], own_site[old])
        start = jnp.dot(first, second, preferred_element_type=F32).T
        vec[s] = jnp.where(j < plan[RANK, s], start, 0.0)
    diags[...] = jnp.zeros_like(diags)

    def wipe(t, carry):
        buf[0, t] = jnp.zeros((edge, edge), BF16)
        buf[1, t] = jnp.zeros((edge, edge), BF16)
        return carry

    lax.fori_loop(0, sectors * chans, wipe, 0)
    step = 2 * group

    def body(g, carry):
        for d in range(step):
            k = step * g + d
            s = plan[SECTOR, k]
            block = (env[plan[SOURCE, k]].astype(F32) * mine[s]).astype(BF16)
            buf[side, plan[TARGET, k]] = block
            diags[side, s, pl.ds(plan[PLACE, k], 1), :] = diag_row(block.astype(F32), i, j)
        return carry

    lax.fori_loop(0, (plan[NUMBER, 0] + step - 1) // step, body, 0)


def outer_kernel(cut, group, plan, prefix, chunk, *refs):
    _, _, buf, diags, outer, outer_diag, rows_ref, weight_ref = refs
    sectors, edge = outer.shape[0], outer.shape[-1]
    side = lax.axis_index("chain") % 2
    extra = weight_rows(sectors)
    start = chunk.shape[0] - extra
    other_weight = joined_rows(chunk[start:, :], sectors)
    weight_ref[...] = jnp.where(side == 0, other_weight, prefix[...] * other_weight)
    for s in range(sectors):
        row = weight_ref[pl.ds(plan[COUNT, s], 1), :]
        outer_diag[s : s + 1, :] = row * row
        row = jnp.broadcast_to(row, (edge, edge))
        outer[s] = row.T * row
    bulk = chunk.at[:start, :]
    unpack(cut, group, 1 - side, bulk, plan, outer, outer_diag, buf, diags, rows_ref)


def mid_kernel(cut, group, plan, outer, outer_diag, vec, chunk, *refs):
    _, _, buf, diags, image, inner, rows_ref = refs
    side = lax.axis_index("chain") % 2
    unpack(cut, group, 1 - side, chunk, plan, outer, outer_diag, buf, diags, rows_ref)
    sectors, chans = vec.shape[0], inner.shape[-1] // vec.shape[-1]
    for few, caps in ((1, widths(sectors, chans)), (0, [chans] * sectors)):

        @pl.when(plan[NUMBER, 1] == few)
        def _(caps=caps):
            all_images(caps, plan, buf, vec, image, inner)


def all_images(caps, plan, buf, vec, image, inner):
    edge = vec.shape[-1]
    chans = inner.shape[-1] // edge
    _, j = grid_ij(edge)
    for s, cap in enumerate(caps):
        right = buf[1, s * chans : s * chans + cap].reshape(cap * edge, edge)
        image_t = jnp.dot(right, vec[s].astype(BF16), preferred_element_type=F32).astype(BF16)
        for c in range(cap):
            inner[s, :, c * edge : (c + 1) * edge] = image_t[c * edge : (c + 1) * edge]
    for s, cap in enumerate(caps):
        left = buf[0, s * chans : s * chans + cap].reshape(cap * edge, edge)
        hv = jnp.dot(inner[s, :, : cap * edge], left, preferred_element_type=F32)
        image[s] = jnp.where(j < plan[RANK, s], hv, 0.0)


def late_images(low, plan, buf, vec, image, inner):
    sectors, edge = vec.shape[0], vec.shape[-1]
    chans = inner.shape[-1] // edge
    _, j = grid_ij(edge)
    fits = plan[NUMBER, 1]
    for s, cap in enumerate(widths(sectors, chans)):
        take = plan[END, s] > low
        for few, width in ((1, cap), (0, chans)):

            @pl.when(jnp.logical_and(take, fits == few))
            def _(s=s, width=width):
                one_image(s, width, plan, buf, vec[s], image, inner, j)


def one_image(s, width, plan, buf, vector, image, inner, j):
    edge = vector.shape[-1]
    chans = inner.shape[-1] // edge
    right = buf[1, s * chans : s * chans + width].reshape(width * edge, edge)
    image_t = jnp.dot(right, vector.astype(BF16), preferred_element_type=F32).astype(BF16)
    for c in range(width):
        inner[s, :, c * edge : (c + 1) * edge] = image_t[c * edge : (c + 1) * edge]
    left = buf[0, s * chans : s * chans + width].reshape(width * edge, edge)
    hv = jnp.dot(inner[s, :, : width * edge], left, preferred_element_type=F32)
    image[s] = jnp.where(j < plan[RANK, s], hv, 0.0)


def apply_all(vectors, plan, *state):
    vec, inner = state[1], state[-1]
    sectors, chans = vec.shape[0], inner.shape[-1] // vec.shape[-1]
    fits = plan[NUMBER, 1]

    @pl.when(fits == 1)
    def _():
        apply_some(vectors, plan, widths(sectors, chans), *state)

    @pl.when(fits == 0)
    def _():
        apply_some(vectors, plan, [chans] * sectors, *state)


def apply_some(vectors, plan, caps, buf, vec, image, part, inner):
    sectors, edge = vec.shape[0], vec.shape[-1]
    chans = inner.shape[-1] // edge
    for s, cap in enumerate(caps):
        vector = vectors(s)
        vec[s] = vector
        right = buf[1, s * chans : s * chans + cap].reshape(cap * edge, edge)
        image_t = jnp.dot(right, vector.astype(BF16), preferred_element_type=F32).astype(BF16)
        for c in range(cap):
            inner[s, :, c * edge : (c + 1) * edge] = image_t[c * edge : (c + 1) * edge]
    _, j = grid_ij(edge)
    along = jnp.zeros((edge, edge), F32)
    square = jnp.zeros((edge, edge), F32)
    for s, cap in enumerate(caps):
        left = buf[0, s * chans : s * chans + cap].reshape(cap * edge, edge)
        hv = jnp.dot(inner[s, :, : cap * edge], left, preferred_element_type=F32)
        hv = jnp.where(j < plan[RANK, s], hv, 0.0)
        image[s] = hv
        vector = vec[s]
        along = along + vector * hv
        square = square + vector * vector
    store_sums(part, along, square)


def store_sums(part, along, square):
    part[0:1, :] = jnp.sum(along, axis=0, keepdims=True)
    part[1:2, :] = jnp.sum(square, axis=0, keepdims=True)


def first_kernel(cuts, group, plan, outer, outer_diag, vec, chunk, *refs):
    overs, refs = refs[: len(cuts) - 1], refs[len(cuts) - 1 :]
    _, _, _, buf, diags, image, part, inner, rows_ref, spare, sem = refs
    sectors = vec.shape[0]
    side = lax.axis_index("chain") % 2
    unpack(cuts[0], group, 1 - side, chunk, plan, outer, outer_diag, buf, diags, rows_ref)
    for cut, over in zip(cuts[1:], overs):

        @pl.when(plan[NUMBER, 0] > 2 * cut[0])
        def _(cut=cut, over=over):
            here = spare.at[: over.shape[0]]
            copy = pltpu.make_async_copy(over, here, sem)
            copy.start()
            copy.wait()
            unpack(cut, group, 1 - side, here, plan, outer, outer_diag, buf, diags, rows_ref)

    late_images(2 * cuts[0][0], plan, buf, vec, image, inner)
    along = jnp.zeros(vec.shape[1:], F32)
    square = along
    for s in range(sectors):
        along = along + vec[s] * image[s]
        square = square + vec[s] * vec[s]
    store_sums(part, along, square)


def diag_kernel(chans, diags, dh):
    used = lax.broadcasted_iota(jnp.int32, diags.shape[2:], 0) < chans
    for s in range(dh.shape[0]):
        dh[s] = lax.dot_general(
            jnp.where(used, diags[1, s], 0.0).astype(BF16),
            jnp.where(used, diags[0, s], 0.0).astype(BF16),
            (((0,), (0,)), ((), ())),
            preferred_element_type=F32,
        )


def joined(parts):
    values = [p[...] for p in parts]
    while len(values) > 1:
        values = [values[k] + values[k + 1] for k in range(0, len(values), 2)]
    total = values[0]
    along = jnp.sum(total[0:1, :], axis=1, keepdims=True)
    square = jnp.sum(total[1:2, :], axis=1, keepdims=True)
    return along, square


def step_of(count, along, square):
    theta = along / (square + EPS)
    scale = 1.0 / jnp.sqrt(square / count + EPS)

    def step(vector, hv, dh):
        resid = hv - theta * vector
        return (vector - STEP_SIZE * resid / (1.0 + jnp.abs(dh - theta))) * scale

    return theta, step


def iter_kernel(count, partners, plan, buf, vec_in, image_in, dh, *refs):
    parts = refs[:partners]
    vec, image, part, inner = refs[partners:]
    _, step = step_of(count, *joined(parts))
    apply_all(
        lambda s: step(vec_in[s], image_in[s], dh[s]), plan, buf, vec, image, part, inner
    )


def last_kernel(count, partners, vec_in, image_in, dh, *refs):
    parts = refs[:partners]
    vec, part, energy = refs[partners:]
    theta, step = step_of(count, *joined(parts))
    square = jnp.zeros(dh.shape[1:], F32)
    for s in range(dh.shape[0]):
        vector = step(vec_in[s], image_in[s], dh[s])
        vec[s] = vector
        square = square + vector * vector
    store_sums(part, square, square)
    energy[...] = jnp.broadcast_to(theta, energy.shape)


def turn_kernel(vec, turned):
    for s in range(vec.shape[0]):
        turned[s] = vec[s].T


def psi_kernel(count, partners, plan, vec, *refs):
    parts = refs[:partners]
    psi, ready, sems = refs[partners:]
    square, _ = joined(parts)
    scale = 1.0 / jnp.sqrt(square / count + EPS)
    copies = []
    for s in range(psi.shape[0]):
        ready[s] = (vec[s] * scale).astype(BF16)
        copies.append(pltpu.make_async_copy(ready.at[s], psi.at[plan[COUNT, s]], sems.at[s]))
        copies[-1].start()
    for copy in copies:
        copy.wait()


def swap(value):
    return swapped(value, "chain", 1)


def swapped(value, axis, mask):
    size = lax.axis_size(axis)
    return lax.ppermute(value, axis, [(k, k ^ mask) for k in range(size)])


def from_all(value, axis):
    return [value] + [swapped(value, axis, m) for m in range(1, lax.axis_size(axis))]


def gather_parts(part):
    return [keep(p) for p in from_all(part, "tensor")]


def local(env, site, seg_weight, ranks, mpo_mask):
    sectors, chans, edge = env.shape[1:4]
    blocks = sectors * chans
    tensor = lax.axis_size("tensor")
    count = float(sectors * tensor * edge * edge)
    group = 4
    pairs = -(-blocks // (2 * group)) * group
    base = min(pairs, -(-pairs * 3 // 5 // (2 * group)) * 2 * group)
    third = max(base // 6 // group, 1) * group
    marks = [0, base // 2, base - third, base, min(base + third, pairs), pairs]
    cuts = [(a, b) for a, b in zip(marks[:-1], marks[1:]) if a < b]
    usual = 3
    tails = [-(-2 * (c[1] - c[0]) // 16) * 16 for c in cuts]
    rows = [(c[1] - c[0]) * edge + t for c, t in zip(cuts, tails)]
    rows[0] += weight_rows(sectors)
    block_bytes = 2 * edge * edge
    big = sectors * edge * edge * 4

    own_weight = seg_weight[0]
    weights = [swapped(own_weight, "chain", m) for m in range(2, lax.axis_size("chain"))]
    other_site = swap(site[0])
    flat_env = env.reshape(blocks, edge, edge)
    state_shape = (sectors, edge, edge)
    state = vmem(state_shape, F32)
    row_shape = vmem((sectors, edge), F32)
    table_shape = pltpu.SMEM((8, blocks + 2 * group), jnp.int32)

    hbm = pl.BlockSpec(memory_space=pltpu.HBM)
    dma = pltpu.SemaphoreType.DMA
    tail_rows = pltpu.VMEM((max(tails), edge), F32)
    *overs, first_sent, table, active, env_here = pl.pallas_call(
        functools.partial(pack_kernel, cuts[0], cuts[usual:], group),
        out_shape=[jax.ShapeDtypeStruct((r, edge), BF16) for r in rows[usual:]]
        + [
            jax.ShapeDtypeStruct((rows[0], edge), BF16),
            table_shape,
            pltpu.SMEM((1,), jnp.int32),
            vmem((blocks, edge, edge), BF16),
        ],
        in_specs=[hbm] * 4,
        out_specs=[hbm] * len(cuts[usual:]) + [hbm, SM, SM, VM],
        scratch_shapes=[
            pltpu.VMEM((rows[0], edge), BF16),
            pltpu.VMEM((max(rows[usual:]), edge), BF16),
            pltpu.SMEM(mpo_mask.shape, jnp.int32),
            pltpu.SMEM(ranks.shape, jnp.int32),
            pltpu.VMEM((sectors, edge), F32),
            tail_rows,
            dma((3,)),
            dma((sectors,)),
            dma((cuts[0][1] // group + 1,)),
            dma(()),
        ],
        compiler_params=params(),
        cost_estimate=cost(PACK_COST, 2 * blocks * block_bytes),
        name="pack",
    )(stay(mpo_mask), stay(ranks), stay(own_weight), stay(flat_env))
    table, env_here = keep_scalars(table), keep(env_here)

    def send(k):
        if k == len(overs):
            return []
        moved = functools.partial(lambda x: [swap(x)], overs[k])
        return lax.cond(
            active[0] > 2 * cuts[usual + k][0],
            lambda: moved() + send(k + 1),
            lambda: list(overs[k:]),
        )

    extra = [stay(x) for x in send(0)]
    sent = pl.pallas_call(
        functools.partial(rest_kernel, cuts[1:usual], group),
        out_shape=[vmem((r, edge), BF16) for r in rows[1:usual]],
        in_specs=[SM, VM] + [hbm] * (1 + len(extra) + len(weights)),
        out_specs=[VM] * (usual - 1),
        scratch_shapes=[tail_rows],
        compiler_params=params(),
        cost_estimate=cost(REST_COST, 2 * blocks * block_bytes),
        name="rest",
    )(table, env_here, *extra, stay(other_site), *[stay(w) for w in weights])
    got = [keep(swap(c)) for c in (first_sent, *sent)]

    buf_shape = vmem((2, blocks + 1, edge, edge), BF16)
    diag_shape = vmem((2, sectors, -(-(chans + 1) // 16) * 16, edge), F32)
    sums = vmem((2, edge), F32)
    inner_shape = pltpu.VMEM((sectors, edge, chans * edge), BF16)
    work = 4.0 * blocks * edge**3

    buf, diags, prefix, vec, plan = pl.pallas_call(
        functools.partial(own_kernel, group, chans),
        out_shape=[buf_shape, diag_shape, row_shape, state, table_shape],
        in_specs=[SM] + [VM] * (4 + len(weights)),
        out_specs=[VM] * 4 + [SM],
        scratch_shapes=[pltpu.VMEM(state_shape, F32), pltpu.VMEM((sectors, edge), F32)],
        compiler_params=params(),
        cost_estimate=cost(OWN_COST, 0),
        name="own",
    )(table, env_here, site[0], stay(other_site), own_weight, *[stay(w) for w in weights])
    plan = keep_scalars(plan)

    buf, diags, outer, outer_diag = pl.pallas_call(
        functools.partial(outer_kernel, cuts[0], group),
        out_shape=[buf_shape, diag_shape, state, row_shape],
        in_specs=[SM] + [VM] * 4,
        out_specs=[VM] * 4,
        scratch_shapes=[tail_rows, pltpu.VMEM((sectors, edge), F32)],
        input_output_aliases={3: 0, 4: 1},
        compiler_params=params(),
        cost_estimate=cost(0, 0),
        name="outer",
    )(plan, keep(prefix), got[0], keep(buf), keep(diags))

    buf, diags, image = pl.pallas_call(
        functools.partial(mid_kernel, cuts[1], group),
        out_shape=[buf_shape, diag_shape, state],
        in_specs=[SM] + [VM] * 6,
        out_specs=[VM] * 3,
        scratch_shapes=[inner_shape, tail_rows],
        input_output_aliases={5: 0, 6: 1},
        compiler_params=params(),
        cost_estimate=cost(0, 0),
        name="mid",
    )(plan, keep(outer), keep(outer_diag), keep(vec), got[1], keep(buf), keep(diags))

    kept = 5 + len(extra)
    buf, diags, image, part = pl.pallas_call(
        functools.partial(first_kernel, cuts[usual - 1 :], group),
        out_shape=[buf_shape, diag_shape, state, sums],
        in_specs=[SM] + [VM] * 4 + [hbm] * len(extra) + [VM] * 3,
        out_specs=[VM] * 4,
        scratch_shapes=[
            inner_shape, tail_rows, pltpu.VMEM((max(rows[usual:]), edge), BF16), dma(()),
        ],
        input_output_aliases={kept: 0, kept + 1: 1, kept + 2: 2},
        compiler_params=params(),
        cost_estimate=cost(work, 2 * blocks * block_bytes),
        name="first",
    )(
        plan, keep(outer), keep(outer_diag), keep(vec), got[usual - 1], *extra,
        keep(buf), keep(diags), keep(image),
    )
    dh = pl.pallas_call(
        functools.partial(diag_kernel, chans),
        out_shape=state,
        in_specs=[VM],
        out_specs=VM,
        compiler_params=params(),
        cost_estimate=cost(0, 2 * big),
        name="diagonal",
    )(keep(diags))

    for _ in range(ITERS - 1):
        parts = gather_parts(part)
        vec, image, part = pl.pallas_call(
            functools.partial(iter_kernel, count, tensor),
            out_shape=[state, state, sums],
            in_specs=[SM] + [VM] * (4 + tensor),
            out_specs=[VM] * 3,
            scratch_shapes=[inner_shape],
            compiler_params=params(),
            cost_estimate=cost(work, 2 * blocks * block_bytes),
            name="iterate",
        )(plan, keep(buf), keep(vec), keep(image), keep(dh), *parts)

    parts = gather_parts(part)
    vec, part, energy = pl.pallas_call(
        functools.partial(last_kernel, count, tensor),
        out_shape=[state, sums, vmem((1, edge), F32)],
        in_specs=[VM] * (3 + tensor),
        out_specs=[VM] * 3,
        compiler_params=params(),
        cost_estimate=cost(0, 3 * big),
        name="last",
    )(keep(vec), keep(image), keep(dh), *parts)
    parts = gather_parts(part)
    turned = pl.pallas_call(
        turn_kernel,
        out_shape=state,
        in_specs=[VM],
        out_specs=VM,
        compiler_params=params(),
        cost_estimate=cost(0, 2 * big),
        name="turn",
    )(keep(vec))
    psi = pl.pallas_call(
        functools.partial(psi_kernel, count, tensor),
        out_shape=jax.ShapeDtypeStruct(state_shape, BF16),
        in_specs=[SM] + [VM] * (1 + tensor),
        out_specs=hbm,
        scratch_shapes=[pltpu.VMEM(state_shape, BF16), dma((sectors,))],
        compiler_params=params(),
        cost_estimate=cost(0, big),
        name="psi",
    )(plan, keep(turned), *parts)
    return psi[None], energy[0, :1]


def solution(mesh):
    in_specs = (
        P(("cyl", "chain"), "tensor", None, None, None),
        P(("cyl", "chain"), "tensor", None, None),
        P(("cyl", "chain"), "tensor", None),
        P(("cyl", "tensor")),
        P(("cyl", "tensor"), None),
    )
    out_specs = (P(("cyl", "chain"), "tensor", None, None), P(("cyl", "chain")))
    return jax.shard_map(local, mesh=mesh, in_specs=in_specs, out_specs=out_specs, check_vma=False)
```

```python
import functools

import jax
import jax.numpy as jnp
from jax import lax
from jax.experimental import pallas as pl
from jax.experimental.pallas import tpu as pltpu
from jax.sharding import PartitionSpec as P

ITERS = 4
STEP_SIZE = 0.5
EARLY = 3
PACK_COST = 10**7
REST_COST = 10**10
OWN_COST = 0
EPS = 1e-6
BF16 = jnp.bfloat16
F32 = jnp.float32
VMEM_LIMIT = 16 * 2**20
VM = pl.BlockSpec(memory_space=pltpu.VMEM)
SM = pl.BlockSpec(memory_space=pltpu.SMEM)


def params():
    return pltpu.CompilerParams(vmem_limit_bytes=VMEM_LIMIT)


def cost(flops, bytes_accessed):
    return pl.CostEstimate(flops=int(flops), bytes_accessed=int(bytes_accessed), transcendentals=0)


def vmem(shape, dtype):
    return pltpu.VMEM(shape, dtype)


def keep(x):
    return pltpu.with_memory_space_constraint(x, pltpu.VMEM)


def keep_scalars(x):
    return pltpu.with_memory_space_constraint(x, pltpu.SMEM)


def stay(x):
    return pltpu.with_memory_space_constraint(x, pltpu.HBM)


def grid_ij(edge):
    i = lax.broadcasted_iota(jnp.int32, (edge, edge), 0)
    j = lax.broadcasted_iota(jnp.int32, (edge, edge), 1)
    return i, j


def diag_row(block, i, j):
    return jnp.sum(jnp.where(i == j, block, 0.0), axis=0, keepdims=True)


SOURCE, SECTOR, PLACE, TARGET, RANK, COUNT, NUMBER, END = range(8)


def pack(cut, group, table, env, rows_ref, out, before=lambda g, carry: carry, after=None, carry=0):
    low, high = cut
    edge = env.shape[-1]
    i, j = grid_ij(edge)

    def body(g, carry):
        carry = before(g, carry)
        for d in range(group):
            p = g * group + d
            first = env[table[SOURCE, 2 * p]].astype(F32)
            second = env[table[SOURCE, 2 * p + 1]].astype(F32)
            at = pl.multiple_of((p - low) * edge, edge)
            out[pl.ds(at, edge), :] = jnp.where(i <= j, first, second).astype(BF16)
            rows_ref[pl.ds(2 * (p - low), 1), :] = diag_row(first, i, j)
            rows_ref[pl.ds(2 * (p - low) + 1, 1), :] = diag_row(second, i, j)
        if after is not None:
            after(g)
        return carry

    pairs = (table[NUMBER, 0] + 1) // 2
    stop = (jnp.minimum(high, pairs) + group - 1) // group
    carry = lax.fori_loop(low // group, stop, body, carry)
    size = (high - low) * edge
    out[size:, :] = rows_ref[: out.shape[0] - size, :].astype(BF16)
    return carry


def split_rows(value):
    high = value.astype(BF16).astype(F32)
    middle = (value - high).astype(BF16).astype(F32)
    low = value - high - middle
    pad = jnp.zeros((weight_rows(value.shape[0]) - 3 * value.shape[0], value.shape[1]), F32)
    return jnp.concatenate([high, middle, low, pad], axis=0).astype(BF16)


def joined_rows(rows, sectors):
    rows = rows.astype(F32)
    return rows[:sectors] + rows[sectors : 2 * sectors] + rows[2 * sectors : 3 * sectors]


def weight_rows(sectors):
    return -(-3 * sectors // 16) * 16


def pack_kernel(cut, overs, group, mask_hbm, ranks_hbm, weight_hbm, env_hbm, *refs):
    over_hbm, refs = refs[: len(overs)], refs[len(overs) :]
    out_hbm, table, flag, env, out, spare, mask_ref, ranks_ref, weight_ref, rows_ref = refs[:10]
    scalar_sems, sems, out_sems, over_sem = refs[10:]
    sectors, chans = mask_ref.shape
    scalars = [
        pltpu.make_async_copy(mask_hbm, mask_ref, scalar_sems.at[0]),
        pltpu.make_async_copy(ranks_hbm, ranks_ref, scalar_sems.at[1]),
        pltpu.make_async_copy(weight_hbm, weight_ref, scalar_sems.at[2]),
    ]
    for c in scalars:
        c.start()

    def fetch(s):
        part = pl.ds(s * chans, chans)
        return pltpu.make_async_copy(env_hbm.at[part], env.at[part], sems.at[s])

    for s in range(min(EARLY, sectors)):
        fetch(s).start()
    scalars[0].wait()
    for s in range(EARLY, sectors):
        fetch(s).start()
    n = jnp.int32(0)
    for s in range(sectors):
        k = jnp.int32(0)
        for w in range(chans):
            m = mask_ref[s, w]
            table[SOURCE, n] = jnp.int32(s * chans + w)
            table[SECTOR, n] = jnp.int32(s)
            n = n + m
            k = k + m
        table[COUNT, s] = k
    for d in range(2 * group):
        table[SOURCE, n + d] = jnp.int32(0)
        table[SECTOR, n + d] = jnp.int32(0)
    table[NUMBER, 0] = n
    flag[0] = n

    def wait(s, carry):
        fetch(s).wait()
        return carry

    def before(g, here):
        final = jnp.maximum(jnp.minimum(2 * (g + 1) * group, n) - 1, 0)
        need = jnp.maximum(here, table[SECTOR, final] + 1)
        lax.fori_loop(here, need, wait, 0)
        return need

    for c in scalars[1:]:
        c.wait()
    for s in range(sectors):
        table[RANK, s] = ranks_ref[s]
    extra = weight_rows(sectors)
    edge = env.shape[-1]
    size = (cut[1] - cut[0]) * edge
    out[out.shape[0] - extra :, :] = split_rows(weight_ref[...])
    bulk = out.at[: out.shape[0] - extra, :]

    def send(g):
        part = pl.ds(pl.multiple_of(g * group * edge, group * edge), group * edge)
        return pltpu.make_async_copy(out.at[part], out_hbm.at[part], out_sems.at[g])

    def after(g):
        send(g).start()

    here = pack(cut, group, table, env, rows_ref, bulk, before, after, jnp.int32(0))
    tail = pltpu.make_async_copy(out.at[size:], out_hbm.at[size:], out_sems.at[cut[1] // group])
    tail.start()
    lax.fori_loop(here, sectors, wait, 0)
    for over, to in zip(overs, over_hbm):

        @pl.when(n > 2 * over[0])
        def _(over=over, to=to):
            part = spare.at[: to.shape[0]]
            pack(over, group, table, env, rows_ref, part)
            copy = pltpu.make_async_copy(part, to, over_sem)
            copy.start()
            copy.wait()

    tail.wait()

    def drain(g, carry):
        send(g).wait()
        return carry

    stop = (jnp.minimum(cut[1], (n + 1) // 2) + group - 1) // group
    lax.fori_loop(0, stop, drain, 0)


def rest_kernel(cuts, group, table, env, *refs):
    chunks, rows_ref = refs[-len(cuts) - 1 : -1], refs[-1]
    for cut, out in zip(cuts, chunks):
        pack(cut, group, table, env, rows_ref, out)


def put(k, block, side, table, outer, buf):
    buf[side, table[TARGET, k]] = (block * outer[table[SECTOR, k]]).astype(BF16)


def put_diag(k, row, side, table, outer_diag, diags):
    s = table[SECTOR, k]
    scaled = row * outer_diag[pl.ds(s, 1), :]
    diags[side, s, pl.ds(table[PLACE, k], 1), :] = scaled.astype(BF16).astype(F32)


def unpack(cut, group, side, chunk, table, outer, outer_diag, buf, diags, rows_ref):
    low, high = cut
    edge = chunk.shape[-1]
    i, j = grid_ij(edge)
    n = table[NUMBER, 0]
    size = (high - low) * edge
    rows_ref[: chunk.shape[0] - size, :] = chunk[size:, :].astype(F32)

    def body(g, carry):
        for d in range(group):
            p = g * group + d
            at = pl.multiple_of((p - low) * edge, edge)
            both = chunk[pl.ds(at, edge), :].astype(F32)
            flip = both.T
            row = rows_ref[pl.ds(2 * (p - low), 1), :]
            other = rows_ref[pl.ds(2 * (p - low) + 1, 1), :]
            put(2 * p, jnp.where(i <= j, both, flip), side, table, outer, buf)
            lower = jnp.where(i > j, both, jnp.where(i == j, other, flip))
            put(2 * p + 1, lower, side, table, outer, buf)
            put_diag(2 * p, row, side, table, outer_diag, diags)
            put_diag(2 * p + 1, other, side, table, outer_diag, diags)
        return carry

    stop = (jnp.minimum(high, (n + 1) // 2) + group - 1) // group
    lax.fori_loop(low // group, stop, body, 0)


def widths(sectors, chans):
    parts = [10 if p < -(-sectors // 8) else 8 if p < sectors // 2 else 6 for p in range(sectors)]
    return [min(chans, -(-chans * part // 20) * 2) for part in parts]


def make_plan(plan, table, caps, chans):
    sectors = len(caps)
    counts = [table[COUNT, s] for s in range(sectors)]
    places = []
    for s in range(sectors):
        place = jnp.int32(0)
        for t in range(sectors):
            if t != s:
                ahead = counts[t] >= counts[s] if t < s else counts[t] > counts[s]
                place = place + ahead.astype(jnp.int32)
        plan[COUNT, place] = jnp.int32(s)
        plan[RANK, place] = table[RANK, s]
        places.append(place)
    fits = jnp.int32(1)
    for k, cap in enumerate(caps):
        fits = fits * (table[COUNT, plan[COUNT, k]] <= cap).astype(jnp.int32)
    n = table[NUMBER, 0]
    plan[NUMBER, 0] = n
    plan[NUMBER, 1] = fits
    start = jnp.int32(0)
    for s in range(sectors):

        def body(c, k, s=s):
            plan[SOURCE, k] = table[SOURCE, k]
            plan[SECTOR, k] = places[s]
            plan[PLACE, k] = c
            plan[TARGET, k] = places[s] * chans + c
            return k + 1

        start = lax.fori_loop(0, counts[s], body, start)
        plan[END, places[s]] = start

    def rest(k, carry):
        plan[SOURCE, k] = jnp.int32(0)
        plan[SECTOR, k] = jnp.int32(0)
        plan[PLACE, k] = jnp.int32(chans)
        plan[TARGET, k] = jnp.int32(sectors * chans)
        return carry

    lax.fori_loop(n, n + table.shape[1] - sectors * chans, rest, 0)


def own_kernel(group, chans, table, env, own_site, other_site, *refs):
    weights, (buf, diags, prefix, vec, plan, mine, rows_ref) = refs[:-7], refs[-7:]
    sectors, edge = mine.shape[0], mine.shape[-1]
    make_plan(plan, table, widths(sectors, chans), chans)
    at = lax.axis_index("chain")
    side = at % 2
    before = jnp.ones((sectors, edge), F32)
    for c in range(len(weights) + 1):
        value = before
        for d, weight in enumerate(weights[1:], 2):
            value = jnp.where(at ^ d == c, weight[...], value)
        before = jnp.where(c < at - side, before * value, before)
    prefix[...] = before
    own_weight = weights[0][...]
    rows_ref[...] = jnp.where(side == 0, before * own_weight, own_weight)
    i, j = grid_ij(edge)
    for s in range(sectors):
        old = plan[COUNT, s]
        row = jnp.broadcast_to(rows_ref[pl.ds(old, 1), :], (edge, edge))
        mine[s] = row.T * row
        first = jnp.where(side == 0, own_site[old], other_site[old])
        second = jnp.where(side == 0, other_site[old], own_site[old])
        start = jnp.dot(first, second, preferred_element_type=F32).T
        vec[s] = jnp.where(j < plan[RANK, s], start, 0.0)
    diags[...] = jnp.zeros_like(diags)

    def wipe(t, carry):
        buf[0, t] = jnp.zeros((edge, edge), BF16)
        buf[1, t] = jnp.zeros((edge, edge), BF16)
        return carry

    lax.fori_loop(0, sectors * chans, wipe, 0)
    step = 2 * group

    def body(g, carry):
        for d in range(step):
            k = step * g + d
            s = plan[SECTOR, k]
            block = (env[plan[SOURCE, k]].astype(F32) * mine[s]).astype(BF16)
            buf[side, plan[TARGET, k]] = block
            diags[side, s, pl.ds(plan[PLACE, k], 1), :] = diag_row(block.astype(F32), i, j)
        return carry

    lax.fori_loop(0, (plan[NUMBER, 0] + step - 1) // step, body, 0)


def outer_kernel(cut, group, plan, prefix, chunk, *refs):
    _, _, buf, diags, outer, outer_diag, rows_ref, weight_ref = refs
    sectors, edge = outer.shape[0], outer.shape[-1]
    side = lax.axis_index("chain") % 2
    extra = weight_rows(sectors)
    start = chunk.shape[0] - extra
    other_weight = joined_rows(chunk[start:, :], sectors)
    weight_ref[...] = jnp.where(side == 0, other_weight, prefix[...] * other_weight)
    for s in range(sectors):
        row = weight_ref[pl.ds(plan[COUNT, s], 1), :]
        outer_diag[s : s + 1, :] = row * row
        row = jnp.broadcast_to(row, (edge, edge))
        outer[s] = row.T * row
    bulk = chunk.at[:start, :]
    unpack(cut, group, 1 - side, bulk, plan, outer, outer_diag, buf, diags, rows_ref)


def mid_kernel(cut, group, plan, outer, outer_diag, vec, chunk, *refs):
    _, _, buf, diags, image, inner, rows_ref = refs
    side = lax.axis_index("chain") % 2
    unpack(cut, group, 1 - side, chunk, plan, outer, outer_diag, buf, diags, rows_ref)
    sectors, chans = vec.shape[0], inner.shape[-1] // vec.shape[-1]
    for few, caps in ((1, widths(sectors, chans)), (0, [chans] * sectors)):

        @pl.when(plan[NUMBER, 1] == few)
        def _(caps=caps):
            all_images(caps, plan, buf, vec, image, inner)


def all_images(caps, plan, buf, vec, image, inner):
    edge = vec.shape[-1]
    chans = inner.shape[-1] // edge
    _, j = grid_ij(edge)
    for s, cap in enumerate(caps):
        right = buf[1, s * chans : s * chans + cap].reshape(cap * edge, edge)
        image_t = jnp.dot(right, vec[s].astype(BF16), preferred_element_type=F32).astype(BF16)
        for c in range(cap):
            inner[s, :, c * edge : (c + 1) * edge] = image_t[c * edge : (c + 1) * edge]
    for s, cap in enumerate(caps):
        left = buf[0, s * chans : s * chans + cap].reshape(cap * edge, edge)
        hv = jnp.dot(inner[s, :, : cap * edge], left, preferred_element_type=F32)
        image[s] = jnp.where(j < plan[RANK, s], hv, 0.0)


def late_images(low, plan, buf, vec, image, inner):
    sectors, edge = vec.shape[0], vec.shape[-1]
    chans = inner.shape[-1] // edge
    _, j = grid_ij(edge)
    fits = plan[NUMBER, 1]
    for s, cap in enumerate(widths(sectors, chans)):
        take = plan[END, s] > low
        for few, width in ((1, cap), (0, chans)):

            @pl.when(jnp.logical_and(take, fits == few))
            def _(s=s, width=width):
                one_image(s, width, plan, buf, vec[s], image, inner, j)


def one_image(s, width, plan, buf, vector, image, inner, j):
    edge = vector.shape[-1]
    chans = inner.shape[-1] // edge
    right = buf[1, s * chans : s * chans + width].reshape(width * edge, edge)
    image_t = jnp.dot(right, vector.astype(BF16), preferred_element_type=F32).astype(BF16)
    for c in range(width):
        inner[s, :, c * edge : (c + 1) * edge] = image_t[c * edge : (c + 1) * edge]
    left = buf[0, s * chans : s * chans + width].reshape(width * edge, edge)
    hv = jnp.dot(inner[s, :, : width * edge], left, preferred_element_type=F32)
    image[s] = jnp.where(j < plan[RANK, s], hv, 0.0)


def apply_all(vectors, plan, *state):
    vec, inner = state[1], state[-1]
    sectors, chans = vec.shape[0], inner.shape[-1] // vec.shape[-1]
    fits = plan[NUMBER, 1]

    @pl.when(fits == 1)
    def _():
        apply_some(vectors, plan, widths(sectors, chans), *state)

    @pl.when(fits == 0)
    def _():
        apply_some(vectors, plan, [chans] * sectors, *state)


def apply_some(vectors, plan, caps, buf, vec, image, part, inner):
    sectors, edge = vec.shape[0], vec.shape[-1]
    chans = inner.shape[-1] // edge
    for s, cap in enumerate(caps):
        vector = vectors(s)
        vec[s] = vector
        right = buf[1, s * chans : s * chans + cap].reshape(cap * edge, edge)
        image_t = jnp.dot(right, vector.astype(BF16), preferred_element_type=F32).astype(BF16)
        for c in range(cap):
            inner[s, :, c * edge : (c + 1) * edge] = image_t[c * edge : (c + 1) * edge]
    _, j = grid_ij(edge)
    along = jnp.zeros((edge, edge), F32)
    square = jnp.zeros((edge, edge), F32)
    for s, cap in enumerate(caps):
        left = buf[0, s * chans : s * chans + cap].reshape(cap * edge, edge)
        hv = jnp.dot(inner[s, :, : cap * edge], left, preferred_element_type=F32)
        hv = jnp.where(j < plan[RANK, s], hv, 0.0)
        image[s] = hv
        vector = vec[s]
        along = along + vector * hv
        square = square + vector * vector
    store_sums(part, along, square)


def store_sums(part, along, square):
    part[0:1, :] = jnp.sum(along, axis=0, keepdims=True)
    part[1:2, :] = jnp.sum(square, axis=0, keepdims=True)


def first_kernel(cuts, group, plan, outer, outer_diag, vec, chunk, *refs):
    overs, refs = refs[: len(cuts) - 1], refs[len(cuts) - 1 :]
    _, _, _, buf, diags, image, part, inner, rows_ref, spare, sem = refs
    sectors = vec.shape[0]
    side = lax.axis_index("chain") % 2
    unpack(cuts[0], group, 1 - side, chunk, plan, outer, outer_diag, buf, diags, rows_ref)
    for cut, over in zip(cuts[1:], overs):

        @pl.when(plan[NUMBER, 0] > 2 * cut[0])
        def _(cut=cut, over=over):
            here = spare.at[: over.shape[0]]
            copy = pltpu.make_async_copy(over, here, sem)
            copy.start()
            copy.wait()
            unpack(cut, group, 1 - side, here, plan, outer, outer_diag, buf, diags, rows_ref)

    late_images(2 * cuts[0][0], plan, buf, vec, image, inner)
    along = jnp.zeros(vec.shape[1:], F32)
    square = along
    for s in range(sectors):
        along = along + vec[s] * image[s]
        square = square + vec[s] * vec[s]
    store_sums(part, along, square)


def diag_kernel(chans, diags, dh):
    used = lax.broadcasted_iota(jnp.int32, diags.shape[2:], 0) < chans
    for s in range(dh.shape[0]):
        dh[s] = lax.dot_general(
            jnp.where(used, diags[1, s], 0.0).astype(BF16),
            jnp.where(used, diags[0, s], 0.0).astype(BF16),
            (((0,), (0,)), ((), ())),
            preferred_element_type=F32,
        )


def joined(parts):
    values = [p[...] for p in parts]
    while len(values) > 1:
        values = [values[k] + values[k + 1] for k in range(0, len(values), 2)]
    total = values[0]
    along = jnp.sum(total[0:1, :], axis=1, keepdims=True)
    square = jnp.sum(total[1:2, :], axis=1, keepdims=True)
    return along, square


def step_of(count, along, square):
    theta = along / (square + EPS)
    scale = 1.0 / jnp.sqrt(square / count + EPS)

    def step(vector, hv, dh):
        resid = hv - theta * vector
        return (vector - STEP_SIZE * resid / (1.0 + jnp.abs(dh - theta))) * scale

    return theta, step


def iter_kernel(count, partners, plan, buf, vec_in, image_in, dh, *refs):
    parts = refs[:partners]
    vec, image, part, inner = refs[partners:]
    _, step = step_of(count, *joined(parts))
    apply_all(
        lambda s: step(vec_in[s], image_in[s], dh[s]), plan, buf, vec, image, part, inner
    )


def last_kernel(count, partners, vec_in, image_in, dh, *refs):
    parts = refs[:partners]
    vec, part, energy = refs[partners:]
    theta, step = step_of(count, *joined(parts))
    square = jnp.zeros(dh.shape[1:], F32)
    for s in range(dh.shape[0]):
        vector = step(vec_in[s], image_in[s], dh[s])
        vec[s] = vector
        square = square + vector * vector
    store_sums(part, square, square)
    energy[...] = jnp.broadcast_to(theta, energy.shape)


def turn_kernel(vec, turned):
    for s in range(vec.shape[0]):
        turned[s] = vec[s].T


def psi_kernel(count, partners, plan, vec, *refs):
    parts = refs[:partners]
    psi, ready, sems = refs[partners:]
    square, _ = joined(parts)
    scale = 1.0 / jnp.sqrt(square / count + EPS)
    copies = []
    for s in range(psi.shape[0]):
        ready[s] = (vec[s] * scale).astype(BF16)
        copies.append(pltpu.make_async_copy(ready.at[s], psi.at[plan[COUNT, s]], sems.at[s]))
        copies[-1].start()
    for copy in copies:
        copy.wait()


def swap(value):
    return swapped(value, "chain", 1)


def swapped(value, axis, mask):
    size = lax.axis_size(axis)
    return lax.ppermute(value, axis, [(k, k ^ mask) for k in range(size)])


def from_all(value, axis):
    return [value] + [swapped(value, axis, m) for m in range(1, lax.axis_size(axis))]


def gather_parts(part):
    return [keep(p) for p in from_all(part, "tensor")]


def local(env, site, seg_weight, ranks, mpo_mask):
    sectors, chans, edge = env.shape[1:4]
    blocks = sectors * chans
    tensor = lax.axis_size("tensor")
    count = float(sectors * tensor * edge * edge)
    group = 4
    pairs = -(-blocks // (2 * group)) * group
    base = min(pairs, -(-pairs * 3 // 5 // (2 * group)) * 2 * group)
    third = max(base // 6 // group, 1) * group
    marks = [0, base // 2, base - third, base, min(base + third, pairs), pairs]
    cuts = [(a, b) for a, b in zip(marks[:-1], marks[1:]) if a < b]
    usual = 3
    tails = [-(-2 * (c[1] - c[0]) // 16) * 16 for c in cuts]
    rows = [(c[1] - c[0]) * edge + t for c, t in zip(cuts, tails)]
    rows[0] += weight_rows(sectors)
    block_bytes = 2 * edge * edge
    big = sectors * edge * edge * 4

    own_weight = seg_weight[0]
    weights = [swapped(own_weight, "chain", m) for m in range(2, lax.axis_size("chain"))]
    other_site = swap(site[0])
    flat_env = env.reshape(blocks, edge, edge)
    state_shape = (sectors, edge, edge)
    state = vmem(state_shape, F32)
    row_shape = vmem((sectors, edge), F32)
    table_shape = pltpu.SMEM((8, blocks + 2 * group), jnp.int32)

    hbm = pl.BlockSpec(memory_space=pltpu.HBM)
    dma = pltpu.SemaphoreType.DMA
    tail_rows = pltpu.VMEM((max(tails), edge), F32)
    *overs, first_sent, table, active, env_here = pl.pallas_call(
        functools.partial(pack_kernel, cuts[0], cuts[usual:], group),
        out_shape=[jax.ShapeDtypeStruct((r, edge), BF16) for r in rows[usual:]]
        + [
            jax.ShapeDtypeStruct((rows[0], edge), BF16),
            table_shape,
            pltpu.SMEM((1,), jnp.int32),
            vmem((blocks, edge, edge), BF16),
        ],
        in_specs=[hbm] * 4,
        out_specs=[hbm] * len(cuts[usual:]) + [hbm, SM, SM, VM],
        scratch_shapes=[
            pltpu.VMEM((rows[0], edge), BF16),
            pltpu.VMEM((max(rows[usual:]), edge), BF16),
            pltpu.SMEM(mpo_mask.shape, jnp.int32),
            pltpu.SMEM(ranks.shape, jnp.int32),
            pltpu.VMEM((sectors, edge), F32),
            tail_rows,
            dma((3,)),
            dma((sectors,)),
            dma((cuts[0][1] // group + 1,)),
            dma(()),
        ],
        compiler_params=params(),
        cost_estimate=cost(PACK_COST, 2 * blocks * block_bytes),
        name="pack",
    )(stay(mpo_mask), stay(ranks), stay(own_weight), stay(flat_env))
    table, env_here = keep_scalars(table), keep(env_here)

    def send(k):
        if k == len(overs):
            return []
        moved = functools.partial(lambda x: [swap(x)], overs[k])
        return lax.cond(
            active[0] > 2 * cuts[usual + k][0],
            lambda: moved() + send(k + 1),
            lambda: list(overs[k:]),
        )

    extra = [stay(x) for x in send(0)]
    sent = pl.pallas_call(
        functools.partial(rest_kernel, cuts[1:usual], group),
        out_shape=[vmem((r, edge), BF16) for r in rows[1:usual]],
        in_specs=[SM, VM] + [hbm] * (1 + len(extra) + len(weights)),
        out_specs=[VM] * (usual - 1),
        scratch_shapes=[tail_rows],
        compiler_params=params(),
        cost_estimate=cost(REST_COST, 2 * blocks * block_bytes),
        name="rest",
    )(table, env_here, *extra, stay(other_site), *[stay(w) for w in weights])
    got = [keep(swap(c)) for c in (first_sent, *sent)]

    buf_shape = vmem((2, blocks + 1, edge, edge), BF16)
    diag_shape = vmem((2, sectors, -(-(chans + 1) // 16) * 16, edge), F32)
    sums = vmem((2, edge), F32)
    inner_shape = pltpu.VMEM((sectors, edge, chans * edge), BF16)
    work = 4.0 * blocks * edge**3

    buf, diags, prefix, vec, plan = pl.pallas_call(
        functools.partial(own_kernel, group, chans),
        out_shape=[buf_shape, diag_shape, row_shape, state, table_shape],
        in_specs=[SM] + [VM] * (4 + len(weights)),
        out_specs=[VM] * 4 + [SM],
        scratch_shapes=[pltpu.VMEM(state_shape, F32), pltpu.VMEM((sectors, edge), F32)],
        compiler_params=params(),
        cost_estimate=cost(OWN_COST, 0),
        name="own",
    )(table, env_here, site[0], stay(other_site), own_weight, *[stay(w) for w in weights])
    plan = keep_scalars(plan)

    buf, diags, outer, outer_diag = pl.pallas_call(
        functools.partial(outer_kernel, cuts[0], group),
        out_shape=[buf_shape, diag_shape, state, row_shape],
        in_specs=[SM] + [VM] * 4,
        out_specs=[VM] * 4,
        scratch_shapes=[tail_rows, pltpu.VMEM((sectors, edge), F32)],
        input_output_aliases={3: 0, 4: 1},
        compiler_params=params(),
        cost_estimate=cost(0, 0),
        name="outer",
    )(plan, keep(prefix), got[0], keep(buf), keep(diags))

    buf, diags, image = pl.pallas_call(
        functools.partial(mid_kernel, cuts[1], group),
        out_shape=[buf_shape, diag_shape, state],
        in_specs=[SM] + [VM] * 6,
        out_specs=[VM] * 3,
        scratch_shapes=[inner_shape, tail_rows],
        input_output_aliases={5: 0, 6: 1},
        compiler_params=params(),
        cost_estimate=cost(0, 0),
        name="mid",
    )(plan, keep(outer), keep(outer_diag), keep(vec), got[1], keep(buf), keep(diags))

    kept = 5 + len(extra)
    buf, diags, image, part = pl.pallas_call(
        functools.partial(first_kernel, cuts[usual - 1 :], group),
        out_shape=[buf_shape, diag_shape, state, sums],
        in_specs=[SM] + [VM] * 4 + [hbm] * len(extra) + [VM] * 3,
        out_specs=[VM] * 4,
        scratch_shapes=[
            inner_shape, tail_rows, pltpu.VMEM((max(rows[usual:]), edge), BF16), dma(()),
        ],
        input_output_aliases={kept: 0, kept + 1: 1, kept + 2: 2},
        compiler_params=params(),
        cost_estimate=cost(work, 2 * blocks * block_bytes),
        name="first",
    )(
        plan, keep(outer), keep(outer_diag), keep(vec), got[usual - 1], *extra,
        keep(buf), keep(diags), keep(image),
    )
    dh = pl.pallas_call(
        functools.partial(diag_kernel, chans),
        out_shape=state,
        in_specs=[VM],
        out_specs=VM,
        compiler_params=params(),
        cost_estimate=cost(0, 2 * big),
        name="diagonal",
    )(keep(diags))

    for _ in range(ITERS - 1):
        parts = gather_parts(part)
        vec, image, part = pl.pallas_call(
            functools.partial(iter_kernel, count, tensor),
            out_shape=[state, state, sums],
            in_specs=[SM] + [VM] * (4 + tensor),
            out_specs=[VM] * 3,
            scratch_shapes=[inner_shape],
            compiler_params=params(),
            cost_estimate=cost(work, 2 * blocks * block_bytes),
            name="iterate",
        )(plan, keep(buf), keep(vec), keep(image), keep(dh), *parts)

    parts = gather_parts(part)
    vec, part, energy = pl.pallas_call(
        functools.partial(last_kernel, count, tensor),
        out_shape=[state, sums, vmem((1, edge), F32)],
        in_specs=[VM] * (3 + tensor),
        out_specs=[VM] * 3,
        compiler_params=params(),
        cost_estimate=cost(0, 3 * big),
        name="last",
    )(keep(vec), keep(image), keep(dh), *parts)
    parts = gather_parts(part)
    turned = pl.pallas_call(
        turn_kernel,
        out_shape=state,
        in_specs=[VM],
        out_specs=VM,
        compiler_params=params(),
        cost_estimate=cost(0, 2 * big),
        name="turn",
    )(keep(vec))
    psi = pl.pallas_call(
        functools.partial(psi_kernel, count, tensor),
        out_shape=jax.ShapeDtypeStruct(state_shape, BF16),
        in_specs=[SM] + [VM] * (1 + tensor),
        out_specs=hbm,
        scratch_shapes=[pltpu.VMEM(state_shape, BF16), dma((sectors,))],
        compiler_params=params(),
        cost_estimate=cost(0, big),
        name="psi",
    )(plan, keep(turned), *parts)
    return psi[None], energy[0, :1]


def solution(mesh):
    in_specs = (
        P(("cyl", "chain"), "tensor", None, None, None),
        P(("cyl", "chain"), "tensor", None, None),
        P(("cyl", "chain"), "tensor", None),
        P(("cyl", "tensor")),
        P(("cyl", "tensor"), None),
    )
    out_specs = (P(("cyl", "chain"), "tensor", None, None), P(("cyl", "chain")))
    return jax.shard_map(local, mesh=mesh, in_specs=in_specs, out_specs=out_specs, check_vma=False)
```

```python
import functools

import jax
import jax.numpy as jnp
from jax import lax
from jax.experimental import pallas as pl
from jax.experimental.pallas import tpu as pltpu
from jax.sharding import PartitionSpec as P

ITERS = 4
STEP_SIZE = 0.5
PACK_COST = 10**7
REST_COST = 10**10
OWN_COST = 0
EPS = 1e-6
BF16 = jnp.bfloat16
F32 = jnp.float32
VMEM_LIMIT = 16 * 2**20
VM = pl.BlockSpec(memory_space=pltpu.VMEM)
SM = pl.BlockSpec(memory_space=pltpu.SMEM)


def params():
    return pltpu.CompilerParams(vmem_limit_bytes=VMEM_LIMIT)


def cost(flops, bytes_accessed):
    return pl.CostEstimate(flops=int(flops), bytes_accessed=int(bytes_accessed), transcendentals=0)


def vmem(shape, dtype):
    return pltpu.VMEM(shape, dtype)


def keep(x):
    return pltpu.with_memory_space_constraint(x, pltpu.VMEM)


def keep_scalars(x):
    return pltpu.with_memory_space_constraint(x, pltpu.SMEM)


def stay(x):
    return pltpu.with_memory_space_constraint(x, pltpu.HBM)


def grid_ij(edge):
    i = lax.broadcasted_iota(jnp.int32, (edge, edge), 0)
    j = lax.broadcasted_iota(jnp.int32, (edge, edge), 1)
    return i, j


def diag_row(block, i, j):
    return jnp.sum(jnp.where(i == j, block, 0.0), axis=0, keepdims=True)


SOURCE, SECTOR, PLACE, TARGET, RANK, COUNT, NUMBER, END = range(8)


def pack(cut, group, table, env, rows_ref, out, before=lambda g, carry: carry, after=None, carry=0):
    low, high = cut
    edge = env.shape[-1]
    i, j = grid_ij(edge)

    def body(g, carry):
        carry = before(g, carry)
        for d in range(group):
            p = g * group + d
            first = env[table[SOURCE, 2 * p]].astype(F32)
            second = env[table[SOURCE, 2 * p + 1]].astype(F32)
            at = pl.multiple_of((p - low) * edge, edge)
            out[pl.ds(at, edge), :] = jnp.where(i <= j, first, second).astype(BF16)
            rows_ref[pl.ds(2 * (p - low), 1), :] = diag_row(first, i, j)
            rows_ref[pl.ds(2 * (p - low) + 1, 1), :] = diag_row(second, i, j)
        if after is not None:
            after(g)
        return carry

    pairs = (table[NUMBER, 0] + 1) // 2
    stop = (jnp.minimum(high, pairs) + group - 1) // group
    carry = lax.fori_loop(low // group, stop, body, carry)
    size = (high - low) * edge
    out[size:, :] = rows_ref[: out.shape[0] - size, :].astype(BF16)
    return carry


def split_rows(value):
    high = value.astype(BF16).astype(F32)
    middle = (value - high).astype(BF16).astype(F32)
    low = value - high - middle
    pad = jnp.zeros((weight_rows(value.shape[0]) - 3 * value.shape[0], value.shape[1]), F32)
    return jnp.concatenate([high, middle, low, pad], axis=0).astype(BF16)


def joined_rows(rows, sectors):
    rows = rows.astype(F32)
    return rows[:sectors] + rows[sectors : 2 * sectors] + rows[2 * sectors : 3 * sectors]


def weight_rows(sectors):
    return -(-3 * sectors // 16) * 16


def pack_kernel(cut, overs, group, mask_hbm, ranks_hbm, weight_hbm, env_hbm, *refs):
    over_hbm, refs = refs[: len(overs)], refs[len(overs) :]
    out_hbm, table, flag, env, out, spare, mask_ref, ranks_ref, weight_ref, rows_ref = refs[:10]
    scalar_sems, sems, out_sems, over_sem = refs[10:]
    sectors, chans = mask_ref.shape
    blocks = sectors * chans
    scalars = [
        pltpu.make_async_copy(mask_hbm, mask_ref, scalar_sems.at[0]),
        pltpu.make_async_copy(ranks_hbm, ranks_ref, scalar_sems.at[1]),
        pltpu.make_async_copy(weight_hbm, weight_ref, scalar_sems.at[2]),
    ]
    for c in scalars:
        c.start()

    def fetch(s):
        part = pl.ds(s * chans, chans)
        return pltpu.make_async_copy(env_hbm.at[part], env.at[part], sems.at[s])

    for s in range(sectors):
        fetch(s).start()
    for c in scalars:
        c.wait()
    n = jnp.int32(0)
    for s in range(sectors):
        table[RANK, s] = ranks_ref[s]
        k = jnp.int32(0)
        for w in range(chans):
            m = mask_ref[s, w]
            table[SOURCE, n] = jnp.int32(s * chans + w)
            table[SECTOR, n] = jnp.int32(s)
            table[PLACE, n] = k
            table[TARGET, n] = s * chans + k
            n = n + m
            k = k + m
        table[COUNT, s] = k
    for d in range(2 * group):
        table[SOURCE, n + d] = jnp.int32(0)
        table[SECTOR, n + d] = jnp.int32(0)
        table[PLACE, n + d] = jnp.int32(chans)
        table[TARGET, n + d] = jnp.int32(blocks)
    table[NUMBER, 0] = n
    flag[0] = n

    def wait(s, carry):
        fetch(s).wait()
        return carry

    def before(g, here):
        final = jnp.maximum(jnp.minimum(2 * (g + 1) * group, n) - 1, 0)
        need = jnp.maximum(here, table[SECTOR, final] + 1)
        lax.fori_loop(here, need, wait, 0)
        return need

    extra = weight_rows(sectors)
    edge = env.shape[-1]
    size = (cut[1] - cut[0]) * edge
    out[out.shape[0] - extra :, :] = split_rows(weight_ref[...])
    bulk = out.at[: out.shape[0] - extra, :]

    def send(g):
        part = pl.ds(pl.multiple_of(g * group * edge, group * edge), group * edge)
        return pltpu.make_async_copy(out.at[part], out_hbm.at[part], out_sems.at[g])

    def after(g):
        send(g).start()

    here = pack(cut, group, table, env, rows_ref, bulk, before, after, jnp.int32(0))
    tail = pltpu.make_async_copy(out.at[size:], out_hbm.at[size:], out_sems.at[cut[1] // group])
    tail.start()
    lax.fori_loop(here, sectors, wait, 0)
    for over, to in zip(overs, over_hbm):

        @pl.when(n > 2 * over[0])
        def _(over=over, to=to):
            part = spare.at[: to.shape[0]]
            pack(over, group, table, env, rows_ref, part)
            copy = pltpu.make_async_copy(part, to, over_sem)
            copy.start()
            copy.wait()

    tail.wait()

    def drain(g, carry):
        send(g).wait()
        return carry

    stop = (jnp.minimum(cut[1], (n + 1) // 2) + group - 1) // group
    lax.fori_loop(0, stop, drain, 0)


def rest_kernel(cuts, group, table, env, *refs):
    chunks, rows_ref = refs[-len(cuts) - 1 : -1], refs[-1]
    for cut, out in zip(cuts, chunks):
        pack(cut, group, table, env, rows_ref, out)


def put(k, block, side, table, outer, buf):
    buf[side, table[TARGET, k]] = (block * outer[table[SECTOR, k]]).astype(BF16)


def put_diag(k, row, side, table, outer_diag, diags):
    s = table[SECTOR, k]
    scaled = row * outer_diag[pl.ds(s, 1), :]
    diags[side, s, pl.ds(table[PLACE, k], 1), :] = scaled.astype(BF16).astype(F32)


def unpack(cut, group, side, chunk, table, outer, outer_diag, buf, diags, rows_ref):
    low, high = cut
    edge = chunk.shape[-1]
    i, j = grid_ij(edge)
    n = table[NUMBER, 0]
    size = (high - low) * edge
    rows_ref[: chunk.shape[0] - size, :] = chunk[size:, :].astype(F32)

    def body(g, carry):
        for d in range(group):
            p = g * group + d
            at = pl.multiple_of((p - low) * edge, edge)
            both = chunk[pl.ds(at, edge), :].astype(F32)
            flip = both.T
            row = rows_ref[pl.ds(2 * (p - low), 1), :]
            other = rows_ref[pl.ds(2 * (p - low) + 1, 1), :]
            put(2 * p, jnp.where(i <= j, both, flip), side, table, outer, buf)
            lower = jnp.where(i > j, both, jnp.where(i == j, other, flip))
            put(2 * p + 1, lower, side, table, outer, buf)
            put_diag(2 * p, row, side, table, outer_diag, diags)
            put_diag(2 * p + 1, other, side, table, outer_diag, diags)
        return carry

    stop = (jnp.minimum(high, (n + 1) // 2) + group - 1) // group
    lax.fori_loop(low // group, stop, body, 0)


def widths(sectors, chans):
    parts = [10 if p < -(-sectors // 8) else 8 if p < sectors // 2 else 6 for p in range(sectors)]
    return [min(chans, -(-chans * part // 20) * 2) for part in parts]


def make_plan(plan, table, caps, chans):
    sectors = len(caps)
    counts = [table[COUNT, s] for s in range(sectors)]
    places = []
    for s in range(sectors):
        place = jnp.int32(0)
        for t in range(sectors):
            if t != s:
                ahead = counts[t] >= counts[s] if t < s else counts[t] > counts[s]
                place = place + ahead.astype(jnp.int32)
        plan[COUNT, place] = jnp.int32(s)
        plan[RANK, place] = table[RANK, s]
        places.append(place)
    fits = jnp.int32(1)
    for k, cap in enumerate(caps):
        fits = fits * (table[COUNT, plan[COUNT, k]] <= cap).astype(jnp.int32)
    n = table[NUMBER, 0]
    plan[NUMBER, 0] = n
    plan[NUMBER, 1] = fits
    start = jnp.int32(0)
    for s in range(sectors):

        def body(c, k, s=s):
            plan[SOURCE, k] = table[SOURCE, k]
            plan[SECTOR, k] = places[s]
            plan[PLACE, k] = c
            plan[TARGET, k] = places[s] * chans + c
            return k + 1

        start = lax.fori_loop(0, counts[s], body, start)
        plan[END, places[s]] = start

    def rest(k, carry):
        for row in (SOURCE, SECTOR, PLACE, TARGET):
            plan[row, k] = table[row, k]
        return carry

    lax.fori_loop(n, n + table.shape[1] - sectors * chans, rest, 0)


def own_kernel(group, chans, table, env, own_site, other_site, *refs):
    weights, (buf, diags, prefix, vec, plan, mine, rows_ref) = refs[:-7], refs[-7:]
    sectors, edge = mine.shape[0], mine.shape[-1]
    make_plan(plan, table, widths(sectors, chans), chans)
    at = lax.axis_index("chain")
    side = at % 2
    before = jnp.ones((sectors, edge), F32)
    for c in range(len(weights) + 1):
        value = before
        for d, weight in enumerate(weights[1:], 2):
            value = jnp.where(at ^ d == c, weight[...], value)
        before = jnp.where(c < at - side, before * value, before)
    prefix[...] = before
    own_weight = weights[0][...]
    rows_ref[...] = jnp.where(side == 0, before * own_weight, own_weight)
    i, j = grid_ij(edge)
    for s in range(sectors):
        old = plan[COUNT, s]
        row = jnp.broadcast_to(rows_ref[pl.ds(old, 1), :], (edge, edge))
        mine[s] = row.T * row
        first = jnp.where(side == 0, own_site[old], other_site[old])
        second = jnp.where(side == 0, other_site[old], own_site[old])
        start = jnp.dot(first, second, preferred_element_type=F32).T
        vec[s] = jnp.where(j < plan[RANK, s], start, 0.0)
    diags[...] = jnp.zeros_like(diags)

    def wipe(t, carry):
        buf[0, t] = jnp.zeros((edge, edge), BF16)
        buf[1, t] = jnp.zeros((edge, edge), BF16)
        return carry

    lax.fori_loop(0, sectors * chans, wipe, 0)
    step = 2 * group

    def body(g, carry):
        for d in range(step):
            k = step * g + d
            s = plan[SECTOR, k]
            block = (env[plan[SOURCE, k]].astype(F32) * mine[s]).astype(BF16)
            buf[side, plan[TARGET, k]] = block
            diags[side, s, pl.ds(plan[PLACE, k], 1), :] = diag_row(block.astype(F32), i, j)
        return carry

    lax.fori_loop(0, (plan[NUMBER, 0] + step - 1) // step, body, 0)


def outer_kernel(cut, group, plan, prefix, chunk, *refs):
    _, _, buf, diags, outer, outer_diag, rows_ref, weight_ref = refs
    sectors, edge = outer.shape[0], outer.shape[-1]
    side = lax.axis_index("chain") % 2
    extra = weight_rows(sectors)
    start = chunk.shape[0] - extra
    other_weight = joined_rows(chunk[start:, :], sectors)
    weight_ref[...] = jnp.where(side == 0, other_weight, prefix[...] * other_weight)
    for s in range(sectors):
        row = weight_ref[pl.ds(plan[COUNT, s], 1), :]
        outer_diag[s : s + 1, :] = row * row
        row = jnp.broadcast_to(row, (edge, edge))
        outer[s] = row.T * row
    bulk = chunk.at[:start, :]
    unpack(cut, group, 1 - side, bulk, plan, outer, outer_diag, buf, diags, rows_ref)


def mid_kernel(cut, group, plan, outer, outer_diag, vec, chunk, *refs):
    _, _, buf, diags, image, inner, rows_ref = refs
    side = lax.axis_index("chain") % 2
    unpack(cut, group, 1 - side, chunk, plan, outer, outer_diag, buf, diags, rows_ref)
    sectors, chans = vec.shape[0], inner.shape[-1] // vec.shape[-1]
    for few, caps in ((1, widths(sectors, chans)), (0, [chans] * sectors)):

        @pl.when(plan[NUMBER, 1] == few)
        def _(caps=caps):
            all_images(caps, plan, buf, vec, image, inner)


def all_images(caps, plan, buf, vec, image, inner):
    edge = vec.shape[-1]
    chans = inner.shape[-1] // edge
    _, j = grid_ij(edge)
    for s, cap in enumerate(caps):
        right = buf[1, s * chans : s * chans + cap].reshape(cap * edge, edge)
        image_t = jnp.dot(right, vec[s].astype(BF16), preferred_element_type=F32).astype(BF16)
        for c in range(cap):
            inner[s, :, c * edge : (c + 1) * edge] = image_t[c * edge : (c + 1) * edge]
    for s, cap in enumerate(caps):
        left = buf[0, s * chans : s * chans + cap].reshape(cap * edge, edge)
        hv = jnp.dot(inner[s, :, : cap * edge], left, preferred_element_type=F32)
        image[s] = jnp.where(j < plan[RANK, s], hv, 0.0)


def late_images(low, plan, buf, vec, image, inner):
    sectors, edge = vec.shape[0], vec.shape[-1]
    chans = inner.shape[-1] // edge
    _, j = grid_ij(edge)
    fits = plan[NUMBER, 1]
    for s, cap in enumerate(widths(sectors, chans)):
        take = plan[END, s] > low
        for few, width in ((1, cap), (0, chans)):

            @pl.when(jnp.logical_and(take, fits == few))
            def _(s=s, width=width):
                one_image(s, width, plan, buf, vec[s], image, inner, j)


def one_image(s, width, plan, buf, vector, image, inner, j):
    edge = vector.shape[-1]
    chans = inner.shape[-1] // edge
    right = buf[1, s * chans : s * chans + width].reshape(width * edge, edge)
    image_t = jnp.dot(right, vector.astype(BF16), preferred_element_type=F32).astype(BF16)
    for c in range(width):
        inner[s, :, c * edge : (c + 1) * edge] = image_t[c * edge : (c + 1) * edge]
    left = buf[0, s * chans : s * chans + width].reshape(width * edge, edge)
    hv = jnp.dot(inner[s, :, : width * edge], left, preferred_element_type=F32)
    image[s] = jnp.where(j < plan[RANK, s], hv, 0.0)


def apply_all(vectors, plan, *state):
    vec, inner = state[1], state[-1]
    sectors, chans = vec.shape[0], inner.shape[-1] // vec.shape[-1]
    fits = plan[NUMBER, 1]

    @pl.when(fits == 1)
    def _():
        apply_some(vectors, plan, widths(sectors, chans), *state)

    @pl.when(fits == 0)
    def _():
        apply_some(vectors, plan, [chans] * sectors, *state)


def apply_some(vectors, plan, caps, buf, vec, image, part, inner):
    sectors, edge = vec.shape[0], vec.shape[-1]
    chans = inner.shape[-1] // edge
    for s, cap in enumerate(caps):
        vector = vectors(s)
        vec[s] = vector
        right = buf[1, s * chans : s * chans + cap].reshape(cap * edge, edge)
        image_t = jnp.dot(right, vector.astype(BF16), preferred_element_type=F32).astype(BF16)
        for c in range(cap):
            inner[s, :, c * edge : (c + 1) * edge] = image_t[c * edge : (c + 1) * edge]
    _, j = grid_ij(edge)
    along = jnp.zeros((edge, edge), F32)
    square = jnp.zeros((edge, edge), F32)
    for s, cap in enumerate(caps):
        left = buf[0, s * chans : s * chans + cap].reshape(cap * edge, edge)
        hv = jnp.dot(inner[s, :, : cap * edge], left, preferred_element_type=F32)
        hv = jnp.where(j < plan[RANK, s], hv, 0.0)
        image[s] = hv
        vector = vec[s]
        along = along + vector * hv
        square = square + vector * vector
    store_sums(part, along, square)


def store_sums(part, along, square):
    part[0:1, :] = jnp.sum(along, axis=0, keepdims=True)
    part[1:2, :] = jnp.sum(square, axis=0, keepdims=True)


def first_kernel(cuts, group, plan, outer, outer_diag, vec, chunk, *refs):
    overs, refs = refs[: len(cuts) - 1], refs[len(cuts) - 1 :]
    _, _, _, buf, diags, image, part, inner, rows_ref, spare, sem = refs
    sectors = vec.shape[0]
    side = lax.axis_index("chain") % 2
    unpack(cuts[0], group, 1 - side, chunk, plan, outer, outer_diag, buf, diags, rows_ref)
    for cut, over in zip(cuts[1:], overs):

        @pl.when(plan[NUMBER, 0] > 2 * cut[0])
        def _(cut=cut, over=over):
            here = spare.at[: over.shape[0]]
            copy = pltpu.make_async_copy(over, here, sem)
            copy.start()
            copy.wait()
            unpack(cut, group, 1 - side, here, plan, outer, outer_diag, buf, diags, rows_ref)

    late_images(2 * cuts[0][0], plan, buf, vec, image, inner)
    along = jnp.zeros(vec.shape[1:], F32)
    square = along
    for s in range(sectors):
        along = along + vec[s] * image[s]
        square = square + vec[s] * vec[s]
    store_sums(part, along, square)


def diag_kernel(chans, diags, dh):
    used = lax.broadcasted_iota(jnp.int32, diags.shape[2:], 0) < chans
    for s in range(dh.shape[0]):
        dh[s] = lax.dot_general(
            jnp.where(used, diags[1, s], 0.0).astype(BF16),
            jnp.where(used, diags[0, s], 0.0).astype(BF16),
            (((0,), (0,)), ((), ())),
            preferred_element_type=F32,
        )


def joined(parts):
    values = [p[...] for p in parts]
    while len(values) > 1:
        values = [values[k] + values[k + 1] for k in range(0, len(values), 2)]
    total = values[0]
    along = jnp.sum(total[0:1, :], axis=1, keepdims=True)
    square = jnp.sum(total[1:2, :], axis=1, keepdims=True)
    return along, square


def step_of(count, along, square):
    theta = along / (square + EPS)
    scale = 1.0 / jnp.sqrt(square / count + EPS)

    def step(vector, hv, dh):
        resid = hv - theta * vector
        return (vector - STEP_SIZE * resid / (1.0 + jnp.abs(dh - theta))) * scale

    return theta, step


def iter_kernel(count, partners, plan, buf, vec_in, image_in, dh, *refs):
    parts = refs[:partners]
    vec, image, part, inner = refs[partners:]
    _, step = step_of(count, *joined(parts))
    apply_all(
        lambda s: step(vec_in[s], image_in[s], dh[s]), plan, buf, vec, image, part, inner
    )


def last_kernel(count, partners, vec_in, image_in, dh, *refs):
    parts = refs[:partners]
    vec, part, energy = refs[partners:]
    theta, step = step_of(count, *joined(parts))
    square = jnp.zeros(dh.shape[1:], F32)
    for s in range(dh.shape[0]):
        vector = step(vec_in[s], image_in[s], dh[s])
        vec[s] = vector
        square = square + vector * vector
    store_sums(part, square, square)
    energy[...] = jnp.broadcast_to(theta, energy.shape)


def turn_kernel(vec, turned):
    for s in range(vec.shape[0]):
        turned[s] = vec[s].T


def psi_kernel(count, partners, plan, vec, *refs):
    parts = refs[:partners]
    psi, ready, sems = refs[partners:]
    square, _ = joined(parts)
    scale = 1.0 / jnp.sqrt(square / count + EPS)
    copies = []
    for s in range(psi.shape[0]):
        ready[s] = (vec[s] * scale).astype(BF16)
        copies.append(pltpu.make_async_copy(ready.at[s], psi.at[plan[COUNT, s]], sems.at[s]))
        copies[-1].start()
    for copy in copies:
        copy.wait()


def swap(value):
    return swapped(value, "chain", 1)


def swapped(value, axis, mask):
    size = lax.axis_size(axis)
    return lax.ppermute(value, axis, [(k, k ^ mask) for k in range(size)])


def from_all(value, axis):
    return [value] + [swapped(value, axis, m) for m in range(1, lax.axis_size(axis))]


def gather_parts(part):
    return [keep(p) for p in from_all(part, "tensor")]


def local(env, site, seg_weight, ranks, mpo_mask):
    sectors, chans, edge = env.shape[1:4]
    blocks = sectors * chans
    tensor = lax.axis_size("tensor")
    count = float(sectors * tensor * edge * edge)
    group = 4
    pairs = -(-blocks // (2 * group)) * group
    base = min(pairs, -(-pairs * 3 // 5 // (2 * group)) * 2 * group)
    third = max(base // 6 // group, 1) * group
    marks = [0, base - 2 * third, base - third, base, min(base + third, pairs), pairs]
    cuts = [(a, b) for a, b in zip(marks[:-1], marks[1:]) if a < b]
    usual = 3
    tails = [-(-2 * (c[1] - c[0]) // 16) * 16 for c in cuts]
    rows = [(c[1] - c[0]) * edge + t for c, t in zip(cuts, tails)]
    rows[0] += weight_rows(sectors)
    block_bytes = 2 * edge * edge
    big = sectors * edge * edge * 4

    own_weight = seg_weight[0]
    weights = [swapped(own_weight, "chain", m) for m in range(2, lax.axis_size("chain"))]
    other_site = swap(site[0])
    flat_env = env.reshape(blocks, edge, edge)
    state_shape = (sectors, edge, edge)
    state = vmem(state_shape, F32)
    row_shape = vmem((sectors, edge), F32)
    table_shape = pltpu.SMEM((8, blocks + 2 * group), jnp.int32)

    hbm = pl.BlockSpec(memory_space=pltpu.HBM)
    dma = pltpu.SemaphoreType.DMA
    tail_rows = pltpu.VMEM((max(tails), edge), F32)
    *overs, first_sent, table, active, env_here = pl.pallas_call(
        functools.partial(pack_kernel, cuts[0], cuts[usual:], group),
        out_shape=[jax.ShapeDtypeStruct((r, edge), BF16) for r in rows[usual:]]
        + [
            jax.ShapeDtypeStruct((rows[0], edge), BF16),
            table_shape,
            pltpu.SMEM((1,), jnp.int32),
            vmem((blocks, edge, edge), BF16),
        ],
        in_specs=[hbm] * 4,
        out_specs=[hbm] * len(cuts[usual:]) + [hbm, SM, SM, VM],
        scratch_shapes=[
            pltpu.VMEM((rows[0], edge), BF16),
            pltpu.VMEM((max(rows[usual:]), edge), BF16),
            pltpu.SMEM(mpo_mask.shape, jnp.int32),
            pltpu.SMEM(ranks.shape, jnp.int32),
            pltpu.VMEM((sectors, edge), F32),
            tail_rows,
            dma((3,)),
            dma((sectors,)),
            dma((cuts[0][1] // group + 1,)),
            dma(()),
        ],
        compiler_params=params(),
        cost_estimate=cost(PACK_COST, 2 * blocks * block_bytes),
        name="pack",
    )(stay(mpo_mask), stay(ranks), stay(own_weight), stay(flat_env))
    table, env_here = keep_scalars(table), keep(env_here)

    def send(k):
        if k == len(overs):
            return []
        moved = functools.partial(lambda x: [swap(x)], overs[k])
        return lax.cond(
            active[0] > 2 * cuts[usual + k][0],
            lambda: moved() + send(k + 1),
            lambda: list(overs[k:]),
        )

    extra = [stay(x) for x in send(0)]
    sent = pl.pallas_call(
        functools.partial(rest_kernel, cuts[1:usual], group),
        out_shape=[vmem((r, edge), BF16) for r in rows[1:usual]],
        in_specs=[SM, VM] + [hbm] * (1 + len(extra) + len(weights)),
        out_specs=[VM] * (usual - 1),
        scratch_shapes=[tail_rows],
        compiler_params=params(),
        cost_estimate=cost(REST_COST, 2 * blocks * block_bytes),
        name="rest",
    )(table, env_here, *extra, stay(other_site), *[stay(w) for w in weights])
    got = [keep(swap(c)) for c in (first_sent, *sent)]

    buf_shape = vmem((2, blocks + 1, edge, edge), BF16)
    diag_shape = vmem((2, sectors, -(-(chans + 1) // 16) * 16, edge), F32)
    sums = vmem((2, edge), F32)
    inner_shape = pltpu.VMEM((sectors, edge, chans * edge), BF16)
    work = 4.0 * blocks * edge**3

    buf, diags, prefix, vec, plan = pl.pallas_call(
        functools.partial(own_kernel, group, chans),
        out_shape=[buf_shape, diag_shape, row_shape, state, table_shape],
        in_specs=[SM] + [VM] * (4 + len(weights)),
        out_specs=[VM] * 4 + [SM],
        scratch_shapes=[pltpu.VMEM(state_shape, F32), pltpu.VMEM((sectors, edge), F32)],
        compiler_params=params(),
        cost_estimate=cost(OWN_COST, 0),
        name="own",
    )(table, env_here, site[0], stay(other_site), own_weight, *[stay(w) for w in weights])
    plan = keep_scalars(plan)

    buf, diags, outer, outer_diag = pl.pallas_call(
        functools.partial(outer_kernel, cuts[0], group),
        out_shape=[buf_shape, diag_shape, state, row_shape],
        in_specs=[SM] + [VM] * 4,
        out_specs=[VM] * 4,
        scratch_shapes=[tail_rows, pltpu.VMEM((sectors, edge), F32)],
        input_output_aliases={3: 0, 4: 1},
        compiler_params=params(),
        cost_estimate=cost(0, 0),
        name="outer",
    )(plan, keep(prefix), got[0], keep(buf), keep(diags))

    buf, diags, image = pl.pallas_call(
        functools.partial(mid_kernel, cuts[1], group),
        out_shape=[buf_shape, diag_shape, state],
        in_specs=[SM] + [VM] * 6,
        out_specs=[VM] * 3,
        scratch_shapes=[inner_shape, tail_rows],
        input_output_aliases={5: 0, 6: 1},
        compiler_params=params(),
        cost_estimate=cost(0, 0),
        name="mid",
    )(plan, keep(outer), keep(outer_diag), keep(vec), got[1], keep(buf), keep(diags))

    kept = 5 + len(extra)
    buf, diags, image, part = pl.pallas_call(
        functools.partial(first_kernel, cuts[usual - 1 :], group),
        out_shape=[buf_shape, diag_shape, state, sums],
        in_specs=[SM] + [VM] * 4 + [hbm] * len(extra) + [VM] * 3,
        out_specs=[VM] * 4,
        scratch_shapes=[
            inner_shape, tail_rows, pltpu.VMEM((max(rows[usual:]), edge), BF16), dma(()),
        ],
        input_output_aliases={kept: 0, kept + 1: 1, kept + 2: 2},
        compiler_params=params(),
        cost_estimate=cost(work, 2 * blocks * block_bytes),
        name="first",
    )(
        plan, keep(outer), keep(outer_diag), keep(vec), got[usual - 1], *extra,
        keep(buf), keep(diags), keep(image),
    )
    dh = pl.pallas_call(
        functools.partial(diag_kernel, chans),
        out_shape=state,
        in_specs=[VM],
        out_specs=VM,
        compiler_params=params(),
        cost_estimate=cost(0, 2 * big),
        name="diagonal",
    )(keep(diags))

    for _ in range(ITERS - 1):
        parts = gather_parts(part)
        vec, image, part = pl.pallas_call(
            functools.partial(iter_kernel, count, tensor),
            out_shape=[state, state, sums],
            in_specs=[SM] + [VM] * (4 + tensor),
            out_specs=[VM] * 3,
            scratch_shapes=[inner_shape],
            compiler_params=params(),
            cost_estimate=cost(work, 2 * blocks * block_bytes),
            name="iterate",
        )(plan, keep(buf), keep(vec), keep(image), keep(dh), *parts)

    parts = gather_parts(part)
    vec, part, energy = pl.pallas_call(
        functools.partial(last_kernel, count, tensor),
        out_shape=[state, sums, vmem((1, edge), F32)],
        in_specs=[VM] * (3 + tensor),
        out_specs=[VM] * 3,
        compiler_params=params(),
        cost_estimate=cost(0, 3 * big),
        name="last",
    )(keep(vec), keep(image), keep(dh), *parts)
    parts = gather_parts(part)
    turned = pl.pallas_call(
        turn_kernel,
        out_shape=state,
        in_specs=[VM],
        out_specs=VM,
        compiler_params=params(),
        cost_estimate=cost(0, 2 * big),
        name="turn",
    )(keep(vec))
    psi = pl.pallas_call(
        functools.partial(psi_kernel, count, tensor),
        out_shape=jax.ShapeDtypeStruct(state_shape, BF16),
        in_specs=[SM] + [VM] * (1 + tensor),
        out_specs=hbm,
        scratch_shapes=[pltpu.VMEM(state_shape, BF16), dma((sectors,))],
        compiler_params=params(),
        cost_estimate=cost(0, big),
        name="psi",
    )(plan, keep(turned), *parts)
    return psi[None], energy[0, :1]


def solution(mesh):
    in_specs = (
        P(("cyl", "chain"), "tensor", None, None, None),
        P(("cyl", "chain"), "tensor", None, None),
        P(("cyl", "chain"), "tensor", None),
        P(("cyl", "tensor")),
        P(("cyl", "tensor"), None),
    )
    out_specs = (P(("cyl", "chain"), "tensor", None, None), P(("cyl", "chain")))
    return jax.shard_map(local, mesh=mesh, in_specs=in_specs, out_specs=out_specs, check_vma=False)
```
